32 devices in a mesh: dp: 8 (over y, x, core), tensor: 4 (over z).
Axes of the slice: x: 2, y: 2, z: 4, core: 2. Of those that a mesh axis runs over, the one named last changes fastest.
Arguments:
- tokens: bfloat16 [6304, 768], P(('dp', 'tensor')), may hold values from -6 to 6
- cotangent: bfloat16 [6304, 768], P(('dp', 'tensor')), may hold values from -6 to 6
- qkv_weight: bfloat16 [3, 768, 768], P(None, 'dp', 'tensor'), may hold values from -3 to 3
- qv_bias: bfloat16 [2, 12, 64], P(None, 'tensor', 'dp'), may hold values from -3 to 3
- proj_weight: bfloat16 [768, 768], P('tensor', 'dp'), may hold values from -0.875 to 0.875
- vectors: bfloat16 [6, 768], P(None, 'dp'), may hold values from -2 to 2
- fc1_weight: bfloat16 [768, 3072], P('dp', 'tensor'), may hold values from -0.21875 to 0.21875
- fc1_bias: bfloat16 [48, 64], P('tensor', 'dp'), may hold values from -3 to 3
- fc2_weight: bfloat16 [3072, 768], P('tensor', 'dp'), may hold values from -0.109375 to 0.109375
Outputs:
- output: bfloat16 [6304, 768], P(('dp', 'tensor'))
- input_grad: float32 [6304, 768], P(('dp', 'tensor'))
- qkv_grad: float32 [3, 768, 768], P(None, 'dp', 'tensor')
- qv_bias_grad: float32 [2, 12, 64], P(None, 'tensor', 'dp')
- proj_grad: float32 [768, 768], P('tensor', 'dp')
- vectors_grad: float32 [6, 768], P(None, ('dp', 'tensor'))
- fc1_grad: float32 [768, 3072], P('dp', 'tensor')
- fc1_bias_grad: float32 [48, 64], P('tensor', 'dp')
- fc2_grad: float32 [3072, 768], P('tensor', 'dp')
The draws below stay inside these ranges and needn't reach their ends.
All inputs are finite; a program needn't handle non-finite values.
Results may differ from the reference program's by a relative error of at most 0.015.
Values may be sent and summed in bfloat16 or wider, within the bound.
No kernel may reach another device: no remote copies, remote signals or barrier semaphores. Data moves between devices by JAX's collectives and lax.ppermute only.
A program may use at most 128 MiB of HBM per device.

```python
import math
import jax
import jax.numpy as jnp
from jax import lax

D = 768
H = 12
HD = 64
FF = 3072
SEQ = 197
IMG_DEV = 4
TOKENS = 6304


def draw_tokens(key, part):
    key = jax.random.fold_in(key, 11)
    keys = jax.random.split(key, 3)
    col_scale = jnp.exp(jax.random.uniform(keys[2], (1, D), jnp.float32, math.log(0.3), math.log(3.0)))
    row_scale = jnp.exp(jax.random.uniform(keys[1], (TOKENS, 1), jnp.float32, math.log(0.4), math.log(4.0)))
    mixed = jax.random.normal(keys[0], (TOKENS, D), jnp.float32) * row_scale * col_scale
    return jnp.clip(mixed, -6.0, 6.0).astype(jnp.bfloat16)


def draw_qkv_weight(key, part):
    key = jax.random.fold_in(key, 23)
    keys = jax.random.split(key, 1)
    base = jnp.clip(jax.random.normal(keys[0], (3, D, D), jnp.float32), -6.0, 6.0)
    return (base * (1.0 / math.sqrt(D))).astype(jnp.bfloat16)


def draw_vectors(key, part):
    key = jax.random.fold_in(key, 37)
    keys = jax.random.split(key, 2)
    gains = jnp.exp(jax.random.uniform(keys[0], (6, D), jnp.float32, math.log(0.5), math.log(2.0)))
    shifts = jnp.clip(0.5 * jax.random.normal(keys[1], (6, D), jnp.float32), -2.0, 2.0)
    is_gain = (jnp.arange(6) % 3 == 0)[:, None]
    return jnp.where(is_gain, gains, shifts).astype(jnp.bfloat16)


def spiked(values, key, source, target, blocks, factor):
    owner, partner = [(jnp.arange(values.shape[dim]) // (values.shape[dim] // blocks)).reshape([-1 if axis == dim else 1 for axis in range(values.ndim)]) for dim in (source, target)]
    chosen = jax.random.permutation(key, blocks)[partner]
    strong = (owner == chosen) | (owner == (partner + blocks // 2) % blocks)
    return jnp.where(strong, factor * values, values)


def level_of(rng, dims, pieces, smallest, top_value):
    gain, own = 1.0, jax.random.fold_in(rng, 6)
    for axis_at, blocks in pieces:
        steps = jnp.exp(jax.random.uniform(jax.random.fold_in(own, axis_at), (blocks,), jnp.float32, smallest / len(pieces), top_value / len(pieces)))
        gain = gain * jnp.repeat(steps, dims[axis_at] // blocks).reshape([-1 if axis == axis_at else 1 for axis in range(len(dims))])
    return gain


def bell_draw(key, dims, spread, reach, shards=(), held_as=jnp.bfloat16):
    gain = level_of(key, dims, shards, -0.22, 0.18) if shards else 1.0
    entries = jax.random.normal(key, dims, jnp.float32) * spread * gain
    return jnp.minimum(jnp.maximum(entries, -reach), reach).astype(held_as)


def heavy_noise(key, dims, deviation, limit, cuts, heavy, kind=jnp.bfloat16):
    drawn = deviation * jax.random.normal(key, dims, jnp.float32)
    if cuts:
        drawn = drawn * level_of(key, dims, cuts, -0.22, 0.18)
    return jnp.clip(spiked(drawn, jax.random.fold_in(key, 3), *heavy), -limit, limit).astype(kind)


def setup_inputs(seed: int = 0) -> dict:
    key_list = jax.random.split(jax.random.key(seed), 10)
    tokens = draw_tokens(jax.random.fold_in(key_list[9], 71), 0)
    cotangent = heavy_noise(key_list[1], (TOKENS, D), 1.0, 6.0, ((0, 32),), (0, 1, 32, 2.75))
    qkv_weight = draw_qkv_weight(jax.random.fold_in(key_list[9], 71), 0)
    qv_bias = bell_draw(key_list[3], (2, H, HD), 0.5, 3.0, ((1, 4), (2, 8)))
    proj_weight = bell_draw(key_list[4], (D, D), (D // 16) ** -0.5, 0.875, ((0, 4), (1, 8)))
    vectors = draw_vectors(jax.random.fold_in(key_list[9], 71), 0)
    fc1_weight = bell_draw(key_list[6], (D, FF), D ** -0.5, 0.21875, ((0, 8), (1, 4)))
    fc1_bias = bell_draw(key_list[7], (FF // HD, HD), 0.5, 3.0, ((0, 4), (1, 8)))
    fc2_weight = bell_draw(key_list[8], (FF, D), FF ** -0.5, 0.109375, ((0, 4), (1, 8)))
    return {"tokens": tokens, "cotangent": cotangent, "qkv_weight": qkv_weight, "qv_bias": qv_bias, "proj_weight": proj_weight, "vectors": vectors, "fc1_weight": fc1_weight, "fc1_bias": fc1_bias, "fc2_weight": fc2_weight}


norm_eps = 1e-06
half_root = 0.7071067811865476
density_scale = 0.3989422804014327

def layer_norm(values, scale_row, shift_row):
    centred = values - lax.optimization_barrier(jnp.mean(values, axis=-1, keepdims=True))
    recip_root = lax.rsqrt(lax.optimization_barrier(jnp.mean(centred * centred, axis=-1, keepdims=True)) + norm_eps)
    normed = centred * recip_root
    return (normed, recip_root, normed * scale_row + shift_row)

def norm_back(upstream, normed, recip_root):
    first_mean = lax.optimization_barrier(jnp.mean(upstream, axis=-1, keepdims=True))
    second_mean = lax.optimization_barrier(jnp.mean(upstream * normed, axis=-1, keepdims=True))
    return recip_root * (upstream - first_mean - normed * second_mean)

def gelu_parts(values):
    cumul = 0.5 * (1.0 + lax.erf(values * half_root))
    return (values * cumul, cumul + values * jnp.exp(-0.5 * values * values) * density_scale)

def rounded(values):
    return lax.optimization_barrier(values.astype(jnp.bfloat16)).astype(jnp.float32)

def reference(tokens, cotangent, qkv_weight, qv_bias, proj_weight, vectors, fc1_weight, fc1_bias, fc2_weight):
    vec_float = vectors.astype(jnp.float32)
    qkv_float = qkv_weight.astype(jnp.float32)
    bias_rows = jnp.stack([qv_bias[0].reshape(D).astype(jnp.float32), jnp.zeros((D,), jnp.float32), qv_bias[1].reshape(D).astype(jnp.float32)])
    hidden_bias = fc1_bias.reshape(FF).astype(jnp.float32)
    block_rows = IMG_DEV * SEQ
    block_count = TOKENS // block_rows
    token_blocks = tokens.reshape(block_count, block_rows, D)
    cot_blocks = cotangent.reshape(block_count, block_rows, D)

    def one_block(totals, inputs):
        tok_block, cot_block = inputs
        tok_float = tok_block.astype(jnp.float32)
        norm_one, root_one, scaled_one = layer_norm(tok_float, vec_float[0], vec_float[1])
        ln_one = scaled_one.astype(jnp.bfloat16)
        ln_one_float = ln_one.astype(jnp.float32)
        projected = jnp.einsum('td,cde->cte', ln_one_float, qkv_float) + bias_rows[:, None, :]
        qkv_float_act = rounded(projected)
        head_view = qkv_float_act.reshape(3, IMG_DEV, SEQ, H, HD)
        queries, keys_all, values_all = (head_view[0], head_view[1], head_view[2])
        scores = jnp.einsum('iqhd,ikhd->ihqk', queries, keys_all) * 0.125
        top_score = lax.optimization_barrier(jnp.max(scores, axis=-1, keepdims=True))
        log_total = top_score + jnp.log(lax.optimization_barrier(jnp.sum(jnp.exp(scores - top_score), axis=-1, keepdims=True)))
        probs_full = jnp.exp(scores - log_total)
        probs = rounded(probs_full)
        attended = jnp.einsum('ihqk,ikhd->iqhd', probs, values_all).astype(jnp.bfloat16).reshape(block_rows, D)
        mid = tok_float + jnp.dot(attended, proj_weight, preferred_element_type=jnp.float32) + vec_float[2]
        norm_two, root_two, scaled_two = layer_norm(mid, vec_float[3], vec_float[4])
        ln_two = scaled_two.astype(jnp.bfloat16)
        pre_act = jnp.dot(ln_two, fc1_weight, preferred_element_type=jnp.float32) + hidden_bias
        act_float, act_slope = gelu_parts(pre_act)
        act = act_float.astype(jnp.bfloat16)
        output = (mid + jnp.dot(act, fc2_weight, preferred_element_type=jnp.float32) + vec_float[5]).astype(jnp.bfloat16)
        cot_float = cot_block.astype(jnp.float32)
        fc2_part = jnp.dot(act.T, cot_block, preferred_element_type=jnp.float32)
        pre_grad = jnp.dot(cot_block, fc2_weight.T, preferred_element_type=jnp.float32) * act_slope
        fc1_bias_part = lax.optimization_barrier(jnp.sum(pre_grad, axis=0))
        pre_grad_b = pre_grad.astype(jnp.bfloat16)
        fc1_part = jnp.dot(ln_two.T, pre_grad_b, preferred_element_type=jnp.float32)
        ln2_grad = jnp.dot(pre_grad_b, fc1_weight.T, preferred_element_type=jnp.float32)
        mid_grad = cot_float + norm_back(ln2_grad * vec_float[3], norm_two, root_two)
        mid_grad_b = mid_grad.astype(jnp.bfloat16)
        proj_part = jnp.dot(attended.T, mid_grad_b, preferred_element_type=jnp.float32)
        att_grad = jnp.dot(mid_grad_b, proj_weight.T, preferred_element_type=jnp.float32).astype(jnp.bfloat16)
        att_view = att_grad.astype(jnp.float32).reshape(IMG_DEV, SEQ, H, HD)
        attended_view = attended.astype(jnp.float32).reshape(IMG_DEV, SEQ, H, HD)
        probs_grad = jnp.einsum('iqhd,ikhd->ihqk', att_view, values_all)
        delta = jnp.einsum('iqhd,iqhd->ihq', att_view, attended_view)[..., None]
        score_grad = rounded(probs_full * (probs_grad - delta) * 0.125)
        query_grad = jnp.einsum('ihqk,ikhd->iqhd', score_grad, keys_all)
        key_grad = jnp.einsum('ihqk,iqhd->ikhd', score_grad, queries)
        value_grad = jnp.einsum('ihqk,iqhd->ikhd', probs, att_view)
        act_grads = jnp.stack([query_grad, key_grad, value_grad]).reshape(3, block_rows, D)
        bias_part = jnp.stack([lax.optimization_barrier(jnp.sum(act_grads[0], axis=0)), lax.optimization_barrier(jnp.sum(act_grads[2], axis=0))])
        act_grads_b = rounded(act_grads)
        qkv_part = jnp.einsum('td,cte->cde', ln_one_float, act_grads_b)
        ln1_grad = jnp.einsum('cte,cde->td', act_grads_b, qkv_float)
        input_grad = mid_grad + norm_back(ln1_grad * vec_float[0], norm_one, root_one)
        vec_part = jnp.stack([lax.optimization_barrier(jnp.sum(ln1_grad * norm_one, axis=0)), lax.optimization_barrier(jnp.sum(ln1_grad, axis=0)), lax.optimization_barrier(jnp.sum(mid_grad, axis=0)), lax.optimization_barrier(jnp.sum(ln2_grad * norm_two, axis=0)), lax.optimization_barrier(jnp.sum(ln2_grad, axis=0)), lax.optimization_barrier(jnp.sum(cot_float, axis=0))])
        parts = (qkv_part, bias_part, proj_part, vec_part, fc1_part, fc1_bias_part, fc2_part)
        new_totals = tuple((total + part for total, part in zip(totals, parts)))
        return (new_totals, (output, input_grad))
    start_totals = (jnp.zeros((3, D, D), jnp.float32), jnp.zeros((2, D), jnp.float32), jnp.zeros((D, D), jnp.float32), jnp.zeros((6, D), jnp.float32), jnp.zeros((D, FF), jnp.float32), jnp.zeros((FF,), jnp.float32), jnp.zeros((FF, D), jnp.float32))
    totals, results = lax.scan(one_block, start_totals, (token_blocks, cot_blocks))
    outputs, input_grads = results
    return (outputs.reshape(TOKENS, D), input_grads.reshape(TOKENS, D), totals[0], totals[1].reshape(2, H, HD), totals[2], totals[3], totals[4], totals[5].reshape(FF // HD, HD), totals[6])
```

```python
import functools

import jax
import jax.numpy as jnp
from jax import lax
from jax.experimental import pallas as pl
from jax.experimental.pallas import tpu as pltpu
from jax.sharding import PartitionSpec as P

BF = jnp.bfloat16
F32 = jnp.float32
norm_eps = 1e-06
half_root = 0.7071067811865476
density_scale = 0.3989422804014327
VMEM_LIMIT = 56 * 1024 * 1024


def nn(a, b):
    return jnp.dot(a, b, preferred_element_type=F32)


def nt(a, b):
    return lax.dot_general(a, b, (((1,), (1,)), ((), ())), preferred_element_type=F32)


def tn(a, b):
    return lax.dot_general(a, b, (((0,), (0,)), ((), ())), preferred_element_type=F32)


def norm_parts(values):
    centred = values - jnp.mean(values, axis=-1, keepdims=True)
    recip_root = lax.rsqrt(jnp.mean(centred * centred, axis=-1, keepdims=True) + norm_eps)
    return centred * recip_root, recip_root


def norm_back(upstream, normed, recip_root):
    first_mean = jnp.mean(upstream, axis=-1, keepdims=True)
    second_mean = jnp.mean(upstream * normed, axis=-1, keepdims=True)
    return recip_root * (upstream - first_mean - normed * second_mean)


def gelu_parts(values):
    cumul = 0.5 * (1.0 + lax.erf(values * half_root))
    return (values * cumul, cumul + values * jnp.exp(-0.5 * values * values) * density_scale)


class Layout:
    def __init__(self, fast, groups, width):
        self.fast, self.groups, self.width = fast, groups, width
        self.chunk = width // 8 if fast else width

    def t(self, j, pos):
        return lax.rem(pos[1] + (self.groups - j), self.groups) if self.fast else j

    def out(self, j):
        return (self.groups - j) % self.groups if self.fast else j

    def rows(self, k, pos):
        if not self.fast:
            return pl.ds(0, self.width)
        return pl.ds(pl.multiple_of((pos[0] ^ k) * self.chunk, self.chunk), self.chunk)

    def n_buffers(self):
        return 8 if self.fast else 1

    def sources(self, bufs, j):
        if not self.fast:
            return [(bufs[0].at[j], 0)]
        found = []
        for core in range(2):
            ha, ya, hb, xb = bufs[4 * core : 4 * core + 4]
            if j < 2:
                blocks = [(ha, j, 0), (ha, 2 + j, 2), (ya, j, 4), (ya, 2 + j, 6)]
            else:
                blocks = [(hb, j - 2, 0), (hb, j, 4), (xb, j - 2, 2), (xb, j, 6)]
            for ref, at, k in blocks:
                found.append((ref.at[pl.ds(at * self.chunk, self.chunk), :], k ^ core))
        return found

    def start(self, bufs, dest, sems, pos):
        copies = []
        for j in range(self.groups):
            group = []
            for n, (src, k) in enumerate(self.sources(bufs, j)):
                copy = pltpu.make_async_copy(src, dest.at[j, self.rows(k, pos), :], sems.at[j, n])
                copy.start()
                group.append(copy)
            copies.append(group)
        return copies

    def put(self, scratch, mine, theirs, j, pos):
        if not self.fast:
            mine[j, :, :] = scratch[...].astype(BF)
            return
        for k in range(8):
            block = scratch[self.rows(k, pos), :].astype(BF)
            (theirs if k & 1 else mine)[k >> 1, self.out(j), 0 : self.chunk, :] = block

    def grad_shapes(self, extra=0):
        if not self.fast:
            return [jax.ShapeDtypeStruct((self.groups, self.width, self.width), BF)]
        shape = (4, self.groups, self.chunk + extra, self.width)
        return [jax.ShapeDtypeStruct(shape, BF)] * 2


def kernel_call(body, ins, outs, scratch, any_from=None, any_to=None, flops=0):
    specs = []
    for n in range(len(ins)):
        if n == 0:
            specs.append(pl.BlockSpec(memory_space=pltpu.SMEM))
        elif any_from is not None and any_from <= n < any_to:
            specs.append(pl.BlockSpec(memory_space=pl.ANY))
        else:
            specs.append(pl.BlockSpec(memory_space=pltpu.VMEM))
    nbytes = sum(x.size * x.dtype.itemsize for x in list(ins) + list(outs))
    return pl.pallas_call(
        body,
        out_shape=outs,
        in_specs=specs,
        out_specs=[pl.BlockSpec(memory_space=pltpu.VMEM)] * len(outs),
        scratch_shapes=scratch,
        compiler_params=pltpu.CompilerParams(vmem_limit_bytes=VMEM_LIMIT),
        cost_estimate=pl.CostEstimate(flops=flops, bytes_accessed=nbytes, transcendentals=0),
    )(*ins)


def split_refs(lay, refs, n_in, n_out):
    n = lay.n_buffers()
    bufs, refs = refs[:n], refs[n:]
    return bufs, refs[:n_in], refs[n_in : n_in + n_out], refs[n_in + n_out :]


def pad_rows(dest, source, seq):
    dest[...] = jnp.zeros_like(dest)
    dest[0:seq, :] = source[...].astype(dest.dtype)


def attention_forward(lay, seq, hd, pos, *refs):
    bufs, ins, outs, scratch = split_refs(lay, refs, 3, 6)
    tok_ref, vec_ref, bias_ref = ins
    w_ref, ln_ref, qkv_ref, probs_ref, att_ref, mid_ref = outs
    x_ref, sems = scratch
    copies = lay.start(bufs, w_ref, sems, pos)
    pad_rows(x_ref, tok_ref, seq)
    rows = x_ref.shape[0]
    normed, _ = norm_parts(x_ref[...])
    ln = (normed * vec_ref[0:1, :] + vec_ref[1:2, :]).astype(BF)
    ln_ref[...] = ln
    mid_ref[...] = x_ref[...] + vec_ref[2:3, :]
    wide = att_ref.shape[2]
    heads = wide // hd
    valid = lax.broadcasted_iota(jnp.int32, (rows, rows), 1) < seq
    for j in range(lay.groups):
        for copy in copies[j]:
            copy.wait()
        qkv = nn(ln, w_ref[j, :, 0 : 3 * wide]) + bias_ref[lay.t(j, pos)]
        qkv_ref[j, :, :] = qkv.astype(BF)
        for h in range(heads):
            q = qkv_ref[j, :, h * hd : (h + 1) * hd]
            k = qkv_ref[j, :, wide + h * hd : wide + (h + 1) * hd]
            v = qkv_ref[j, :, 2 * wide + h * hd : 2 * wide + (h + 1) * hd]
            scores = jnp.where(valid, nt(q, k) * (hd**-0.5), -1e30)
            top = jnp.max(scores, axis=-1, keepdims=True)
            e = jnp.exp(scores - top)
            p = (e * (1.0 / jnp.sum(e, axis=-1, keepdims=True))).astype(BF)
            probs_ref[j * heads + h, :, :] = p
            att_ref[j, :, h * hd : (h + 1) * hd] = nn(p, v).astype(BF)
        mid_ref[...] += nt(att_ref[j, :, :], w_ref[j, :, 3 * wide : 4 * wide])


def feed_forward(lay, seq, pos, *refs):
    bufs, ins, outs, scratch = split_refs(lay, refs, 4, 4 + len(lay.grad_shapes()))
    mid_ref, cot_ref, vec_ref, bias_ref = ins
    w_ref, ln_ref, act_ref, slope_ref, mine = outs[:5]
    theirs = outs[5] if lay.fast else None
    cotp_ref, g_ref, sems = scratch
    copies = lay.start(bufs, w_ref, sems, pos)
    pad_rows(cotp_ref, cot_ref, seq)
    normed, _ = norm_parts(mid_ref[...])
    ln = (normed * vec_ref[3:4, :] + vec_ref[4:5, :]).astype(BF)
    ln_ref[...] = ln
    for j in range(lay.groups):
        for copy in copies[j]:
            copy.wait()
        pre = nn(ln, w_ref[j]) + bias_ref[lay.t(j, pos)]
        act, slope = gelu_parts(pre)
        act_ref[j, :, :] = act.astype(BF)
        slope_ref[j, :, :] = slope
        g_ref[...] = tn(cotp_ref[...], act_ref[j])
        lay.put(g_ref, mine, theirs, j, pos)


def feed_backward(lay, seq, pos, *refs):
    bufs, ins, outs, scratch = split_refs(lay, refs, 7, 3 + len(lay.grad_shapes()))
    w1_ref, ln_ref, act_ref, slope_ref, mid_ref, cot_ref, vec_ref = ins
    out_ref, mg_ref, small_ref, mine = outs[:4]
    theirs = outs[4] if lay.fast else None
    w2_ref, cotp_ref, g_ref, out_acc, ln_acc, sems = scratch
    copies = lay.start(bufs, w2_ref, sems, pos)
    pad_rows(cotp_ref, cot_ref, seq)
    cot = cotp_ref[...]
    small_ref[...] = jnp.zeros_like(small_ref)
    out_acc[...] = mid_ref[...] + vec_ref[5:6, :]
    ln_acc[...] = jnp.zeros_like(ln_acc)
    for j in range(lay.groups):
        for copy in copies[j]:
            copy.wait()
        pre_grad = nn(cot, w2_ref[j]) * slope_ref[j]
        small_ref[pl.ds(6 + lay.t(j, pos), 1), :] = jnp.sum(pre_grad, axis=0, keepdims=True)
        pgb = pre_grad.astype(BF)
        g_ref[...] = tn(ln_ref[...], pgb)
        lay.put(g_ref, mine, theirs, j, pos)
        ln_acc[...] += nt(pgb, w1_ref[j])
        out_acc[...] += nt(act_ref[j], w2_ref[j])
    out_ref[...] = out_acc[0:seq, :].astype(BF)
    normed, root = norm_parts(mid_ref[...])
    grad = ln_acc[...]
    cotf = cot.astype(F32)
    mid_grad = cotf + norm_back(grad * vec_ref[3:4, :], normed, root)
    mg_ref[...] = mid_grad
    small_ref[2:3, :] = jnp.sum(mid_grad, axis=0, keepdims=True)
    small_ref[3:4, :] = jnp.sum(grad * normed, axis=0, keepdims=True)
    small_ref[4:5, :] = jnp.sum(grad, axis=0, keepdims=True)
    small_ref[5:6, :] = jnp.sum(cotf, axis=0, keepdims=True)


def attention_backward(lay, seq, hd, pos, *refs):
    n_out = 2 + len(lay.grad_shapes())
    ins, outs, scratch = refs[:9], refs[9 : 9 + n_out], refs[9 + n_out :]
    tok_ref, w_ref, ln_ref, qkv_ref, probs_ref, att_ref, mg_ref, small_in, vec_ref = ins
    dx_ref, small_ref, mine = outs[:3]
    theirs = outs[3] if lay.fast else None
    x_ref, dqkv_ref, g_ref, ln_acc = scratch
    wide = att_ref.shape[2]
    heads = wide // hd
    scale = hd**-0.5
    small_ref[...] = small_in[...]
    pad_rows(x_ref, tok_ref, seq)
    mgb = mg_ref[...].astype(BF)
    ln = ln_ref[...]
    ln_acc[...] = jnp.zeros_like(ln_acc)
    for j in range(lay.groups):
        att_grad = nn(mgb, w_ref[j, :, 3 * wide : 4 * wide]).astype(BF)
        att = att_ref[j]
        g_ref[:, 3 * wide : 4 * wide] = tn(mgb, att)
        prod = att_grad.astype(F32) * att.astype(F32)
        for h in range(heads):
            at = slice(h * hd, (h + 1) * hd)
            q = qkv_ref[j, :, h * hd : (h + 1) * hd]
            k = qkv_ref[j, :, wide + h * hd : wide + (h + 1) * hd]
            v = qkv_ref[j, :, 2 * wide + h * hd : 2 * wide + (h + 1) * hd]
            p = probs_ref[j * heads + h]
            da = att_grad[:, at]
            delta = jnp.sum(prod[:, at], axis=-1, keepdims=True)
            ds = (p.astype(F32) * (nt(da, v) - delta) * scale).astype(BF)
            dqkv_ref[:, h * hd : (h + 1) * hd] = nn(ds, k)
            dqkv_ref[:, wide + h * hd : wide + (h + 1) * hd] = tn(ds, q)
            dqkv_ref[:, 2 * wide + h * hd : 2 * wide + (h + 1) * hd] = tn(p, da)
        dqkv = dqkv_ref[...]
        small_ref[pl.ds(10 + lay.t(j, pos), 1), 0 : 3 * wide] = jnp.sum(dqkv, axis=0, keepdims=True)
        dqkv = dqkv.astype(BF)
        g_ref[:, 0 : 3 * wide] = tn(ln, dqkv)
        lay.put(g_ref, mine, theirs, j, pos)
        ln_acc[...] += nt(dqkv, w_ref[j, :, 0 : 3 * wide])
    normed, root = norm_parts(x_ref[...])
    grad = ln_acc[...]
    dx = mg_ref[...] + norm_back(grad * vec_ref[0:1, :], normed, root)
    dx_ref[...] = dx[0:seq, :]
    small_ref[0:1, :] = jnp.sum(grad * normed, axis=0, keepdims=True)
    small_ref[1:2, :] = jnp.sum(grad, axis=0, keepdims=True)
    if lay.fast:
        extra = small_ref[...].astype(BF)
        for k in range(8):
            for j in range(lay.groups):
                dest = theirs if k & 1 else mine
                dest[k >> 1, j, lay.chunk : lay.chunk + 16, :] = extra


def shift(x, by):
    n = lax.axis_size("tensor")
    return lax.ppermute(x, "tensor", [(i, (i + by) % n) for i in range(n)])


def flip(x, bit):
    n = lax.axis_size("dp")
    return lax.ppermute(x, "dp", [(i, i ^ bit) for i in range(n)])


CORE, AXIS_X, AXIS_Y = 1, 2, 4


def gather_piece(piece):
    z = [piece] + [shift(piece, k) for k in (1, 2, 3)]
    h1 = jnp.concatenate(z[0:2], axis=0)
    h2 = jnp.concatenate(z[2:4], axis=0)
    ha = jnp.concatenate([h1, flip(h1, AXIS_X)], axis=0)
    hb = jnp.concatenate([h2, flip(h2, AXIS_Y)], axis=0)
    ya = flip(ha, AXIS_Y)
    xb = flip(hb, AXIS_X)
    mine = [ha, ya, hb, xb]
    return mine + [flip(b, CORE) for b in mine]


def scatter_piece(mine, theirs):
    recv = flip(theirs, CORE)

    def summed(chips, groups):
        return (mine[chips, groups].astype(F32) + recv[chips, groups].astype(F32)).astype(BF)

    low, high = slice(0, 2), slice(2, 4)
    far = flip(summed(slice(2, 4), low), AXIS_Y)
    near = (summed(slice(0, 2), low).astype(F32) + far.astype(F32)).astype(BF)
    first = near[0].astype(F32) + flip(near[1], AXIS_X).astype(F32)
    far = flip(summed(slice(1, 4, 2), high), AXIS_X)
    near = (summed(slice(0, 4, 2), high).astype(F32) + far.astype(F32)).astype(BF)
    second = near[0].astype(F32) + flip(near[1], AXIS_Y).astype(F32)
    total = first[0]
    for k, part in ((1, first[1]), (2, second[0]), (3, second[1])):
        total = total + shift(part.astype(BF), k).astype(F32)
    return total


def per_device(
    tokens, cotangent, qkv_weight, qv_bias, proj_weight, vectors, fc1_weight, fc1_bias, fc2_weight
):
    n_dp, groups = lax.axis_size("dp"), lax.axis_size("tensor")
    seq, width = tokens.shape
    chunk, wide = qkv_weight.shape[1], qkv_weight.shape[2]
    hd = qv_bias.shape[2] * n_dp
    units = fc1_weight.shape[1]
    fast = n_dp == 8 and groups == 4
    lay = Layout(fast, groups, width)
    d, z = lax.axis_index("dp"), lax.axis_index("tensor")
    pos = jnp.stack([d, z]).astype(jnp.int32)

    piece_a = jnp.concatenate(
        [qkv_weight[0], qkv_weight[1], qkv_weight[2], proj_weight.T], axis=1
    )
    piece_b = fc1_weight
    piece_c = fc2_weight.T
    flat = jnp.concatenate([vectors.reshape(-1), qv_bias.reshape(-1), fc1_bias.reshape(-1)])
    params = lax.all_gather(flat, ("dp", "tensor")).reshape(n_dp, groups, -1)
    if fast:
        bufs_a, bufs_b, bufs_c = [gather_piece(p) for p in (piece_a, piece_b, piece_c)]
    else:

        def gather(p):
            return [lax.all_gather(lax.all_gather(p, "dp", axis=0, tiled=True), "tensor", axis=0)]

        bufs_a, bufs_b, bufs_c = gather(piece_a), gather(piece_b), gather(piece_c)

    n_vec, n_qv = vectors.size, qv_bias.size
    vec = params[:, 0, :n_vec].reshape(n_dp, 6, chunk).transpose(1, 0, 2).reshape(6, width)
    vec = jnp.pad(vec, ((0, 2), (0, 0))).astype(F32)
    heads = wide // hd
    qv = params[:, :, n_vec : n_vec + n_qv].reshape(n_dp, groups, 2, heads, hd // n_dp)
    qv = qv.transpose(1, 2, 3, 0, 4).reshape(groups, 2, wide)
    bias = jnp.stack([qv[:, 0], jnp.zeros_like(qv[:, 0]), qv[:, 1]], axis=1)
    bias = bias.reshape(groups, 1, 3 * wide).astype(F32)
    fb = params[:, :, n_vec + n_qv :].reshape(n_dp, groups, units // hd, hd // n_dp)
    fb = fb.transpose(1, 2, 0, 3).reshape(groups, 1, units).astype(F32)

    rows = -(-seq // 16) * 16
    sds = jax.ShapeDtypeStruct
    nb = lay.n_buffers()
    sems = pltpu.SemaphoreType.DMA((groups, nb))
    w_shape = sds((groups, width, width), BF)
    mm = 2 * rows * width * width * groups

    w_a, ln1, qkv, probs, att, mid = kernel_call(
        functools.partial(attention_forward, lay, seq, hd),
        [pos, *bufs_a, tokens, vec, bias],
        [
            w_shape,
            sds((rows, width), BF),
            sds((groups, rows, 3 * wide), BF),
            sds((groups * heads, rows, rows), BF),
            sds((groups, rows, wide), BF),
            sds((rows, width), F32),
        ],
        [pltpu.VMEM((rows, width), F32), sems],
        1,
        1 + nb,
        flops=mm,
    )
    w_b, ln2, act, slope, *grads_c = kernel_call(
        functools.partial(feed_forward, lay, seq),
        [pos, *bufs_b, mid, cotangent, vec, fb],
        [
            w_shape,
            sds((rows, width), BF),
            sds((groups, rows, units), BF),
            sds((groups, rows, units), F32),
            *lay.grad_shapes(),
        ],
        [pltpu.VMEM((rows, width), BF), pltpu.VMEM((width, width), F32), sems],
        1,
        1 + nb,
        flops=2 * mm,
    )
    output, mid_grad, small, *grads_b = kernel_call(
        functools.partial(feed_backward, lay, seq),
        [pos, *bufs_c, w_b, ln2, act, slope, mid, cotangent, vec],
        [
            sds((seq, width), BF),
            sds((rows, width), F32),
            sds((16, width), F32),
            *lay.grad_shapes(),
        ],
        [
            pltpu.VMEM(w_shape.shape, BF),
            pltpu.VMEM((rows, width), BF),
            pltpu.VMEM((width, width), F32),
            pltpu.VMEM((rows, width), F32),
            pltpu.VMEM((rows, width), F32),
            sems,
        ],
        1,
        1 + nb,
        flops=4 * mm,
    )
    input_grad, small, *grads_a = kernel_call(
        functools.partial(attention_backward, lay, seq, hd),
        [pos, tokens, w_a, ln1, qkv, probs, att, mid_grad, small, vec],
        [sds((seq, width), F32), sds((16, width), F32), *lay.grad_shapes(16)],
        [
            pltpu.VMEM((rows, width), F32),
            pltpu.VMEM((rows, 3 * wide), F32),
            pltpu.VMEM((width, width), F32),
            pltpu.VMEM((rows, width), F32),
        ],
        flops=2 * mm,
    )
    if fast:
        sum_c, sum_b, sum_a = [scatter_piece(*g) for g in (grads_c, grads_b, grads_a)]
        small = sum_a[chunk:]
    else:

        def scatter(g):
            g = lax.psum_scatter(g[0], "tensor", scatter_dimension=0, tiled=False)
            return lax.psum_scatter(g, "dp", scatter_dimension=0, tiled=True).astype(F32)

        sum_c, sum_b, sum_a = scatter(grads_c), scatter(grads_b), scatter(grads_a)
        small = lax.psum(small, ("dp", "tensor"))
    qkv_grad = jnp.stack([sum_a[:chunk, c * wide : (c + 1) * wide] for c in range(3)])
    proj_grad = sum_a[:chunk, 3 * wide : 4 * wide].T
    sub = chunk // groups
    vec_grad = lax.dynamic_slice(small, (0, d * chunk + z * sub), (6, sub))
    each = hd // n_dp
    fb_row = lax.dynamic_slice(small, (6 + z, 0), (1, units)).reshape(units // hd, hd)
    fc1b_grad = lax.dynamic_slice(fb_row, (0, d * each), (units // hd, each))
    qv_row = lax.dynamic_slice(small, (10 + z, 0), (1, 3 * wide)).reshape(3, heads, hd)
    qv_grad = lax.dynamic_slice(qv_row[0::2], (0, 0, d * each), (2, heads, each))
    return (
        output,
        input_grad,
        qkv_grad,
        qv_grad,
        proj_grad,
        vec_grad,
        sum_b,
        fc1b_grad,
        sum_c.T,
    )


def solution(mesh):
    return jax.shard_map(
        per_device,
        mesh=mesh,
        in_specs=(
            P(("dp", "tensor"), None),
            P(("dp", "tensor"), None),
            P(None, "dp", "tensor"),
            P(None, "tensor", "dp"),
            P("tensor", "dp"),
            P(None, "dp"),
            P("dp", "tensor"),
            P("tensor", "dp"),
            P("tensor", "dp"),
        ),
        out_specs=(
            P(("dp", "tensor"), None),
            P(("dp", "tensor"), None),
            P(None, "dp", "tensor"),
            P(None, "tensor", "dp"),
            P("tensor", "dp"),
            P(None, ("dp", "tensor")),
            P("dp", "tensor"),
            P("tensor", "dp"),
            P("tensor", "dp"),
        ),
        check_vma=False,
    )
```

```python
import functools

import jax
import jax.numpy as jnp
from jax import lax
from jax.experimental import pallas as pl
from jax.experimental.pallas import tpu as pltpu
from jax.sharding import PartitionSpec as P

BF = jnp.bfloat16
F32 = jnp.float32
norm_eps = 1e-06
half_root = 0.7071067811865476
density_scale = 0.3989422804014327
VMEM_LIMIT = 56 * 1024 * 1024


def nn(a, b):
    return jnp.dot(a, b, preferred_element_type=F32)


def nt(a, b):
    return lax.dot_general(a, b, (((1,), (1,)), ((), ())), preferred_element_type=F32)


def tn(a, b):
    return lax.dot_general(a, b, (((0,), (0,)), ((), ())), preferred_element_type=F32)


def norm_parts(values):
    centred = values - jnp.mean(values, axis=-1, keepdims=True)
    recip_root = lax.rsqrt(jnp.mean(centred * centred, axis=-1, keepdims=True) + norm_eps)
    return centred * recip_root, recip_root


def norm_back(upstream, normed, recip_root):
    first_mean = jnp.mean(upstream, axis=-1, keepdims=True)
    second_mean = jnp.mean(upstream * normed, axis=-1, keepdims=True)
    return recip_root * (upstream - first_mean - normed * second_mean)


def gelu_parts(values):
    cumul = 0.5 * (1.0 + lax.erf(values * half_root))
    return (values * cumul, cumul + values * jnp.exp(-0.5 * values * values) * density_scale)


class Layout:
    def __init__(self, fast, groups, width):
        self.fast, self.groups, self.width = fast, groups, width
        self.chunk = width // 8 if fast else width

    def t(self, j, pos):
        return lax.rem(pos[1] + (self.groups - j), self.groups) if self.fast else j

    def out(self, j):
        return (self.groups - j) % self.groups if self.fast else j

    def rows(self, k, pos):
        if not self.fast:
            return pl.ds(0, self.width)
        return pl.ds(pl.multiple_of((pos[0] ^ k) * self.chunk, self.chunk), self.chunk)

    def n_buffers(self):
        return 8 if self.fast else 1

    def n_blocks(self):
        return 8 if self.fast else 1

    def sources(self, bufs, j):
        if not self.fast:
            return [(bufs[0].at[j], 0)]
        found = []
        first, second = (AXIS_X, AXIS_Y) if j < 2 else (AXIS_Y, AXIS_X)
        for core in range(2):
            near, far = bufs[4 * core + 2 * (j // 2) :][:2]
            for ref, axis in ((near, 0), (far, second)):
                for n in range(2):
                    at = pl.ds((2 * n + j % 2) * self.chunk, self.chunk)
                    found.append((ref.at[at, :], axis ^ (first * n) ^ core))
        return found

    def start(self, bufs, dest, sems, pos):
        copies = []
        for j in range(self.groups):
            group = []
            for n, (src, k) in enumerate(self.sources(bufs, j)):
                copy = pltpu.make_async_copy(src, dest.at[j, self.rows(k, pos), :], sems.at[j, n])
                copy.start()
                group.append(copy)
            copies.append(group)
        return copies

    def put(self, scratch, outs, j, pos):
        if not self.fast:
            outs[0][j, :, :] = scratch[...].astype(BF)
            return
        for k in range(8):
            outs[k & 1][k >> 1, self.out(j), :, :] = scratch[self.rows(k, pos), :].astype(BF)

    def grad_shapes(self, wide):
        if not self.fast:
            return [jax.ShapeDtypeStruct((self.groups, self.width, wide), BF)]
        return [jax.ShapeDtypeStruct((4, self.groups, self.chunk, wide), BF)] * 2


SPARE = 64
CORE, AXIS_X, AXIS_Y = 1, 2, 4


def unit_order(width, n):
    i = lax.broadcasted_iota(jnp.int32, (width, width), 0)
    c = lax.broadcasted_iota(jnp.int32, (width, width), 1)
    per = width // n
    hit = i == (lax.rem(c, 64) // 8) * per + (c // 64) * 8 + lax.rem(c, 8)
    same = i == c
    return jnp.where(hit, 1.0, 0.0).astype(BF), jnp.where(same, 1.0, 0.0).astype(BF)


def kernel_call(body, pos, bufs, ins, outs, scratch):
    vmem, smem = pl.BlockSpec(memory_space=pltpu.VMEM), pl.BlockSpec(memory_space=pltpu.SMEM)
    return pl.pallas_call(
        body,
        out_shape=outs,
        in_specs=[smem] + [pl.BlockSpec(memory_space=pl.ANY)] * len(bufs) + [vmem] * len(ins),
        out_specs=[vmem] * len(outs),
        scratch_shapes=scratch,
        compiler_params=pltpu.CompilerParams(vmem_limit_bytes=VMEM_LIMIT),
        cost_estimate=pl.CostEstimate(flops=0, bytes_accessed=0, transcendentals=0),
    )(pos, *bufs, *ins)


def split_refs(refs, n_bufs, n_in, n_out):
    bufs, refs = refs[:n_bufs], refs[n_bufs:]
    return bufs, refs[:n_in], refs[n_in : n_in + n_out], refs[n_in + n_out :]


def prepare_qkv(qkv_ref, vec_ref, qv_ref, fb_ref, out_ref, rows_ref, fb_pad, qv_pad):
    wide, chunk = qkv_ref.shape[2], qkv_ref.shape[1]
    heads, each = qv_ref.shape[0], qv_ref.shape[2]
    for c in range(3):
        out_ref[:, c * wide : (c + 1) * wide] = qkv_ref[c]
    for ref in (rows_ref, fb_pad, qv_pad):
        ref[...] = jnp.zeros_like(ref)
    rows_ref[0 : vec_ref.shape[0], :] = vec_ref[...].astype(F32)
    fb_pad[0:each, 0 : fb_ref.shape[1]] = fb_ref[...].astype(F32)
    for h in range(heads):
        both = qv_ref[h].astype(F32)
        qv_pad[h : h + 1, 0:each] = both[0:1]
        qv_pad[2 * heads + h : 2 * heads + h + 1, 0:each] = both[1:2]
    row = lax.broadcasted_iota(jnp.int32, (16, SPARE), 0)
    col = lax.broadcasted_iota(jnp.int32, (16, SPARE), 1)
    spare = tn(rows_ref[...].astype(BF), jnp.where(row == col, 1.0, 0.0).astype(BF))
    at = lax.broadcasted_iota(jnp.int32, (chunk, 16), 0)
    slot = lax.broadcasted_iota(jnp.int32, (chunk, 16), 1)
    by_group = jnp.where(at // each == slot, 1.0, 0.0).astype(BF)
    by_unit = jnp.where(lax.rem(at, each) == slot, 1.0, 0.0).astype(BF)
    at = lax.broadcasted_iota(jnp.int32, (chunk, 128), 0)
    lane = lax.broadcasted_iota(jnp.int32, (chunk, 128), 1)
    out_col = lax.broadcasted_iota(jnp.int32, (chunk, SPARE), 1)
    fb = jnp.where(lane == at // each, nn(by_unit, fb_pad[...].astype(BF)), 0.0)
    qv = jnp.where(lane == lax.rem(at, each), nn(by_group, qv_pad[...].astype(BF)), 0.0)
    for c, spread in ((6, fb), (7, qv)):
        spare += jnp.where(out_col == c, jnp.sum(spread, axis=1, keepdims=True), 0.0)
    out_ref[:, 3 * wide : 3 * wide + SPARE] = spare.astype(BF)


def prepare_fc1(fc1_ref, proj_ref, out_ref):
    width, wide = fc1_ref.shape[1], proj_ref.shape[0]
    out_ref[:, 0:width] = fc1_ref[...]
    row = lax.broadcasted_iota(jnp.int32, (wide, wide), 0)
    col = lax.broadcasted_iota(jnp.int32, (wide, wide), 1)
    one = jnp.where(row == col, 1.0, 0.0).astype(BF)
    out_ref[:, width:] = jnp.zeros_like(out_ref[:, width:])
    out_ref[:, width : width + wide] = tn(proj_ref[...], one).astype(BF)


def pad_rows(dest, source, seq):
    dest[...] = jnp.zeros_like(dest)
    dest[0:seq, :] = source[...].astype(dest.dtype)


def attention_forward(lay, seq, hd, pos, *refs):
    bufs, ins, outs, scratch = split_refs(refs, lay.n_buffers(), 2, 5)
    tok_ref, par_in = ins
    ln_ref, qkv_ref, probs_ref, att_ref, par_ref = outs
    x_ref, w_ref, sems = scratch
    copies = lay.start(bufs, w_ref, sems, pos)
    pad_rows(x_ref, tok_ref, seq)
    rows = x_ref.shape[0]
    wide = att_ref.shape[2]
    heads = wide // hd
    normed, _ = norm_parts(x_ref[...])
    if lay.fast:
        width = lay.width
        order, _ = unit_order(width, 8)
        row = lax.broadcasted_iota(jnp.int32, (16, SPARE), 0)
        col = lax.broadcasted_iota(jnp.int32, (16, SPARE), 1)
        par = jnp.zeros((16, width), F32)
        units = jnp.zeros((16, width), F32)
        for j in range(lay.groups):
            for copy in copies[j]:
                copy.wait()
            spare = w_ref[j, :, 3 * wide : 3 * wide + SPARE]
            t = lay.t(j, pos)
            if j == 0:
                par = nt(jnp.where((row == col) & (row < 6), 1.0, 0.0).astype(BF), spare)
            pick = ((row == 6 + t) & (col == 6)) | ((row == 10 + t) & (col == 7))
            units += nt(jnp.where(pick, 1.0, 0.0).astype(BF), spare)
        par_ref[...] = par + nn(units.astype(BF), order)
    else:
        for j in range(lay.groups):
            for copy in copies[j]:
                copy.wait()
        par_ref[...] = par_in[...]
    ln = (normed * par_ref[0:1, :] + par_ref[1:2, :]).astype(BF)
    ln_ref[...] = ln
    valid = lax.broadcasted_iota(jnp.int32, (rows, rows), 1) < seq
    for j in range(lay.groups):
        bias = par_ref[pl.ds(10 + lay.t(j, pos), 1), 0 : 3 * wide]
        qkv_ref[j, :, :] = (nn(ln, w_ref[j, :, 0 : 3 * wide]) + bias).astype(BF)
        for h in range(heads):
            q = qkv_ref[j, :, h * hd : (h + 1) * hd]
            k = qkv_ref[j, :, wide + h * hd : wide + (h + 1) * hd]
            v = qkv_ref[j, :, 2 * wide + h * hd : 2 * wide + (h + 1) * hd]
            scores = jnp.where(valid, nt(q, k) * (hd**-0.5), -1e30)
            top = jnp.max(scores, axis=-1, keepdims=True)
            e = jnp.exp(scores - top)
            p = (e * (1.0 / jnp.sum(e, axis=-1, keepdims=True))).astype(BF)
            probs_ref[j * heads + h, :, :] = p
            att_ref[j, :, h * hd : (h + 1) * hd] = nn(p, v).astype(BF)


def feed_forward(lay, seq, pos, *refs):
    bufs, ins, outs, scratch = split_refs(refs, lay.n_buffers(), 4, 4 + (2 if lay.fast else 1))
    tok_ref, att_ref, cot_ref, par_ref = ins
    mid_ref, ln_ref, act_ref, slope_ref = outs[:4]
    cotp_ref, g_ref, w_ref, sems = scratch
    copies = lay.start(bufs, w_ref, sems, pos)
    pad_rows(cotp_ref, cot_ref, seq)
    pad_rows(mid_ref, tok_ref, seq)
    width, wide = lay.width, att_ref.shape[2]
    mid = mid_ref[...] + par_ref[2:3, :]
    for j in range(lay.groups):
        for copy in copies[j]:
            copy.wait()
        mid += nt(att_ref[j], w_ref[j, :, width : width + wide])
    mid_ref[...] = mid
    normed, _ = norm_parts(mid)
    ln = (normed * par_ref[3:4, :] + par_ref[4:5, :]).astype(BF)
    ln_ref[...] = ln
    for j in range(lay.groups):
        bias = par_ref[pl.ds(6 + lay.t(j, pos), 1), :]
        act, slope = gelu_parts(nn(ln, w_ref[j, :, 0:width]) + bias)
        act_ref[j, :, :] = act.astype(BF)
        slope_ref[j, :, :] = slope.astype(BF)
        g_ref[...] = tn(cotp_ref[...], act_ref[j])
        lay.put(g_ref, outs[4:], j, pos)


def feed_backward(lay, seq, pos, *refs):
    nb = lay.n_buffers()
    bufs, ins, outs, scratch = split_refs(refs, 2 * nb, 4, 4)
    slope_ref, mid_ref, cot_ref, par_ref = ins
    mg_ref, ag_ref, pg_ref, small_ref = outs
    w1_ref, w2_ref, cotp_ref, ln_acc, sems1, sems2 = scratch
    copies = lay.start(bufs[nb:], w2_ref, sems2, pos)
    copies = [a + b for a, b in zip(copies, lay.start(bufs[:nb], w1_ref, sems1, pos))]
    pad_rows(cotp_ref, cot_ref, seq)
    cot = cotp_ref[...]
    width, wide = lay.width, ag_ref.shape[2]
    small_ref[...] = jnp.zeros_like(small_ref)
    ln_acc[...] = jnp.zeros_like(ln_acc)
    for j in range(lay.groups):
        for copy in copies[j]:
            copy.wait()
        pre_grad = nn(cot, w2_ref[j]) * slope_ref[j].astype(F32)
        small_ref[pl.ds(6 + lay.t(j, pos), 1), :] = jnp.sum(pre_grad, axis=0, keepdims=True)
        pgb = pre_grad.astype(BF)
        pg_ref[j, :, :] = pgb
        ln_acc[...] += nt(pgb, w1_ref[j, :, 0:width])
    normed, root = norm_parts(mid_ref[...])
    grad = ln_acc[...]
    cotf = cot.astype(F32)
    mid_grad = cotf + norm_back(grad * par_ref[3:4, :], normed, root)
    mg_ref[...] = mid_grad
    small_ref[2:3, :] = jnp.sum(mid_grad, axis=0, keepdims=True)
    small_ref[3:4, :] = jnp.sum(grad * normed, axis=0, keepdims=True)
    small_ref[4:5, :] = jnp.sum(grad, axis=0, keepdims=True)
    small_ref[5:6, :] = jnp.sum(cotf, axis=0, keepdims=True)
    mgb = mid_grad.astype(BF)
    for j in range(lay.groups):
        ag_ref[j, :, :] = nn(mgb, w1_ref[j, :, width : width + wide]).astype(BF)


def feed_output(lay, seq, pos, *refs):
    bufs, ins, (out_ref,), (w_ref, acc, sems) = split_refs(refs, lay.n_buffers(), 3, 1)
    act_ref, mid_ref, par_ref = ins
    copies = lay.start(bufs, w_ref, sems, pos)
    acc[...] = mid_ref[...] + par_ref[5:6, :]
    for j in range(lay.groups):
        for copy in copies[j]:
            copy.wait()
        acc[...] += nt(act_ref[j], w_ref[j])
    out_ref[...] = acc[0:seq, :].astype(BF)


def feed_weights(lay, pos, *refs):
    ln_ref, pg_ref, mg_ref, att_ref, *outs, g_ref = refs
    width, wide = lay.width, att_ref.shape[2]
    ln = ln_ref[...]
    mgb = mg_ref[...].astype(BF)
    g_ref[...] = jnp.zeros_like(g_ref)
    for j in range(lay.groups):
        g_ref[:, 0:width] = tn(ln, pg_ref[j])
        g_ref[:, width : width + wide] = tn(mgb, att_ref[j])
        lay.put(g_ref, outs, j, pos)


def attention_backward(lay, seq, hd, pos, *refs):
    bufs, ins, outs, scratch = split_refs(refs, lay.n_buffers(), 8, 3)
    tok_ref, qkv_ref, probs_ref, att_ref, ag_ref, mg_ref, small_in, par_ref = ins
    dx_ref, small_ref, db_ref = outs
    x_ref, w_ref, dqkv_ref, ln_acc, sems = scratch
    copies = lay.start(bufs, w_ref, sems, pos)
    wide = att_ref.shape[2]
    heads = wide // hd
    scale = hd**-0.5
    small_ref[...] = small_in[...]
    pad_rows(x_ref, tok_ref, seq)
    ln_acc[...] = jnp.zeros_like(ln_acc)
    three = slice(0, 3 * wide)
    for j in range(lay.groups):
        for copy in copies[j]:
            copy.wait()
        att_grad = ag_ref[j]
        prod = att_grad.astype(F32) * att_ref[j].astype(F32)
        for h in range(heads):
            at = slice(h * hd, (h + 1) * hd)
            q = qkv_ref[j, :, h * hd : (h + 1) * hd]
            k = qkv_ref[j, :, wide + h * hd : wide + (h + 1) * hd]
            v = qkv_ref[j, :, 2 * wide + h * hd : 2 * wide + (h + 1) * hd]
            p = probs_ref[j * heads + h]
            da = att_grad[:, at]
            delta = jnp.sum(prod[:, at], axis=-1, keepdims=True)
            ds = (p.astype(F32) * (nt(da, v) - delta) * scale).astype(BF)
            dqkv_ref[:, h * hd : (h + 1) * hd] = nn(ds, k)
            dqkv_ref[:, wide + h * hd : wide + (h + 1) * hd] = tn(ds, q)
            dqkv_ref[:, 2 * wide + h * hd : 2 * wide + (h + 1) * hd] = tn(p, da)
        dqkv = dqkv_ref[...]
        small_ref[pl.ds(10 + lay.t(j, pos), 1), three] = jnp.sum(dqkv, axis=0, keepdims=True)
        dqkv = dqkv.astype(BF)
        db_ref[j, :, :] = dqkv
        ln_acc[...] += nt(dqkv, w_ref[j, :, three])
    normed, root = norm_parts(x_ref[...])
    grad = ln_acc[...]
    dx = mg_ref[...] + norm_back(grad * par_ref[0:1, :], normed, root)
    dx_ref[...] = dx[0:seq, :]
    small_ref[0:1, :] = jnp.sum(grad * normed, axis=0, keepdims=True)
    small_ref[1:2, :] = jnp.sum(grad, axis=0, keepdims=True)


def attention_weights(lay, pos, *refs):
    ln_ref, db_ref, small_ref, *outs, g_ref = refs
    width, three = lay.width, db_ref.shape[2]
    ln = ln_ref[...]
    g_ref[:, three:] = jnp.zeros((width, SPARE), F32)
    if lay.fast:
        small = small_ref[...].astype(BF)
        order, same = unit_order(width, 8)
        col = lax.broadcasted_iota(jnp.int32, (width, 16), 1)
        g_ref[:, three : three + 16] = jnp.where(col < 6, nt(same, small), nt(order, small))
    for j in range(lay.groups):
        g_ref[:, 0:three] = tn(ln, db_ref[j])
        lay.put(g_ref, outs, j, pos)


def shift(x, by):
    n = lax.axis_size("tensor")
    return lax.ppermute(x, "tensor", [(i, (i + by) % n) for i in range(n)])


def flip(x, bit):
    n = lax.axis_size("dp")
    return lax.ppermute(x, "dp", [(i, i ^ bit) for i in range(n)])


def gather_columns(piece):
    return [piece] + [shift(piece, k) for k in (1, 2, 3)]


def join(a, b):
    return jnp.concatenate([a, b], axis=0)


def gather_near(h):
    return flip(h[0], AXIS_X), flip(h[1], AXIS_Y)


def gather_far(both):
    return flip(both[0], AXIS_Y), flip(both[1], AXIS_X)


def flip_cores(blocks):
    return [flip(b, CORE) for b in blocks]


def in_order(near, far, core_near, core_far):
    return [near[0], far[0], near[1], far[1], core_near[0], core_far[0], core_near[1], core_far[1]]


def add(a, b):
    return (a.astype(F32) + b.astype(F32)).astype(BF)


class Scatter:
    def __init__(self, mine, theirs):
        self.mine, self.recv = mine, flip(theirs, CORE)

    def first(self):
        low, high = (slice(2, 4), slice(0, 2)), (slice(1, 4, 2), slice(2, 4))
        return [add(self.mine[at], self.recv[at]) for at in (low, high)]

    def send_first(self, values):
        return [flip(values[0], AXIS_Y), flip(values[1], AXIS_X)]

    def second(self, got):
        low, high = (slice(0, 2), slice(0, 2)), (slice(0, 4, 2), slice(2, 4))
        return [
            add(self.mine[at].astype(F32) + self.recv[at].astype(F32), part)
            for at, part in zip((low, high), got)
        ]

    def send_second(self, values):
        return [flip(values[0][1], AXIS_X), flip(values[1][1], AXIS_Y)]

    def third(self, values, got):
        low = values[0][0].astype(F32) + got[0].astype(F32)
        high = values[1][0].astype(F32) + got[1].astype(F32)
        return [low[0], low[1].astype(BF), high[0].astype(BF), high[1].astype(BF)]

    def send_third(self, parts):
        return [shift(parts[k], k) for k in (1, 2, 3)]

    def last(self, parts, got):
        total = parts[0]
        for part in got:
            total = total + part.astype(F32)
        return total


def barrier(*groups):
    flat, tree = jax.tree.flatten(groups)
    return jax.tree.unflatten(tree, lax.optimization_barrier(tuple(flat)))


def per_device(
    tokens, cotangent, qkv_weight, qv_bias, proj_weight, vectors, fc1_weight, fc1_bias, fc2_weight
):
    n_dp, groups = lax.axis_size("dp"), lax.axis_size("tensor")
    seq, width = tokens.shape
    chunk, wide = qkv_weight.shape[1], qkv_weight.shape[2]
    heads, each = qv_bias.shape[1], qv_bias.shape[2]
    hd = each * n_dp
    units = fc1_weight.shape[1]
    fast = n_dp == 8 and groups == 4
    lay = Layout(fast, groups, width)
    d, z = lax.axis_index("dp"), lax.axis_index("tensor")
    pos = jnp.stack([d, z]).astype(jnp.int32)
    three = 3 * wide
    rows = -(-seq // 16) * 16
    sds = jax.ShapeDtypeStruct
    nb = lay.n_buffers()
    sems = pltpu.SemaphoreType.DMA((groups, lay.n_blocks()))
    wide_a, wide_b = three + SPARE, -(-(width + wide) // 128) * 128

    def run_attention_forward(bufs, par):
        return kernel_call(
            functools.partial(attention_forward, lay, seq, hd),
            pos,
            bufs,
            [tokens, par],
            [
                sds((rows, width), BF),
                sds((groups, rows, three), BF),
                sds((groups * heads, rows, rows), BF),
                sds((groups, rows, wide), BF),
                sds((16, width), F32),
            ],
            [pltpu.VMEM((rows, width), F32), pltpu.VMEM((groups, width, wide_a), BF), sems],
        )

    def run_feed_forward(bufs, att, par):
        return kernel_call(
            functools.partial(feed_forward, lay, seq),
            pos,
            bufs,
            [tokens, att, cotangent, par],
            [
                sds((rows, width), F32),
                sds((rows, width), BF),
                sds((groups, rows, units), BF),
                sds((groups, rows, units), BF),
                *lay.grad_shapes(width),
            ],
            [
                pltpu.VMEM((rows, width), BF),
                pltpu.VMEM((width, width), F32),
                pltpu.VMEM((groups, width, wide_b), BF),
                sems,
            ],
        )

    def run_feed_backward(bufs, slope, mid, par):
        return kernel_call(
            functools.partial(feed_backward, lay, seq),
            pos,
            bufs,
            [slope, mid, cotangent, par],
            [
                sds((rows, width), F32),
                sds((groups, rows, wide), BF),
                sds((groups, rows, units), BF),
                sds((16, width), F32),
            ],
            [
                pltpu.VMEM((groups, width, wide_b), BF),
                pltpu.VMEM((groups, width, width), BF),
                pltpu.VMEM((rows, width), BF),
                pltpu.VMEM((rows, width), F32),
                sems,
                sems,
            ],
        )

    def run_feed_output(bufs, act, mid, par):
        return kernel_call(
            functools.partial(feed_output, lay, seq),
            pos,
            bufs,
            [act, mid, par],
            [sds((seq, width), BF)],
            [pltpu.VMEM((groups, width, width), BF), pltpu.VMEM((rows, width), F32), sems],
        )[0]

    def run_feed_weights(ln2, pre_grad, mid_grad, att):
        return kernel_call(
            functools.partial(feed_weights, lay),
            pos,
            [],
            [ln2, pre_grad, mid_grad, att],
            lay.grad_shapes(wide_b),
            [pltpu.VMEM((width, wide_b), F32)],
        )

    def run_attention_backward(bufs, qkv, probs, att, att_grad, mid_grad, small, par):
        return kernel_call(
            functools.partial(attention_backward, lay, seq, hd),
            pos,
            bufs,
            [tokens, qkv, probs, att, att_grad, mid_grad, small, par],
            [sds((seq, width), F32), sds((16, width), F32), sds((groups, rows, three), BF)],
            [
                pltpu.VMEM((rows, width), F32),
                pltpu.VMEM((groups, width, wide_a), BF),
                pltpu.VMEM((rows, three), F32),
                pltpu.VMEM((rows, width), F32),
                sems,
            ],
        )

    def run_attention_weights(ln1, act_grads, small):
        return kernel_call(
            functools.partial(attention_weights, lay),
            pos,
            [],
            [ln1, act_grads, small],
            lay.grad_shapes(wide_a),
            [pltpu.VMEM((width, wide_a), F32)],
        )

    sub = chunk // groups
    if fast:
        vmem = pl.BlockSpec(memory_space=pltpu.VMEM)
        piece_a = pl.pallas_call(
            prepare_qkv,
            out_shape=sds((chunk, wide_a), BF),
            in_specs=[vmem] * 4,
            out_specs=vmem,
            scratch_shapes=[
                pltpu.VMEM((16, chunk), F32),
                pltpu.VMEM((16, 128), F32),
                pltpu.VMEM((16, 128), F32),
            ],
        )(qkv_weight, vectors, qv_bias.transpose(1, 0, 2), fc1_bias.T)
        piece_b = pl.pallas_call(
            prepare_fc1,
            out_shape=sds((chunk, wide_b), BF),
            in_specs=[vmem] * 2,
            out_specs=vmem,
        )(fc1_weight, proj_weight)
        piece_c = fc2_weight.T
        z_a = gather_columns(piece_a)
        z_a, piece_b = barrier(z_a, piece_b)
        h_a = barrier(join(*z_a[0:2]), join(*z_a[2:4]))
        near_a = gather_near(h_a)
        z_b = gather_columns(piece_b)
        both_a = barrier(join(h_a[0], near_a[0]), join(h_a[1], near_a[1]))
        far_a = gather_far(both_a)
        z_b, both_a = barrier(z_b, both_a)
        core_a = flip_cores(both_a)
        h_b = join(*z_b[0:2]), join(*z_b[2:4])
        far_a, core_a, h_b = barrier(far_a, core_a, h_b)
        near_b = gather_near(h_b)
        bufs_a = in_order(both_a, far_a, core_a, flip_cores(far_a))
        ln1, qkv, probs, att, par = run_attention_forward(bufs_a, jnp.zeros((16, width), F32))

        near_b, piece_c, att = barrier(near_b, piece_c, att)
        both_b = barrier(join(h_b[0], near_b[0]), join(h_b[1], near_b[1]))
        far_b = gather_far(both_b)
        z_c = gather_columns(piece_c)
        z_c, both_b = barrier(z_c, both_b)
        core_b = flip_cores(both_b)
        h_c = join(*z_c[0:2]), join(*z_c[2:4])
        far_b, core_b, h_c = barrier(far_b, core_b, h_c)
        near_c = gather_near(h_c)
        bufs_b = in_order(both_b, far_b, core_b, flip_cores(far_b))
        mid, ln2, act, slope, *grads_c = run_feed_forward(bufs_b, att, par)

        near_c, mid, grads_c = barrier(near_c, mid, grads_c)
        both_c = barrier(join(h_c[0], near_c[0]), join(h_c[1], near_c[1]))
        far_c = gather_far(both_c)
        way_c = Scatter(*grads_c)
        first_c = way_c.first()
        core_c = flip_cores(both_c)
        first_c, core_c = barrier(first_c, core_c)
        got_c = way_c.send_first(first_c)
        far_c = barrier(*far_c)
        bufs_c = in_order(both_c, far_c, core_c, flip_cores(far_c))
        mid_grad, att_grad, pre_grad, small = run_feed_backward([*bufs_b, *bufs_c], slope, mid, par)

        got_c, pre_grad, mid_grad = barrier(got_c, pre_grad, mid_grad)
        second_c = way_c.second(got_c)
        second_c, pre_grad = barrier(second_c, pre_grad)
        got_c = way_c.send_second(second_c)
        grads_b = run_feed_weights(ln2, pre_grad, mid_grad, att)
        got_c, grads_b, act = barrier(got_c, grads_b, act)
        way_b = Scatter(*grads_b)
        third_c = way_c.third(second_c, got_c)
        third_c, act = barrier(third_c, act)
        got_c = way_c.send_third(third_c)
        output = run_feed_output(bufs_c, act, mid, par)
        first_b = way_b.first()
        first_b, output, mid_grad = barrier(first_b, output, mid_grad)
        got_b = way_b.send_first(first_b)
        input_grad, small, act_grads = run_attention_backward(
            bufs_a, qkv, probs, att, att_grad, mid_grad, small, par
        )
        grads_a = run_attention_weights(ln1, act_grads, small)
        got_b, grads_a, got_c = barrier(got_b, grads_a, got_c)
        way_a = Scatter(*grads_a)
        second_b = way_b.second(got_b)
        second_b, got_c = barrier(second_b, got_c)
        got_b = way_b.send_second(second_b)
        sum_c = way_c.last(third_c, got_c)
        first_a = way_a.first()
        first_a, sum_c = barrier(first_a, sum_c)
        got_a = way_a.send_first(first_a)
        third_b = way_b.third(second_b, got_b)
        third_b, first_a = barrier(third_b, first_a)
        got_b = way_b.send_third(third_b)
        second_a = way_a.second(got_a)
        second_a = barrier(*second_a)
        got_a = way_a.send_second(second_a)
        third_a = way_a.third(second_a, got_a)
        third_a, got_b = barrier(third_a, got_b)
        got_a = way_a.send_third(third_a)
        sum_b = way_b.last(third_b, got_b)
        sum_b, got_a = barrier(sum_b, got_a)
        sum_a = way_a.last(third_a, got_a)
        vec_grad = lax.dynamic_slice(sum_a, (z * sub, three), (sub, 6)).T
        fc1b_grad = lax.dynamic_slice(sum_a, (0, three + 6 + z), (chunk, 1))
        qv_grad = lax.dynamic_slice(sum_a, (0, three + 10 + z), (chunk, 1))
    else:
        none = jnp.zeros_like(qv_bias[0])
        qkv_col = jnp.stack([qv_bias[0], none, qv_bias[1], none]).reshape(chunk)
        spare = jnp.concatenate([vectors, fc1_bias.reshape(1, chunk), qkv_col[None]], axis=0).T
        spare = jnp.pad(spare, ((0, 0), (0, SPARE - spare.shape[1])))
        piece_a = jnp.concatenate([qkv_weight[0], qkv_weight[1], qkv_weight[2], spare], axis=1)
        piece_b = jnp.concatenate([fc1_weight, proj_weight.T], axis=1)
        piece_b = jnp.pad(piece_b, ((0, 0), (0, wide_b - width - wide)))

        def gather(p):
            return [lax.all_gather(lax.all_gather(p, "dp", axis=0, tiled=True), "tensor", axis=0)]

        bufs_a, bufs_b, bufs_c = gather(piece_a), gather(piece_b), gather(fc2_weight.T)
        cols = bufs_a[0][:, :, three : three + 8]
        vec = cols[0, :, 0:6].T
        by_unit = cols.reshape(groups, n_dp, chunk // each, each, 8).transpose(0, 4, 2, 1, 3)
        by_unit = by_unit.reshape(groups, 8, width)
        par = jnp.concatenate([vec, by_unit[:, 6], by_unit[:, 7]], axis=0).astype(F32)
        par = jnp.pad(par, ((0, 16 - par.shape[0]), (0, 0)))
        ln1, qkv, probs, att, par = run_attention_forward(bufs_a, par)
        mid, ln2, act, slope, grads_c = run_feed_forward(bufs_b, att, par)
        mid_grad, att_grad, pre_grad, small = run_feed_backward([*bufs_b, *bufs_c], slope, mid, par)
        output = run_feed_output(bufs_c, act, mid, par)
        (grads_b,) = run_feed_weights(ln2, pre_grad, mid_grad, att)
        input_grad, small, act_grads = run_attention_backward(
            bufs_a, qkv, probs, att, att_grad, mid_grad, small, par
        )
        (grads_a,) = run_attention_weights(ln1, act_grads, small)

        def scatter(g):
            g = lax.psum_scatter(g, "tensor", scatter_dimension=0, tiled=False)
            return lax.psum_scatter(g, "dp", scatter_dimension=0, tiled=True).astype(F32)

        sum_c, sum_b, sum_a = scatter(grads_c), scatter(grads_b), scatter(grads_a)
        small = lax.psum(small, ("dp", "tensor"))
        vec_grad = lax.dynamic_slice(small, (0, d * chunk + z * sub), (6, sub))
        by_unit = small[6:14].reshape(2, groups, chunk // each, hd)
        by_unit = lax.dynamic_slice(
            by_unit, (0, z, 0, d * each), (2, 1, chunk // each, each)
        ).reshape(2, chunk)
        fc1b_grad, qv_grad = by_unit[0], by_unit[1]
    fc1b_grad = fc1b_grad.reshape(fc1_bias.shape)
    qv_grad = qv_grad.reshape(4, heads, each)[0::2]
    qkv_grad = jnp.stack([sum_a[:, c * wide : (c + 1) * wide] for c in range(3)])
    return (
        output,
        input_grad,
        qkv_grad,
        qv_grad,
        sum_b[:, width : width + wide].T,
        vec_grad,
        sum_b[:, :width],
        fc1b_grad,
        sum_c.T,
    )


def solution(mesh):
    return jax.shard_map(
        per_device,
        mesh=mesh,
        in_specs=(
            P(("dp", "tensor"), None),
            P(("dp", "tensor"), None),
            P(None, "dp", "tensor"),
            P(None, "tensor", "dp"),
            P("tensor", "dp"),
            P(None, "dp"),
            P("dp", "tensor"),
            P("tensor", "dp"),
            P("tensor", "dp"),
        ),
        out_specs=(
            P(("dp", "tensor"), None),
            P(("dp", "tensor"), None),
            P(None, "dp", "tensor"),
            P(None, "tensor", "dp"),
            P("tensor", "dp"),
            P(None, ("dp", "tensor")),
            P("dp", "tensor"),
            P("tensor", "dp"),
            P("tensor", "dp"),
        ),
        check_vma=False,
    )
```

```python
import functools

import jax
import jax.numpy as jnp
from jax import lax
from jax.experimental import pallas as pl
from jax.experimental.pallas import tpu as pltpu
from jax.sharding import PartitionSpec as P

BF = jnp.bfloat16
F32 = jnp.float32
norm_eps = 1e-06
half_root = 0.7071067811865476
density_scale = 0.3989422804014327
VMEM_LIMIT = 56 * 1024 * 1024


def nn(a, b):
    return jnp.dot(a, b, preferred_element_type=F32)


def nt(a, b):
    return lax.dot_general(a, b, (((1,), (1,)), ((), ())), preferred_element_type=F32)


def tn(a, b):
    return lax.dot_general(a, b, (((0,), (0,)), ((), ())), preferred_element_type=F32)


def norm_parts(values):
    centred = values - jnp.mean(values, axis=-1, keepdims=True)
    recip_root = lax.rsqrt(jnp.mean(centred * centred, axis=-1, keepdims=True) + norm_eps)
    return centred * recip_root, recip_root


def norm_back(upstream, normed, recip_root):
    first_mean = jnp.mean(upstream, axis=-1, keepdims=True)
    second_mean = jnp.mean(upstream * normed, axis=-1, keepdims=True)
    return recip_root * (upstream - first_mean - normed * second_mean)


def gelu_parts(values):
    cumul = 0.5 * (1.0 + lax.erf(values * half_root))
    return (values * cumul, cumul + values * jnp.exp(-0.5 * values * values) * density_scale)


class Layout:
    def __init__(self, fast, groups, width):
        self.fast, self.groups, self.width = fast, groups, width
        self.chunk = width // 8 if fast else width

    def t(self, j, pos):
        return lax.rem(pos[1] + (self.groups - j), self.groups) if self.fast else j

    def out(self, j):
        return (self.groups - j) % self.groups if self.fast else j

    def rows(self, k, pos):
        if not self.fast:
            return pl.ds(0, self.width)
        return pl.ds(pl.multiple_of((pos[0] ^ k) * self.chunk, self.chunk), self.chunk)

    def n_buffers(self):
        return 8 if self.fast else 1

    def n_blocks(self):
        return 8 if self.fast else 1

    def sources(self, bufs, j):
        if not self.fast:
            return [(bufs[0].at[j], 0)]
        found = []
        first, second = (AXIS_X, AXIS_Y) if j < 2 else (AXIS_Y, AXIS_X)
        for core in range(2):
            near, far = bufs[4 * core + 2 * (j // 2) :][:2]
            for ref, axis in ((near, 0), (far, second)):
                for n in range(2):
                    at = pl.ds((2 * n + j % 2) * self.chunk, self.chunk)
                    found.append((ref.at[at, :], axis ^ (first * n) ^ core))
        return found

    def fetch(self, bufs, dest, sems, pos):
        def begin(j):
            found = []
            for n, (src, k) in enumerate(self.sources(bufs, j)):
                copy = pltpu.make_async_copy(src, dest.at[j, self.rows(k, pos), :], sems.at[j, n])
                copy.start()
                found.append(copy)
            return found

        copies = [begin(0), begin(1)]

        def use(j):
            for copy in copies[j]:
                copy.wait()
            if j + 2 < self.groups:
                copies.append(begin(j + 2))

        return use

    def put(self, grad, stage, outs, sems, j, pos):
        at = self.out(j)
        if not self.fast:
            stage[at, :, :] = grad
            copies = [pltpu.make_async_copy(stage.at[at], outs[0].at[at], sems.at[j, 0])]
        else:
            for r in range(8):
                other = pos[0] ^ r
                stage[other & 1, other >> 1, at, :, :] = grad[r * self.chunk : (r + 1) * self.chunk]
            copies = [
                pltpu.make_async_copy(stage.at[n, :, at], outs[n].at[:, at], sems.at[j, n])
                for n in range(2)
            ]
        for copy in copies:
            copy.start()
        return copies

    def stage_shapes(self, wide):
        shape = (2, 4, self.groups, self.chunk, wide) if self.fast else (self.groups, self.width, wide)
        return [pltpu.VMEM(shape, BF), pltpu.SemaphoreType.DMA((self.groups, 2))]

    def n_grads(self):
        return 2 if self.fast else 1

    def grad_shapes(self, wide):
        if not self.fast:
            return [jax.ShapeDtypeStruct((self.groups, self.width, wide), BF)]
        return [jax.ShapeDtypeStruct((4, self.groups, self.chunk, wide), BF)] * 2


SPARE = 64
CORE, AXIS_X, AXIS_Y = 1, 2, 4


def unit_order(width, n):
    i = lax.broadcasted_iota(jnp.int32, (width, width), 0)
    c = lax.broadcasted_iota(jnp.int32, (width, width), 1)
    per = width // n
    hit = i == (lax.rem(c, 64) // 8) * per + (c // 64) * 8 + lax.rem(c, 8)
    same = i == c
    return jnp.where(hit, 1.0, 0.0).astype(BF), jnp.where(same, 1.0, 0.0).astype(BF)


def kernel_call(body, pos, bufs, ins, outs, scratch, n_any=0):
    in_hbm = pl.BlockSpec(memory_space=pl.ANY)
    vmem, smem = pl.BlockSpec(memory_space=pltpu.VMEM), pl.BlockSpec(memory_space=pltpu.SMEM)
    return pl.pallas_call(
        body,
        out_shape=outs,
        in_specs=[smem] + [in_hbm] * len(bufs) + [vmem] * len(ins),
        out_specs=[vmem] * (len(outs) - n_any) + [in_hbm] * n_any,
        scratch_shapes=scratch,
        compiler_params=pltpu.CompilerParams(vmem_limit_bytes=VMEM_LIMIT),
        cost_estimate=pl.CostEstimate(flops=0, bytes_accessed=0, transcendentals=0),
    )(pos, *bufs, *ins)


def split_refs(refs, n_bufs, n_in, n_out):
    bufs, refs = refs[:n_bufs], refs[n_bufs:]
    return bufs, refs[:n_in], refs[n_in : n_in + n_out], refs[n_in + n_out :]


def prepare_qkv(qkv_ref, vec_ref, qv_ref, fb_ref, out_ref, rows_ref, fb_pad, qv_pad):
    wide, chunk = qkv_ref.shape[2], qkv_ref.shape[1]
    heads, each = qv_ref.shape[0], qv_ref.shape[2]
    for c in range(3):
        out_ref[:, c * wide : (c + 1) * wide] = qkv_ref[c]
    for ref in (rows_ref, fb_pad, qv_pad):
        ref[...] = jnp.zeros_like(ref)
    rows_ref[0 : vec_ref.shape[0], :] = vec_ref[...].astype(F32)
    fb_pad[0:each, 0 : fb_ref.shape[1]] = fb_ref[...].astype(F32)
    for h in range(heads):
        both = qv_ref[h].astype(F32)
        qv_pad[h : h + 1, 0:each] = both[0:1]
        qv_pad[2 * heads + h : 2 * heads + h + 1, 0:each] = both[1:2]
    row = lax.broadcasted_iota(jnp.int32, (16, SPARE), 0)
    col = lax.broadcasted_iota(jnp.int32, (16, SPARE), 1)
    spare = tn(rows_ref[...].astype(BF), jnp.where(row == col, 1.0, 0.0).astype(BF))
    at = lax.broadcasted_iota(jnp.int32, (chunk, 16), 0)
    slot = lax.broadcasted_iota(jnp.int32, (chunk, 16), 1)
    by_group = jnp.where(at // each == slot, 1.0, 0.0).astype(BF)
    by_unit = jnp.where(lax.rem(at, each) == slot, 1.0, 0.0).astype(BF)
    at = lax.broadcasted_iota(jnp.int32, (chunk, 128), 0)
    lane = lax.broadcasted_iota(jnp.int32, (chunk, 128), 1)
    out_col = lax.broadcasted_iota(jnp.int32, (chunk, SPARE), 1)
    fb = jnp.where(lane == at // each, nn(by_unit, fb_pad[...].astype(BF)), 0.0)
    qv = jnp.where(lane == lax.rem(at, each), nn(by_group, qv_pad[...].astype(BF)), 0.0)
    for c, spread in ((6, fb), (7, qv)):
        spare += jnp.where(out_col == c, jnp.sum(spread, axis=1, keepdims=True), 0.0)
    out_ref[:, 3 * wide : 3 * wide + SPARE] = spare.astype(BF)


def prepare_fc1(fc1_ref, proj_ref, out_ref):
    width, wide = fc1_ref.shape[1], proj_ref.shape[0]
    out_ref[:, 0:width] = fc1_ref[...]
    row = lax.broadcasted_iota(jnp.int32, (wide, wide), 0)
    col = lax.broadcasted_iota(jnp.int32, (wide, wide), 1)
    one = jnp.where(row == col, 1.0, 0.0).astype(BF)
    out_ref[:, width:] = jnp.zeros_like(out_ref[:, width:])
    out_ref[:, width : width + wide] = tn(proj_ref[...], one).astype(BF)


def pad_rows(dest, source, seq):
    dest[...] = jnp.zeros_like(dest)
    dest[0:seq, :] = source[...].astype(dest.dtype)


def attention_forward(lay, seq, hd, pos, *refs):
    bufs, ins, outs, scratch = split_refs(refs, lay.n_buffers(), 2, 5)
    tok_ref, par_in = ins
    ln_ref, qkv_ref, probs_ref, att_ref, par_ref = outs
    x_ref, w_ref, sems = scratch
    use = lay.fetch(bufs, w_ref, sems, pos)
    pad_rows(x_ref, tok_ref, seq)
    rows = x_ref.shape[0]
    wide = att_ref.shape[2]
    heads = wide // hd
    normed, _ = norm_parts(x_ref[...])
    if lay.fast:
        width = lay.width
        order, _ = unit_order(width, 8)
        row = lax.broadcasted_iota(jnp.int32, (16, SPARE), 0)
        col = lax.broadcasted_iota(jnp.int32, (16, SPARE), 1)
        par = jnp.zeros((16, width), F32)
        units = jnp.zeros((16, width), F32)
        for j in range(lay.groups):
            use(j)
            spare = w_ref[j, :, 3 * wide : 3 * wide + SPARE]
            t = lay.t(j, pos)
            if j == 0:
                par = nt(jnp.where((row == col) & (row < 6), 1.0, 0.0).astype(BF), spare)
            pick = ((row == 6 + t) & (col == 6)) | ((row == 10 + t) & (col == 7))
            units += nt(jnp.where(pick, 1.0, 0.0).astype(BF), spare)
        par_ref[...] = par + nn(units.astype(BF), order)
    else:
        for j in range(lay.groups):
            use(j)
        par_ref[...] = par_in[...]
    ln = (normed * par_ref[0:1, :] + par_ref[1:2, :]).astype(BF)
    ln_ref[...] = ln
    valid = lax.broadcasted_iota(jnp.int32, (rows, rows), 1) < seq
    for j in range(lay.groups):
        bias = par_ref[pl.ds(10 + lay.t(j, pos), 1), 0 : 3 * wide]
        qkv_ref[j, :, :] = (nn(ln, w_ref[j, :, 0 : 3 * wide]) + bias).astype(BF)
        for h in range(heads):
            q = qkv_ref[j, :, h * hd : (h + 1) * hd]
            k = qkv_ref[j, :, wide + h * hd : wide + (h + 1) * hd]
            v = qkv_ref[j, :, 2 * wide + h * hd : 2 * wide + (h + 1) * hd]
            scores = jnp.where(valid, nt(q, k) * (hd**-0.5), -1e30)
            top = jnp.max(scores, axis=-1, keepdims=True)
            e = jnp.exp(scores - top)
            p = (e * (1.0 / jnp.sum(e, axis=-1, keepdims=True))).astype(BF)
            probs_ref[j * heads + h, :, :] = p
            att_ref[j, :, h * hd : (h + 1) * hd] = nn(p, v).astype(BF)


def feed_forward(lay, seq, pos, *refs):
    bufs, ins, outs, scratch = split_refs(refs, lay.n_buffers(), 3, 4)
    tok_ref, att_ref, par_ref = ins
    mid_ref, ln_ref, act_ref, slope_ref = outs[:4]
    w_ref, sems = scratch
    use = lay.fetch(bufs, w_ref, sems, pos)
    pad_rows(mid_ref, tok_ref, seq)
    width, wide = lay.width, att_ref.shape[2]
    mid = mid_ref[...] + par_ref[2:3, :]
    for j in range(lay.groups):
        use(j)
        mid += nt(att_ref[j], w_ref[j, :, width : width + wide])
    mid_ref[...] = mid
    normed, _ = norm_parts(mid)
    ln = (normed * par_ref[3:4, :] + par_ref[4:5, :]).astype(BF)
    ln_ref[...] = ln
    for j in range(lay.groups):
        bias = par_ref[pl.ds(6 + lay.t(j, pos), 1), :]
        act, slope = gelu_parts(nn(ln, w_ref[j, :, 0:width]) + bias)
        act_ref[j, :, :] = act.astype(BF)
        slope_ref[j, :, :] = slope.astype(BF)


def output_weights(lay, seq, pos, act_ref, cot_ref, *refs):
    outs, (cotp_ref, stage, out_sems) = refs[: lay.n_grads()], refs[lay.n_grads() :]
    pad_rows(cotp_ref, cot_ref, seq)
    sent = []
    for j in range(lay.groups):
        grad = tn(cotp_ref[...], act_ref[j]).astype(BF)
        sent += lay.put(grad, stage, outs, out_sems, j, pos)
    for copy in sent:
        copy.wait()


def feed_backward(lay, seq, pos, *refs):
    bufs, ins, outs, scratch = split_refs(refs, lay.n_buffers(), 3, 2 + lay.n_grads())
    slope_ref, ln_ref, cot_ref = ins
    pg_ref, small_ref = outs[:2]
    w_ref, cotp_ref, sems, stage, out_sems = scratch
    use = lay.fetch(bufs, w_ref, sems, pos)
    pad_rows(cotp_ref, cot_ref, seq)
    cot = cotp_ref[...]
    ln = ln_ref[...]
    sent = []
    small_ref[...] = jnp.zeros_like(small_ref)
    for j in range(lay.groups):
        use(j)
        pre_grad = nn(cot, w_ref[j]) * slope_ref[j].astype(F32)
        small_ref[pl.ds(6 + lay.t(j, pos), 1), :] = jnp.sum(pre_grad, axis=0, keepdims=True)
        pgb = pre_grad.astype(BF)
        pg_ref[j, :, :] = pgb
        sent += lay.put(tn(ln, pgb).astype(BF), stage, outs[2:], out_sems, j, pos)
    for copy in sent:
        copy.wait()


def mid_backward(lay, seq, pos, *refs):
    bufs, ins, outs, scratch = split_refs(refs, lay.n_buffers(), 6, 3 + lay.n_grads())
    pg_ref, mid_ref, att_ref, cot_ref, small_in, par_ref = ins
    mg_ref, ag_ref, small_ref = outs[:3]
    w_ref, cotp_ref, acc, sems, stage, out_sems = scratch
    use = lay.fetch(bufs, w_ref, sems, pos)
    pad_rows(cotp_ref, cot_ref, seq)
    width, wide = lay.width, ag_ref.shape[2]
    acc[...] = jnp.zeros_like(acc)
    for j in range(lay.groups):
        use(j)
        acc[...] += nt(pg_ref[j], w_ref[j, :, 0:width])
    normed, root = norm_parts(mid_ref[...])
    grad = acc[...]
    cot = cotp_ref[...]
    mid_grad = cot + norm_back(grad * par_ref[3:4, :], normed, root)
    mg_ref[...] = mid_grad
    small_ref[...] = small_in[...]
    small_ref[2:3, :] = jnp.sum(mid_grad, axis=0, keepdims=True)
    small_ref[3:4, :] = jnp.sum(grad * normed, axis=0, keepdims=True)
    small_ref[4:5, :] = jnp.sum(grad, axis=0, keepdims=True)
    small_ref[5:6, :] = jnp.sum(cot, axis=0, keepdims=True)
    mgb = mid_grad.astype(BF)
    pad = jnp.zeros((width, outs[3].shape[-1] - wide), F32)
    sent = []
    for j in range(lay.groups):
        proj = jnp.concatenate([tn(mgb, att_ref[j]), pad], axis=1)
        sent += lay.put(proj.astype(BF), stage, outs[3:], out_sems, j, pos)
        ag_ref[j, :, :] = nn(mgb, w_ref[j, :, width : width + wide]).astype(BF)
    for copy in sent:
        copy.wait()


def feed_output(lay, seq, pos, *refs):
    bufs, ins, (out_ref,), (w_ref, acc, sems) = split_refs(refs, lay.n_buffers(), 3, 1)
    act_ref, mid_ref, par_ref = ins
    use = lay.fetch(bufs, w_ref, sems, pos)
    acc[...] = mid_ref[...] + par_ref[5:6, :]
    for j in range(lay.groups):
        use(j)
        acc[...] += nt(act_ref[j], w_ref[j])
    out_ref[...] = acc[0:seq, :].astype(BF)


def attention_backward(lay, seq, hd, pos, *refs):
    bufs, ins, outs, scratch = split_refs(refs, lay.n_buffers(), 9, 2 + lay.n_grads())
    tok_ref, ln_ref, qkv_ref, probs_ref, att_ref, ag_ref, mg_ref, small_in, par_ref = ins
    dx_ref, small_ref = outs[:2]
    x_ref, w_ref, dqkv_ref, db_ref, ln_acc, sems, stage, out_sems = scratch
    use = lay.fetch(bufs, w_ref, sems, pos)
    wide = att_ref.shape[2]
    heads = wide // hd
    scale = hd**-0.5
    small_ref[...] = small_in[...]
    pad_rows(x_ref, tok_ref, seq)
    ln_acc[...] = jnp.zeros_like(ln_acc)
    three = slice(0, 3 * wide)
    for j in range(lay.groups):
        use(j)
        att_grad = ag_ref[j]
        prod = att_grad.astype(F32) * att_ref[j].astype(F32)
        for h in range(heads):
            at = slice(h * hd, (h + 1) * hd)
            q = qkv_ref[j, :, h * hd : (h + 1) * hd]
            k = qkv_ref[j, :, wide + h * hd : wide + (h + 1) * hd]
            v = qkv_ref[j, :, 2 * wide + h * hd : 2 * wide + (h + 1) * hd]
            p = probs_ref[j * heads + h]
            da = att_grad[:, at]
            delta = jnp.sum(prod[:, at], axis=-1, keepdims=True)
            ds = (p.astype(F32) * (nt(da, v) - delta) * scale).astype(BF)
            dqkv_ref[:, h * hd : (h + 1) * hd] = nn(ds, k)
            dqkv_ref[:, wide + h * hd : wide + (h + 1) * hd] = tn(ds, q)
            dqkv_ref[:, 2 * wide + h * hd : 2 * wide + (h + 1) * hd] = tn(p, da)
        dqkv = dqkv_ref[...]
        small_ref[pl.ds(10 + lay.t(j, pos), 1), three] = jnp.sum(dqkv, axis=0, keepdims=True)
        dqkv = dqkv.astype(BF)
        db_ref[j, :, :] = dqkv
        ln_acc[...] += nt(dqkv, w_ref[j, :, three])
    normed, root = norm_parts(x_ref[...])
    grad = ln_acc[...]
    dx = mg_ref[...] + norm_back(grad * par_ref[0:1, :], normed, root)
    dx_ref[...] = dx[0:seq, :]
    small_ref[0:1, :] = jnp.sum(grad * normed, axis=0, keepdims=True)
    small_ref[1:2, :] = jnp.sum(grad, axis=0, keepdims=True)
    width = lay.width
    spare = jnp.zeros((width, SPARE), F32)
    if lay.fast:
        small = small_ref[...].astype(BF)
        order, same = unit_order(width, 8)
        col = lax.broadcasted_iota(jnp.int32, (width, 16), 1)
        spare = jnp.where(col < 6, nt(same, small), nt(order, small))
        spare = jnp.concatenate([spare, jnp.zeros((width, SPARE - 16), F32)], axis=1)
    ln = ln_ref[...]
    sent = []
    for j in range(lay.groups):
        grad = jnp.concatenate([tn(ln, db_ref[j]), spare], axis=1).astype(BF)
        sent += lay.put(grad, stage, outs[2:], out_sems, j, pos)
    for copy in sent:
        copy.wait()


def finish_attention(chunk, pos, part_ref, *refs):
    got, (qkv_ref, vec_ref, qv_ref, fb_ref, spare_ref) = refs[:3], refs[3:]
    total = part_ref[...]
    for ref in got:
        total = total + ref[...].astype(F32)
    wide = qkv_ref.shape[2]
    for c in range(3):
        qkv_ref[c, :, :] = total[:, c * wide : (c + 1) * wide]
    spare_ref[...] = total[:, 3 * wide : 3 * wide + SPARE]
    exact = dict(precision=lax.Precision.HIGHEST, preferred_element_type=F32)
    sub, each = vec_ref.shape[1], fb_ref.shape[0]
    rows = spare_ref[pl.ds(pl.multiple_of(pos[1] * sub, sub), sub), :]
    row = lax.broadcasted_iota(jnp.int32, (8, SPARE), 0)
    col = lax.broadcasted_iota(jnp.int32, (8, SPARE), 1)
    one = jnp.where(row == col, 1.0, 0.0)
    vec = lax.dot_general(one, rows, (((1,), (1,)), ((), ())), **exact)
    vec_ref[...] = vec[0 : vec_ref.shape[0]]
    lane = lax.broadcasted_iota(jnp.int32, (chunk, SPARE), 1)
    spare = spare_ref[...]

    def column(c):
        return jnp.sum(jnp.where(lane == c + pos[1], spare, 0.0), axis=1, keepdims=True)

    def spread(shape, dim, other, by_unit):
        at = lax.broadcasted_iota(jnp.int32, shape, dim)
        at = lax.rem(at, each) if by_unit else at // each
        return at == lax.broadcasted_iota(jnp.int32, shape, other)

    left = jnp.where(spread((8, chunk), 1, 0, True), 1.0, 0.0)
    right = jnp.where(spread((chunk, 16), 0, 1, False), column(6), 0.0)
    fb_ref[...] = jnp.dot(left, right, **exact)[0:each, 0 : fb_ref.shape[1]]
    left = jnp.where(spread((16, chunk), 1, 0, False), 1.0, 0.0)
    right = jnp.where(spread((chunk, 8), 0, 1, True), column(10), 0.0)
    both = jnp.dot(left, right, **exact)
    heads = qv_ref.shape[0]
    for h in range(heads):
        qv_ref[h, 0:1, :] = both[h : h + 1, 0:each]
        qv_ref[h, 1:2, :] = both[2 * heads + h : 2 * heads + h + 1, 0:each]


def shift(x, by):
    n = lax.axis_size("tensor")
    return lax.ppermute(x, "tensor", [(i, (i + by) % n) for i in range(n)])


def flip(x, bit):
    n = lax.axis_size("dp")
    return lax.ppermute(x, "dp", [(i, i ^ bit) for i in range(n)])


def gather_columns(piece):
    return [piece] + [shift(piece, k) for k in (1, 2, 3)]


def join(a, b):
    return jnp.concatenate([a, b], axis=0)


def gather_near(h):
    return flip(h[0], AXIS_X), flip(h[1], AXIS_Y)


def gather_far(both):
    return flip(both[0], AXIS_Y), flip(both[1], AXIS_X)


def flip_cores(blocks):
    return [flip(b, CORE) for b in blocks]


def in_order(near, far, core_near, core_far):
    return [near[0], far[0], near[1], far[1], core_near[0], core_far[0], core_near[1], core_far[1]]


def add(a, b):
    return (a.astype(F32) + b.astype(F32)).astype(BF)


class Scatter:
    def __init__(self, *parts):
        self.parts = parts

    def over_cores(self, at):
        sums = [mine[at].astype(F32) + recv[at].astype(F32) for mine, recv in self.parts]
        return sums[0] if len(sums) == 1 else jnp.concatenate(sums, axis=-1)

    def first(self):
        low, high = (slice(2, 4), slice(0, 2)), (slice(1, 4, 2), slice(2, 4))
        return [self.over_cores(at).astype(BF) for at in (low, high)]

    def send_first(self, values):
        return [flip(values[0], AXIS_Y), flip(values[1], AXIS_X)]

    def second(self, got):
        low, high = (slice(0, 2), slice(0, 2)), (slice(0, 4, 2), slice(2, 4))
        return [add(self.over_cores(at), part) for at, part in zip((low, high), got)]

    def send_second(self, values):
        return [flip(values[0][1], AXIS_X), flip(values[1][1], AXIS_Y)]

    def third(self, values, got):
        low = values[0][0].astype(F32) + got[0].astype(F32)
        high = values[1][0].astype(F32) + got[1].astype(F32)
        return [low[0], low[1].astype(BF), high[0].astype(BF), high[1].astype(BF)]

    def send_third(self, parts):
        return [shift(parts[k], k) for k in (1, 2, 3)]

    def last(self, parts, got):
        total = parts[0]
        for part in got:
            total = total + part.astype(F32)
        return total


def barrier(*groups):
    flat, tree = jax.tree.flatten(groups)
    return jax.tree.unflatten(tree, lax.optimization_barrier(tuple(flat)))


def per_device(
    tokens, cotangent, qkv_weight, qv_bias, proj_weight, vectors, fc1_weight, fc1_bias, fc2_weight
):
    n_dp, groups = lax.axis_size("dp"), lax.axis_size("tensor")
    seq, width = tokens.shape
    chunk, wide = qkv_weight.shape[1], qkv_weight.shape[2]
    heads, each = qv_bias.shape[1], qv_bias.shape[2]
    hd = each * n_dp
    units = fc1_weight.shape[1]
    fast = n_dp == 8 and groups == 4
    lay = Layout(fast, groups, width)
    d, z = lax.axis_index("dp"), lax.axis_index("tensor")
    pos = jnp.stack([d, z]).astype(jnp.int32)
    three = 3 * wide
    rows = -(-seq // 16) * 16
    sds = jax.ShapeDtypeStruct
    nb = lay.n_buffers()
    sems = pltpu.SemaphoreType.DMA((groups, lay.n_blocks()))
    wide_a, wide_b = three + SPARE, -(-(width + wide) // 128) * 128

    def run_attention_forward(bufs, par):
        return kernel_call(
            functools.partial(attention_forward, lay, seq, hd),
            pos,
            bufs,
            [tokens, par],
            [
                sds((rows, width), BF),
                sds((groups, rows, three), BF),
                sds((groups * heads, rows, rows), BF),
                sds((groups, rows, wide), BF),
                sds((16, width), F32),
            ],
            [pltpu.VMEM((rows, width), F32), pltpu.VMEM((groups, width, wide_a), BF), sems],
        )

    def run_feed_forward(bufs, att, par):
        return kernel_call(
            functools.partial(feed_forward, lay, seq),
            pos,
            bufs,
            [tokens, att, par],
            [
                sds((rows, width), F32),
                sds((rows, width), BF),
                sds((groups, rows, units), BF),
                sds((groups, rows, units), BF),
            ],
            [pltpu.VMEM((groups, width, wide_b), BF), sems],
        )

    def run_output_weights(act):
        return kernel_call(
            functools.partial(output_weights, lay, seq),
            pos,
            [],
            [act, cotangent],
            lay.grad_shapes(width),
            [pltpu.VMEM((rows, width), BF), *lay.stage_shapes(width)],
            lay.n_grads(),
        )

    def run_feed_backward(bufs, slope, ln2):
        return kernel_call(
            functools.partial(feed_backward, lay, seq),
            pos,
            bufs,
            [slope, ln2, cotangent],
            [sds((groups, rows, units), BF), sds((16, width), F32), *lay.grad_shapes(width)],
            [
                pltpu.VMEM((groups, width, width), BF),
                pltpu.VMEM((rows, width), BF),
                sems,
                *lay.stage_shapes(width),
            ],
            lay.n_grads(),
        )

    def run_mid_backward(bufs, pre_grad, mid, att, small, par):
        return kernel_call(
            functools.partial(mid_backward, lay, seq),
            pos,
            bufs,
            [pre_grad, mid, att, cotangent, small, par],
            [
                sds((rows, width), F32),
                sds((groups, rows, wide), BF),
                sds((16, width), F32),
                *lay.grad_shapes(wide_b - width),
            ],
            [
                pltpu.VMEM((groups, width, wide_b), BF),
                pltpu.VMEM((rows, width), F32),
                pltpu.VMEM((rows, width), F32),
                sems,
                *lay.stage_shapes(wide_b - width),
            ],
            lay.n_grads(),
        )

    def run_feed_output(bufs, act, mid, par):
        return kernel_call(
            functools.partial(feed_output, lay, seq),
            pos,
            bufs,
            [act, mid, par],
            [sds((seq, width), BF)],
            [pltpu.VMEM((groups, width, width), BF), pltpu.VMEM((rows, width), F32), sems],
        )[0]

    def run_attention_backward(bufs, ln1, qkv, probs, att, att_grad, mid_grad, small, par):
        return kernel_call(
            functools.partial(attention_backward, lay, seq, hd),
            pos,
            bufs,
            [tokens, ln1, qkv, probs, att, att_grad, mid_grad, small, par],
            [sds((seq, width), F32), sds((16, width), F32), *lay.grad_shapes(wide_a)],
            [
                pltpu.VMEM((rows, width), F32),
                pltpu.VMEM((groups, width, wide_a), BF),
                pltpu.VMEM((rows, three), F32),
                pltpu.VMEM((groups, rows, three), BF),
                pltpu.VMEM((rows, width), F32),
                sems,
                *lay.stage_shapes(wide_a),
            ],
            lay.n_grads(),
        )

    sub = chunk // groups
    if fast:
        vmem = pl.BlockSpec(memory_space=pltpu.VMEM)
        piece_a = pl.pallas_call(
            prepare_qkv,
            out_shape=sds((chunk, wide_a), BF),
            in_specs=[vmem] * 4,
            out_specs=vmem,
            scratch_shapes=[
                pltpu.VMEM((16, chunk), F32),
                pltpu.VMEM((16, 128), F32),
                pltpu.VMEM((16, 128), F32),
            ],
        )(qkv_weight, vectors, qv_bias.transpose(1, 0, 2), fc1_bias.T)
        piece_b = pl.pallas_call(
            prepare_fc1,
            out_shape=sds((chunk, wide_b), BF),
            in_specs=[vmem] * 2,
            out_specs=vmem,
        )(fc1_weight, proj_weight)
        piece_c = fc2_weight.T
        z_a = gather_columns(piece_a)
        z_a, piece_b = barrier(z_a, piece_b)
        h_a = barrier(join(*z_a[0:2]), join(*z_a[2:4]))
        near_a = gather_near(h_a)
        z_b = [piece_b, shift(piece_b, 1)]
        near_a, z_b = barrier(near_a, z_b)
        both_a = barrier(join(h_a[0], near_a[0]), join(h_a[1], near_a[1]))
        far_a = gather_far(both_a)
        z_b = [*z_b, shift(z_b[0], 2), shift(z_b[0], 3)]
        far_a, z_b, both_a = barrier(far_a, z_b, both_a)
        h_b = join(*z_b[0:2]), join(*z_b[2:4])
        near_b = gather_near(h_b)
        bufs_a = in_order(both_a, far_a, flip_cores(both_a), flip_cores(far_a))
        ln1, qkv, probs, att, par = run_attention_forward(bufs_a, jnp.zeros((16, width), F32))

        near_b, att = barrier(near_b, att)
        both_b = barrier(join(h_b[0], near_b[0]), join(h_b[1], near_b[1]))
        far_b = gather_far(both_b)
        core_b = flip_cores(both_b)
        core_b, piece_c = barrier(core_b, piece_c)
        z_c = gather_columns(piece_c)
        far_b, z_c = barrier(far_b, z_c)
        h_c = join(*z_c[0:2]), join(*z_c[2:4])
        near_c = gather_near(h_c)
        bufs_b = in_order(both_b, far_b, core_b, flip_cores(far_b))
        mid, ln2, act, slope = run_feed_forward(bufs_b, att, par)

        near_c, mid, act = barrier(near_c, mid, act)
        both_c = barrier(join(h_c[0], near_c[0]), join(h_c[1], near_c[1]))
        both_c, act = barrier(both_c, act)
        far_c = gather_far(both_c)
        grads_c = run_output_weights(act)
        recv_c = flip(grads_c[1], CORE)
        way_c = Scatter((grads_c[0], recv_c))
        first_c = way_c.first()
        far_c, first_c, slope = barrier(far_c, first_c, slope)
        bufs_c = in_order(both_c, far_c, flip_cores(both_c), flip_cores(far_c))
        got_c = way_c.send_first(first_c)
        pre_grad, small, *grads_b = run_feed_backward(bufs_c, slope, ln2)
        got_c, grads_b, pre_grad = barrier(got_c, grads_b, pre_grad)

        recv_b = flip(grads_b[1], CORE)
        second_c = way_c.second(got_c)
        second_c, pre_grad = barrier(second_c, pre_grad)
        got_c = way_c.send_second(second_c)
        mid_grad, att_grad, small, *grads_p = run_mid_backward(
            bufs_b, pre_grad, mid, att, small, par
        )
        got_c, recv_b, grads_p, mid_grad = barrier(got_c, recv_b, grads_p, mid_grad)

        recv_p = flip(grads_p[1], CORE)
        way_b = Scatter((grads_b[0], recv_b), (grads_p[0], recv_p))
        first_b = way_b.first()
        first_b, mid_grad, got_c = barrier(first_b, mid_grad, got_c)
        got_b = way_b.send_first(first_b)
        third_c = way_c.third(second_c, got_c)
        got_c = [shift(third_c[k], k) for k in (1, 3)]
        input_grad, small, *grads_a = run_attention_backward(
            bufs_a, ln1, qkv, probs, att, att_grad, mid_grad, small, par
        )
        got_b, got_c, third_c, grads_a = barrier(got_b, got_c, third_c, grads_a)

        recv_a = flip(grads_a[1], CORE)
        second_b = way_b.second(got_b)
        second_b, third_c = barrier(second_b, third_c)
        got_b = way_b.send_second(second_b)
        got_c = [*got_c, shift(third_c[2], 2)]
        way_a = Scatter((grads_a[0], recv_a))
        first_a = way_a.first()
        first_a, got_b, got_c, act = barrier(first_a, got_b, got_c, act)
        got_a = way_a.send_first(first_a)
        third_b = way_b.third(second_b, got_b)
        third_b, act = barrier(third_b, act)
        got_b = [shift(third_b[k], k) for k in (1, 3)]
        output = run_feed_output(bufs_c, act, mid, par)
        sum_c = way_c.last(third_c, got_c)
        got_a, output, sum_c, got_b, third_b = barrier(got_a, output, sum_c, got_b, third_b)
        second_a = way_a.second(got_a)
        second_a, third_b = barrier(second_a, third_b)
        got_a = way_a.send_second(second_a)
        got_b = [*got_b, shift(third_b[2], 2)]
        got_a, got_b = barrier(got_a, got_b)
        third_a = way_a.third(second_a, got_a)
        third_a = barrier(*third_a)
        got_a = way_a.send_third(third_a)
        sum_b = way_b.last(third_b, got_b)
        sum_b, proj_grad = sum_b[:, :width], sum_b[:, width : width + wide].T
        sum_b, proj_grad, got_a = barrier(sum_b, proj_grad, got_a)
        vmem = pl.BlockSpec(memory_space=pltpu.VMEM)
        qkv_grad, vec_grad, qv_grad, fc1b_grad = pl.pallas_call(
            functools.partial(finish_attention, chunk),
            out_shape=[
                sds((3, chunk, wide), F32),
                sds((6, sub), F32),
                sds((heads, 2, each), F32),
                sds((each, units // hd), F32),
            ],
            in_specs=[pl.BlockSpec(memory_space=pltpu.SMEM)] + [vmem] * 4,
            out_specs=[vmem] * 4,
            scratch_shapes=[pltpu.VMEM((chunk, SPARE), F32)],
        )(pos, third_a[0], *got_a)
        qv_grad, fc1b_grad = qv_grad.transpose(1, 0, 2), fc1b_grad.T
    else:
        none = jnp.zeros_like(qv_bias[0])
        qkv_col = jnp.stack([qv_bias[0], none, qv_bias[1], none]).reshape(chunk)
        spare = jnp.concatenate([vectors, fc1_bias.reshape(1, chunk), qkv_col[None]], axis=0).T
        spare = jnp.pad(spare, ((0, 0), (0, SPARE - spare.shape[1])))
        piece_a = jnp.concatenate([qkv_weight[0], qkv_weight[1], qkv_weight[2], spare], axis=1)
        piece_b = jnp.concatenate([fc1_weight, proj_weight.T], axis=1)
        piece_b = jnp.pad(piece_b, ((0, 0), (0, wide_b - width - wide)))

        def gather(p):
            return [lax.all_gather(lax.all_gather(p, "dp", axis=0, tiled=True), "tensor", axis=0)]

        bufs_a, bufs_b, bufs_c = gather(piece_a), gather(piece_b), gather(fc2_weight.T)
        cols = bufs_a[0][:, :, three : three + 8]
        vec = cols[0, :, 0:6].T
        by_unit = cols.reshape(groups, n_dp, chunk // each, each, 8).transpose(0, 4, 2, 1, 3)
        by_unit = by_unit.reshape(groups, 8, width)
        par = jnp.concatenate([vec, by_unit[:, 6], by_unit[:, 7]], axis=0).astype(F32)
        par = jnp.pad(par, ((0, 16 - par.shape[0]), (0, 0)))
        ln1, qkv, probs, att, par = run_attention_forward(bufs_a, par)
        mid, ln2, act, slope = run_feed_forward(bufs_b, att, par)
        (grads_c,) = run_output_weights(act)
        pre_grad, small, grads_b = run_feed_backward(bufs_c, slope, ln2)
        mid_grad, att_grad, small, grads_p = run_mid_backward(
            bufs_b, pre_grad, mid, att, small, par
        )
        output = run_feed_output(bufs_c, act, mid, par)
        input_grad, small, grads_a = run_attention_backward(
            bufs_a, ln1, qkv, probs, att, att_grad, mid_grad, small, par
        )

        def scatter(g):
            g = lax.psum_scatter(g, "tensor", scatter_dimension=0, tiled=False)
            return lax.psum_scatter(g, "dp", scatter_dimension=0, tiled=True).astype(F32)

        sum_c, sum_b, sum_a = scatter(grads_c), scatter(grads_b), scatter(grads_a)
        sum_p = lax.optimization_barrier(scatter(grads_p))
        small = lax.psum(small, ("dp", "tensor"))
        vec_grad = lax.dynamic_slice(small, (0, d * chunk + z * sub), (6, sub))
        by_unit = small[6:14].reshape(2, groups, chunk // each, hd)
        by_unit = lax.dynamic_slice(
            by_unit, (0, z, 0, d * each), (2, 1, chunk // each, each)
        ).reshape(2, chunk)
        fc1b_grad, qv_grad = by_unit[0], by_unit[1]
        fc1b_grad = fc1b_grad.reshape(fc1_bias.shape)
        qv_grad = qv_grad.reshape(4, heads, each)[0::2]
        qkv_grad = jnp.stack([sum_a[:, c * wide : (c + 1) * wide] for c in range(3)])
        proj_grad = sum_p[:, :wide].T
    return (
        output,
        input_grad,
        qkv_grad,
        qv_grad,
        proj_grad,
        vec_grad,
        sum_b,
        fc1b_grad,
        sum_c.T,
    )


def solution(mesh):
    return jax.shard_map(
        per_device,
        mesh=mesh,
        in_specs=(
            P(("dp", "tensor"), None),
            P(("dp", "tensor"), None),
            P(None, "dp", "tensor"),
            P(None, "tensor", "dp"),
            P("tensor", "dp"),
            P(None, "dp"),
            P("dp", "tensor"),
            P("tensor", "dp"),
            P("tensor", "dp"),
        ),
        out_specs=(
            P(("dp", "tensor"), None),
            P(("dp", "tensor"), None),
            P(None, "dp", "tensor"),
            P(None, "tensor", "dp"),
            P("tensor", "dp"),
            P(None, ("dp", "tensor")),
            P("dp", "tensor"),
            P("tensor", "dp"),
            P("tensor", "dp"),
        ),
        check_vma=False,
    )
```

```python
import functools

import jax
import jax.numpy as jnp
from jax import lax
from jax.experimental import pallas as pl
from jax.experimental.pallas import tpu as pltpu
from jax.sharding import PartitionSpec as P

BF = jnp.bfloat16
F32 = jnp.float32
norm_eps = 1e-06
half_root = 0.7071067811865476
density_scale = 0.3989422804014327
VMEM_LIMIT = 56 * 1024 * 1024


def nn(a, b):
    return jnp.dot(a, b, preferred_element_type=F32)


def nt(a, b):
    return lax.dot_general(a, b, (((1,), (1,)), ((), ())), preferred_element_type=F32)


def tn(a, b):
    return lax.dot_general(a, b, (((0,), (0,)), ((), ())), preferred_element_type=F32)


def norm_parts(values):
    centred = values - jnp.mean(values, axis=-1, keepdims=True)
    recip_root = lax.rsqrt(jnp.mean(centred * centred, axis=-1, keepdims=True) + norm_eps)
    return centred * recip_root, recip_root


def norm_back(upstream, normed, recip_root):
    first_mean = jnp.mean(upstream, axis=-1, keepdims=True)
    second_mean = jnp.mean(upstream * normed, axis=-1, keepdims=True)
    return recip_root * (upstream - first_mean - normed * second_mean)


def gelu_parts(values):
    cumul = 0.5 * (1.0 + lax.erf(values * half_root))
    return (values * cumul, cumul + values * jnp.exp(-0.5 * values * values) * density_scale)


class Layout:
    def __init__(self, fast, groups, width):
        self.fast, self.groups, self.width = fast, groups, width
        self.chunk = width // 8 if fast else width

    def t(self, j, pos):
        return lax.rem(pos[1] + (self.groups - j), self.groups) if self.fast else j

    def out(self, j):
        return (self.groups - j) % self.groups if self.fast else j

    def rows(self, k, pos):
        if not self.fast:
            return pl.ds(0, self.width)
        return pl.ds(pl.multiple_of((pos[0] ^ k) * self.chunk, self.chunk), self.chunk)

    def n_buffers(self):
        return 8 if self.fast else 1

    def n_direct(self):
        return 16 if self.fast else 1

    def n_blocks(self):
        return 8 if self.fast else 1

    def sources(self, bufs, j, direct):
        if not self.fast:
            return [(bufs[0].at[j], 0)]
        found = []
        if direct:
            at = pl.ds((j % 2) * self.chunk, self.chunk)
            for core in range(2):
                for n, k in enumerate((0, AXIS_X, AXIS_Y, AXIS_X | AXIS_Y)):
                    found.append((bufs[8 * core + 4 * (j // 2) + n].at[at, :], k ^ core))
            return found
        first, second = (AXIS_X, AXIS_Y) if j < 2 else (AXIS_Y, AXIS_X)
        for core in range(2):
            near, far = bufs[4 * core + 2 * (j // 2) :][:2]
            for ref, axis in ((near, 0), (far, second)):
                for n in range(2):
                    at = pl.ds((2 * n + j % 2) * self.chunk, self.chunk)
                    found.append((ref.at[at, :], axis ^ (first * n) ^ core))
        return found

    def fetch(self, bufs, dest, sems, pos, direct=False, ahead=2):
        def begin(j):
            found = []
            for n, (src, k) in enumerate(self.sources(bufs, j, direct)):
                copy = pltpu.make_async_copy(src, dest.at[j, self.rows(k, pos), :], sems.at[j, n])
                copy.start()
                found.append(copy)
            return found

        copies = [begin(j) for j in range(min(ahead, self.groups))]

        def use(j):
            for copy in copies[j]:
                copy.wait()
            if j + ahead < self.groups:
                copies.append(begin(j + ahead))

        return use

    def put(self, grad, stage, outs, sems, j, pos):
        at = self.out(j)
        if not self.fast:
            stage[at, :, :] = grad
            copies = [pltpu.make_async_copy(stage.at[at], outs[0].at[at], sems.at[j, 0])]
        else:
            for r in range(8):
                other = pos[0] ^ r
                stage[other & 1, other >> 1, at, :, :] = grad[r * self.chunk : (r + 1) * self.chunk]
            copies = [
                pltpu.make_async_copy(stage.at[n, :, at], outs[n].at[:, at], sems.at[j, n])
                for n in range(2)
            ]
        for copy in copies:
            copy.start()
        return copies

    def stage_shapes(self, wide):
        shape = (2, 4, self.groups, self.chunk, wide) if self.fast else (self.groups, self.width, wide)
        return [pltpu.VMEM(shape, BF), pltpu.SemaphoreType.DMA((self.groups, 2))]

    def n_grads(self):
        return 2 if self.fast else 1

    def grad_shapes(self, wide):
        if not self.fast:
            return [jax.ShapeDtypeStruct((self.groups, self.width, wide), BF)]
        return [jax.ShapeDtypeStruct((4, self.groups, self.chunk, wide), BF)] * 2


SPARE = 64
CORE, AXIS_X, AXIS_Y = 1, 2, 4


def unit_order(width, n):
    i = lax.broadcasted_iota(jnp.int32, (width, width), 0)
    c = lax.broadcasted_iota(jnp.int32, (width, width), 1)
    per = width // n
    hit = i == (lax.rem(c, 64) // 8) * per + (c // 64) * 8 + lax.rem(c, 8)
    same = i == c
    return jnp.where(hit, 1.0, 0.0).astype(BF), jnp.where(same, 1.0, 0.0).astype(BF)


def kernel_call(body, pos, bufs, ins, outs, scratch, n_any=0):
    in_hbm = pl.BlockSpec(memory_space=pl.ANY)
    vmem, smem = pl.BlockSpec(memory_space=pltpu.VMEM), pl.BlockSpec(memory_space=pltpu.SMEM)
    return pl.pallas_call(
        body,
        out_shape=outs,
        in_specs=[smem] + [in_hbm] * len(bufs) + [vmem] * len(ins),
        out_specs=[vmem] * (len(outs) - n_any) + [in_hbm] * n_any,
        scratch_shapes=scratch,
        compiler_params=pltpu.CompilerParams(vmem_limit_bytes=VMEM_LIMIT),
        cost_estimate=pl.CostEstimate(flops=0, bytes_accessed=0, transcendentals=0),
    )(pos, *bufs, *ins)


def split_refs(refs, n_bufs, n_in, n_out):
    bufs, refs = refs[:n_bufs], refs[n_bufs:]
    return bufs, refs[:n_in], refs[n_in : n_in + n_out], refs[n_in + n_out :]


def prepare_qkv(qkv_ref, vec_ref, qv_ref, fb_ref, out_ref, rows_ref, fb_pad, qv_pad):
    wide, chunk = qkv_ref.shape[2], qkv_ref.shape[1]
    heads, each = qv_ref.shape[0], qv_ref.shape[2]
    for c in range(3):
        out_ref[:, c * wide : (c + 1) * wide] = qkv_ref[c]
    for ref in (rows_ref, fb_pad, qv_pad):
        ref[...] = jnp.zeros_like(ref)
    rows_ref[0 : vec_ref.shape[0], :] = vec_ref[...].astype(F32)
    fb_pad[0:each, 0 : fb_ref.shape[1]] = fb_ref[...].astype(F32)
    for h in range(heads):
        both = qv_ref[h].astype(F32)
        qv_pad[h : h + 1, 0:each] = both[0:1]
        qv_pad[2 * heads + h : 2 * heads + h + 1, 0:each] = both[1:2]
    row = lax.broadcasted_iota(jnp.int32, (16, SPARE), 0)
    col = lax.broadcasted_iota(jnp.int32, (16, SPARE), 1)
    spare = tn(rows_ref[...].astype(BF), jnp.where(row == col, 1.0, 0.0).astype(BF))
    at = lax.broadcasted_iota(jnp.int32, (chunk, 16), 0)
    slot = lax.broadcasted_iota(jnp.int32, (chunk, 16), 1)
    by_group = jnp.where(at // each == slot, 1.0, 0.0).astype(BF)
    by_unit = jnp.where(lax.rem(at, each) == slot, 1.0, 0.0).astype(BF)
    at = lax.broadcasted_iota(jnp.int32, (chunk, 128), 0)
    lane = lax.broadcasted_iota(jnp.int32, (chunk, 128), 1)
    out_col = lax.broadcasted_iota(jnp.int32, (chunk, SPARE), 1)
    fb = jnp.where(lane == at // each, nn(by_unit, fb_pad[...].astype(BF)), 0.0)
    qv = jnp.where(lane == lax.rem(at, each), nn(by_group, qv_pad[...].astype(BF)), 0.0)
    for c, spread in ((6, fb), (7, qv)):
        spare += jnp.where(out_col == c, jnp.sum(spread, axis=1, keepdims=True), 0.0)
    out_ref[:, 3 * wide : 3 * wide + SPARE] = spare.astype(BF)


def prepare_fc1(fc1_ref, proj_ref, out_ref):
    width, wide = fc1_ref.shape[1], proj_ref.shape[0]
    out_ref[:, 0:width] = fc1_ref[...]
    row = lax.broadcasted_iota(jnp.int32, (wide, wide), 0)
    col = lax.broadcasted_iota(jnp.int32, (wide, wide), 1)
    one = jnp.where(row == col, 1.0, 0.0).astype(BF)
    out_ref[:, width:] = jnp.zeros_like(out_ref[:, width:])
    out_ref[:, width : width + wide] = tn(proj_ref[...], one).astype(BF)


def pad_rows(dest, source, seq):
    dest[...] = jnp.zeros_like(dest)
    dest[0:seq, :] = source[...].astype(dest.dtype)


def attention_forward(lay, seq, hd, pos, *refs):
    bufs, ins, outs, scratch = split_refs(refs, lay.n_buffers(), 1 if lay.fast else 2, 5)
    tok_ref = ins[0]
    ln_ref, qkv_ref, probs_ref, att_ref, par_ref = outs
    x_ref, w_ref, sems = scratch
    use = lay.fetch(bufs, w_ref, sems, pos, ahead=lay.groups)
    pad_rows(x_ref, tok_ref, seq)
    rows = x_ref.shape[0]
    wide = att_ref.shape[2]
    heads = wide // hd
    normed, _ = norm_parts(x_ref[...])
    if lay.fast:
        width = lay.width
        order, _ = unit_order(width, 8)
        row = lax.broadcasted_iota(jnp.int32, (16, SPARE), 0)
        col = lax.broadcasted_iota(jnp.int32, (16, SPARE), 1)
        par = jnp.zeros((16, width), F32)
        units = jnp.zeros((16, width), F32)
        for j in range(lay.groups):
            use(j)
            spare = w_ref[j, :, 3 * wide : 3 * wide + SPARE]
            t = lay.t(j, pos)
            if j == 0:
                par = nt(jnp.where((row == col) & (row < 6), 1.0, 0.0).astype(BF), spare)
            pick = ((row == 6 + t) & (col == 6)) | ((row == 10 + t) & (col == 7))
            units += nt(jnp.where(pick, 1.0, 0.0).astype(BF), spare)
        par_ref[...] = par + nn(units.astype(BF), order)
    else:
        for j in range(lay.groups):
            use(j)
        par_ref[...] = ins[1][...]
    ln = (normed * par_ref[0:1, :] + par_ref[1:2, :]).astype(BF)
    ln_ref[...] = ln
    valid = lax.broadcasted_iota(jnp.int32, (rows, rows), 1) < seq
    for j in range(lay.groups):
        bias = par_ref[pl.ds(10 + lay.t(j, pos), 1), 0 : 3 * wide]
        qkv_ref[j, :, :] = (nn(ln, w_ref[j, :, 0 : 3 * wide]) + bias).astype(BF)
        for h in range(heads):
            q = qkv_ref[j, :, h * hd : (h + 1) * hd]
            k = qkv_ref[j, :, wide + h * hd : wide + (h + 1) * hd]
            v = qkv_ref[j, :, 2 * wide + h * hd : 2 * wide + (h + 1) * hd]
            scores = jnp.where(valid, nt(q, k) * (hd**-0.5), -1e30)
            top = jnp.max(scores, axis=-1, keepdims=True)
            e = jnp.exp(scores - top)
            p = (e * (1.0 / jnp.sum(e, axis=-1, keepdims=True))).astype(BF)
            probs_ref[j * heads + h, :, :] = p
            att_ref[j, :, h * hd : (h + 1) * hd] = nn(p, v).astype(BF)


def feed_forward(lay, seq, pos, *refs):
    bufs, ins, outs, scratch = split_refs(refs, lay.n_buffers(), 4, 4 + lay.n_grads())
    tok_ref, att_ref, cot_ref, par_ref = ins
    mid_ref, ln_ref, act_ref, slope_ref = outs[:4]
    cotp_ref, w_ref, sems, stage, out_sems = scratch
    use = lay.fetch(bufs, w_ref, sems, pos)
    pad_rows(cotp_ref, cot_ref, seq)
    pad_rows(mid_ref, tok_ref, seq)
    width, wide = lay.width, att_ref.shape[2]
    mid = mid_ref[...] + par_ref[2:3, :]
    for j in range(lay.groups):
        use(j)
        mid += nt(att_ref[j], w_ref[j, :, width : width + wide])
    mid_ref[...] = mid
    normed, _ = norm_parts(mid)
    ln = (normed * par_ref[3:4, :] + par_ref[4:5, :]).astype(BF)
    ln_ref[...] = ln
    sent = []
    for j in range(lay.groups):
        bias = par_ref[pl.ds(6 + lay.t(j, pos), 1), :]
        act, slope = gelu_parts(nn(ln, w_ref[j, :, 0:width]) + bias)
        act_ref[j, :, :] = act.astype(BF)
        slope_ref[j, :, :] = slope.astype(BF)
        grad = tn(cotp_ref[...], act_ref[j]).astype(BF)
        sent += lay.put(grad, stage, outs[4:], out_sems, j, pos)
    for copy in sent:
        copy.wait()


def feed_backward(lay, seq, pos, *refs):
    nb = lay.n_buffers()
    bufs, ins, outs, scratch = split_refs(refs, nb + lay.n_direct(), 3, 2 + lay.n_grads())
    slope_ref, ln_ref, cot_ref = ins
    lg_ref, small_ref = outs[:2]
    w2_ref, w1_ref, cotp_ref, sems2, sems1, stage, out_sems = scratch
    use2 = lay.fetch(bufs[nb:], w2_ref, sems2, pos, True)
    use1 = lay.fetch(bufs[:nb], w1_ref, sems1, pos)
    pad_rows(cotp_ref, cot_ref, seq)
    cot = cotp_ref[...]
    ln = ln_ref[...]
    small_ref[...] = jnp.zeros_like(small_ref)
    sent = []
    for j in range(lay.groups):
        use2(j)
        pre_grad = nn(cot, w2_ref[j]) * slope_ref[j].astype(F32)
        small_ref[pl.ds(6 + lay.t(j, pos), 1), :] = jnp.sum(pre_grad, axis=0, keepdims=True)
        pgb = pre_grad.astype(BF)
        sent += lay.put(tn(ln, pgb).astype(BF), stage, outs[2:], out_sems, j, pos)
        use1(j)
        part = nt(pgb, w1_ref[j, :, 0 : lay.width])
        if j == 0:
            lg_ref[...] = part
        else:
            lg_ref[...] += part
    for copy in sent:
        copy.wait()


def mid_backward(lay, seq, pos, *refs):
    bufs, ins, outs, scratch = split_refs(refs, lay.n_buffers(), 6, 3 + lay.n_grads())
    lg_ref, mid_ref, att_ref, cot_ref, small_in, par_ref = ins
    mg_ref, ag_ref, small_ref = outs[:3]
    w_ref, cotp_ref, sems, stage, out_sems = scratch
    width, wide = lay.width, ag_ref.shape[2]
    bufs = [buf.at[:, width:] if lay.fast else buf.at[:, :, width:] for buf in bufs]
    use = lay.fetch(bufs, w_ref, sems, pos)
    pad_rows(cotp_ref, cot_ref, seq)
    normed, root = norm_parts(mid_ref[...])
    grad = lg_ref[...]
    cot = cotp_ref[...]
    mid_grad = cot + norm_back(grad * par_ref[3:4, :], normed, root)
    mg_ref[...] = mid_grad
    mgb = mid_grad.astype(BF)
    pad = jnp.zeros((width, outs[3].shape[-1] - wide), F32)
    sent = []
    for j in range(lay.groups):
        proj = jnp.concatenate([tn(mgb, att_ref[j]), pad], axis=1)
        sent += lay.put(proj.astype(BF), stage, outs[3:], out_sems, j, pos)
    small_ref[...] = small_in[...]
    small_ref[2:3, :] = jnp.sum(mid_grad, axis=0, keepdims=True)
    small_ref[3:4, :] = jnp.sum(grad * normed, axis=0, keepdims=True)
    small_ref[4:5, :] = jnp.sum(grad, axis=0, keepdims=True)
    small_ref[5:6, :] = jnp.sum(cot, axis=0, keepdims=True)
    for j in range(lay.groups):
        use(j)
        ag_ref[j, :, :] = nn(mgb, w_ref[j, :, 0:wide]).astype(BF)
    for copy in sent:
        copy.wait()


def feed_output(lay, seq, pos, *refs):
    bufs, ins, (out_ref,), (w_ref, acc, sems) = split_refs(refs, lay.n_direct(), 3, 1)
    act_ref, mid_ref, par_ref = ins
    use = lay.fetch(bufs, w_ref, sems, pos, True)
    acc[...] = mid_ref[...] + par_ref[5:6, :]
    for j in range(lay.groups):
        use(j)
        acc[...] += nt(act_ref[j], w_ref[j])
    out_ref[...] = acc[0:seq, :].astype(BF)


def attention_backward(lay, seq, hd, pos, *refs):
    bufs, ins, outs, scratch = split_refs(refs, lay.n_buffers(), 9, 2 + lay.n_grads())
    tok_ref, ln_ref, qkv_ref, probs_ref, att_ref, ag_ref, mg_ref, small_in, par_ref = ins
    dx_ref, small_ref = outs[:2]
    x_ref, w_ref, dqkv_ref, db_ref, ln_acc, sems, stage, out_sems = scratch
    use = lay.fetch(bufs, w_ref, sems, pos)
    wide = att_ref.shape[2]
    heads = wide // hd
    scale = hd**-0.5
    small_ref[...] = small_in[...]
    pad_rows(x_ref, tok_ref, seq)
    ln_acc[...] = jnp.zeros_like(ln_acc)
    three = slice(0, 3 * wide)
    for j in range(lay.groups):
        use(j)
        att_grad = ag_ref[j]
        prod = att_grad.astype(F32) * att_ref[j].astype(F32)
        for h in range(heads):
            at = slice(h * hd, (h + 1) * hd)
            q = qkv_ref[j, :, h * hd : (h + 1) * hd]
            k = qkv_ref[j, :, wide + h * hd : wide + (h + 1) * hd]
            v = qkv_ref[j, :, 2 * wide + h * hd : 2 * wide + (h + 1) * hd]
            p = probs_ref[j * heads + h]
            da = att_grad[:, at]
            delta = jnp.sum(prod[:, at], axis=-1, keepdims=True)
            ds = (p.astype(F32) * (nt(da, v) - delta) * scale).astype(BF)
            dqkv_ref[:, h * hd : (h + 1) * hd] = nn(ds, k)
            dqkv_ref[:, wide + h * hd : wide + (h + 1) * hd] = tn(ds, q)
            dqkv_ref[:, 2 * wide + h * hd : 2 * wide + (h + 1) * hd] = tn(p, da)
        dqkv = dqkv_ref[...]
        small_ref[pl.ds(10 + lay.t(j, pos), 1), three] = jnp.sum(dqkv, axis=0, keepdims=True)
        dqkv = dqkv.astype(BF)
        db_ref[j, :, :] = dqkv
        ln_acc[...] += nt(dqkv, w_ref[j, :, three])
    normed, root = norm_parts(x_ref[...])
    grad = ln_acc[...]
    dx = mg_ref[...] + norm_back(grad * par_ref[0:1, :], normed, root)
    dx_ref[...] = dx[0:seq, :]
    small_ref[0:1, :] = jnp.sum(grad * normed, axis=0, keepdims=True)
    small_ref[1:2, :] = jnp.sum(grad, axis=0, keepdims=True)
    width = lay.width
    spare = jnp.zeros((width, SPARE), F32)
    if lay.fast:
        small = small_ref[...].astype(BF)
        order, same = unit_order(width, 8)
        col = lax.broadcasted_iota(jnp.int32, (width, 16), 1)
        spare = jnp.where(col < 6, nt(same, small), nt(order, small))
        spare = jnp.concatenate([spare, jnp.zeros((width, SPARE - 16), F32)], axis=1)
    ln = ln_ref[...]
    sent = []
    for j in range(lay.groups):
        grad = jnp.concatenate([tn(ln, db_ref[j]), spare], axis=1).astype(BF)
        sent += lay.put(grad, stage, outs[2:], out_sems, j, pos)
    for copy in sent:
        copy.wait()


def finish_attention(chunk, pos, part_ref, *refs):
    got, (qkv_ref, vec_ref, qv_ref, fb_ref, spare_ref) = refs[:3], refs[3:]
    total = part_ref[...]
    for ref in got:
        total = total + ref[...].astype(F32)
    wide = qkv_ref.shape[2]
    for c in range(3):
        qkv_ref[c, :, :] = total[:, c * wide : (c + 1) * wide]
    spare_ref[...] = total[:, 3 * wide : 3 * wide + SPARE]
    exact = dict(precision=lax.Precision.HIGHEST, preferred_element_type=F32)
    sub, each = vec_ref.shape[1], fb_ref.shape[0]
    rows = spare_ref[pl.ds(pl.multiple_of(pos[1] * sub, sub), sub), :]
    row = lax.broadcasted_iota(jnp.int32, (8, SPARE), 0)
    col = lax.broadcasted_iota(jnp.int32, (8, SPARE), 1)
    one = jnp.where(row == col, 1.0, 0.0)
    vec = lax.dot_general(one, rows, (((1,), (1,)), ((), ())), **exact)
    vec_ref[...] = vec[0 : vec_ref.shape[0]]
    lane = lax.broadcasted_iota(jnp.int32, (chunk, SPARE), 1)
    spare = spare_ref[...]

    def column(c):
        return jnp.sum(jnp.where(lane == c + pos[1], spare, 0.0), axis=1, keepdims=True)

    def spread(shape, dim, other, by_unit):
        at = lax.broadcasted_iota(jnp.int32, shape, dim)
        at = lax.rem(at, each) if by_unit else at // each
        return at == lax.broadcasted_iota(jnp.int32, shape, other)

    left = jnp.where(spread((8, chunk), 1, 0, True), 1.0, 0.0)
    right = jnp.where(spread((chunk, 16), 0, 1, False), column(6), 0.0)
    fb_ref[...] = jnp.dot(left, right, **exact)[0:each, 0 : fb_ref.shape[1]]
    left = jnp.where(spread((16, chunk), 1, 0, False), 1.0, 0.0)
    right = jnp.where(spread((chunk, 8), 0, 1, True), column(10), 0.0)
    both = jnp.dot(left, right, **exact)
    heads = qv_ref.shape[0]
    for h in range(heads):
        qv_ref[h, 0:1, :] = both[h : h + 1, 0:each]
        qv_ref[h, 1:2, :] = both[2 * heads + h : 2 * heads + h + 1, 0:each]


def shift(x, by):
    n = lax.axis_size("tensor")
    return lax.ppermute(x, "tensor", [(i, (i + by) % n) for i in range(n)])


def flip(x, bit):
    n = lax.axis_size("dp")
    return lax.ppermute(x, "dp", [(i, i ^ bit) for i in range(n)])


def gather_columns(piece):
    return [piece] + [shift(piece, k) for k in (1, 2, 3)]


def join(a, b):
    return jnp.concatenate([a, b], axis=0)


def gather_near(h):
    return flip(h[0], AXIS_X), flip(h[1], AXIS_Y)


def gather_far(both):
    return flip(both[0], AXIS_Y), flip(both[1], AXIS_X)


def direct_near(h):
    return [flip(h[0], AXIS_X), flip(h[0], AXIS_Y), flip(h[1], AXIS_X), flip(h[1], AXIS_Y)]


def direct_far(near):
    return [flip(near[0], AXIS_Y), flip(near[3], AXIS_X)]


def in_direct_order(h, near, far):
    return [h[0], near[0], near[1], far[0], h[1], near[2], near[3], far[1]]


def flip_cores(blocks):
    return [flip(b, CORE) for b in blocks]


def in_order(near, far, core_near, core_far):
    return [near[0], far[0], near[1], far[1], core_near[0], core_far[0], core_near[1], core_far[1]]


def add(a, b):
    return (a.astype(F32) + b.astype(F32)).astype(BF)


class Scatter:
    def __init__(self, *parts):
        self.parts = parts

    def over_cores(self, at):
        sums = [mine[at].astype(F32) + recv[at].astype(F32) for mine, recv in self.parts]
        return sums[0] if len(sums) == 1 else jnp.concatenate(sums, axis=-1)

    def first(self):
        low, high = (slice(2, 4), slice(0, 2)), (slice(1, 4, 2), slice(2, 4))
        return [self.over_cores(at).astype(BF) for at in (low, high)]

    def send_first(self, values):
        return [flip(values[0], AXIS_Y), flip(values[1], AXIS_X)]

    def second(self, got):
        low, high = (slice(0, 2), slice(0, 2)), (slice(0, 4, 2), slice(2, 4))
        return [add(self.over_cores(at), part) for at, part in zip((low, high), got)]

    def send_second(self, values):
        return [flip(values[0][1], AXIS_X), flip(values[1][1], AXIS_Y)]

    def third(self, values, got):
        low = values[0][0].astype(F32) + got[0].astype(F32)
        high = values[1][0].astype(F32) + got[1].astype(F32)
        return [low[0], low[1].astype(BF), high[0].astype(BF), high[1].astype(BF)]

    def send_third(self, parts):
        return [shift(parts[k], k) for k in (1, 2, 3)]

    def last(self, parts, got):
        total = parts[0]
        for part in got:
            total = total + part.astype(F32)
        return total


def barrier(*groups):
    flat, tree = jax.tree.flatten(groups)
    return jax.tree.unflatten(tree, lax.optimization_barrier(tuple(flat)))


def per_device(
    tokens, cotangent, qkv_weight, qv_bias, proj_weight, vectors, fc1_weight, fc1_bias, fc2_weight
):
    n_dp, groups = lax.axis_size("dp"), lax.axis_size("tensor")
    seq, width = tokens.shape
    chunk, wide = qkv_weight.shape[1], qkv_weight.shape[2]
    heads, each = qv_bias.shape[1], qv_bias.shape[2]
    hd = each * n_dp
    units = fc1_weight.shape[1]
    fast = n_dp == 8 and groups == 4
    lay = Layout(fast, groups, width)
    d, z = lax.axis_index("dp"), lax.axis_index("tensor")
    pos = jnp.stack([d, z]).astype(jnp.int32)
    three = 3 * wide
    rows = -(-seq // 16) * 16
    sds = jax.ShapeDtypeStruct
    nb = lay.n_buffers()
    sems = pltpu.SemaphoreType.DMA((groups, lay.n_blocks()))
    wide_a, wide_b = three + SPARE, -(-(width + wide) // 128) * 128

    def run_attention_forward(bufs, *par):
        return kernel_call(
            functools.partial(attention_forward, lay, seq, hd),
            pos,
            bufs,
            [tokens, *par],
            [
                sds((rows, width), BF),
                sds((groups, rows, three), BF),
                sds((groups * heads, rows, rows), BF),
                sds((groups, rows, wide), BF),
                sds((16, width), F32),
            ],
            [pltpu.VMEM((rows, width), F32), pltpu.VMEM((groups, width, wide_a), BF), sems],
        )

    def run_feed_forward(bufs, att, par):
        return kernel_call(
            functools.partial(feed_forward, lay, seq),
            pos,
            bufs,
            [tokens, att, cotangent, par],
            [
                sds((rows, width), F32),
                sds((rows, width), BF),
                sds((groups, rows, units), BF),
                sds((groups, rows, units), BF),
                *lay.grad_shapes(width),
            ],
            [
                pltpu.VMEM((rows, width), BF),
                pltpu.VMEM((groups, width, wide_b), BF),
                sems,
                *lay.stage_shapes(width),
            ],
            lay.n_grads(),
        )

    def run_feed_backward(bufs, slope, ln2):
        return kernel_call(
            functools.partial(feed_backward, lay, seq),
            pos,
            bufs,
            [slope, ln2, cotangent],
            [sds((rows, width), F32), sds((16, width), F32), *lay.grad_shapes(width)],
            [
                pltpu.VMEM((groups, width, width), BF),
                pltpu.VMEM((groups, width, wide_b), BF),
                pltpu.VMEM((rows, width), BF),
                sems,
                sems,
                *lay.stage_shapes(width),
            ],
            lay.n_grads(),
        )

    def run_mid_backward(bufs, ln2_grad, mid, att, small, par):
        return kernel_call(
            functools.partial(mid_backward, lay, seq),
            pos,
            bufs,
            [ln2_grad, mid, att, cotangent, small, par],
            [
                sds((rows, width), F32),
                sds((groups, rows, wide), BF),
                sds((16, width), F32),
                *lay.grad_shapes(wide_b - width),
            ],
            [
                pltpu.VMEM((groups, width, wide_b - width), BF),
                pltpu.VMEM((rows, width), F32),
                sems,
                *lay.stage_shapes(wide_b - width),
            ],
            lay.n_grads(),
        )

    def run_feed_output(bufs, act, mid, par):
        return kernel_call(
            functools.partial(feed_output, lay, seq),
            pos,
            bufs,
            [act, mid, par],
            [sds((seq, width), BF)],
            [pltpu.VMEM((groups, width, width), BF), pltpu.VMEM((rows, width), F32), sems],
        )[0]

    def run_attention_backward(bufs, ln1, qkv, probs, att, att_grad, mid_grad, small, par):
        return kernel_call(
            functools.partial(attention_backward, lay, seq, hd),
            pos,
            bufs,
            [tokens, ln1, qkv, probs, att, att_grad, mid_grad, small, par],
            [sds((seq, width), F32), sds((16, width), F32), *lay.grad_shapes(wide_a)],
            [
                pltpu.VMEM((rows, width), F32),
                pltpu.VMEM((groups, width, wide_a), BF),
                pltpu.VMEM((rows, three), F32),
                pltpu.VMEM((groups, rows, three), BF),
                pltpu.VMEM((rows, width), F32),
                sems,
                *lay.stage_shapes(wide_a),
            ],
            lay.n_grads(),
        )

    sub = chunk // groups
    if fast:
        vmem = pl.BlockSpec(memory_space=pltpu.VMEM)
        piece_a = pl.pallas_call(
            prepare_qkv,
            out_shape=sds((chunk, wide_a), BF),
            in_specs=[vmem] * 4,
            out_specs=vmem,
            scratch_shapes=[
                pltpu.VMEM((16, chunk), F32),
                pltpu.VMEM((16, 128), F32),
                pltpu.VMEM((16, 128), F32),
            ],
        )(qkv_weight, vectors, qv_bias.transpose(1, 0, 2), fc1_bias.T)
        piece_b = pl.pallas_call(
            prepare_fc1,
            out_shape=sds((chunk, wide_b), BF),
            in_specs=[vmem] * 2,
            out_specs=vmem,
        )(fc1_weight, proj_weight)
        piece_c = fc2_weight.T
        z_a = gather_columns(piece_a)
        z_a, piece_b, pos = barrier(z_a, piece_b, pos)
        h_a = barrier(join(*z_a[0:2]), join(*z_a[2:4]))
        near_a = gather_near(h_a)
        z_b = [piece_b, shift(piece_b, 1)]
        near_a, z_b = barrier(near_a, z_b)
        both_a = barrier(join(h_a[0], near_a[0]), join(h_a[1], near_a[1]))
        far_a = gather_far(both_a)
        z_b = [*z_b, shift(z_b[0], 2), shift(z_b[0], 3)]
        h_b = join(*z_b[0:2])
        far_a, z_b, both_a, h_b = barrier(far_a, z_b, both_a, h_b)
        h_b = h_b, join(*z_b[2:4])
        near_b = gather_near(h_b)
        bufs_a = in_order(both_a, far_a, flip_cores(both_a), flip_cores(far_a))
        ln1, qkv, probs, att, par = run_attention_forward(bufs_a)

        near_b, att = barrier(near_b, att)
        both_b = barrier(join(h_b[0], near_b[0]), join(h_b[1], near_b[1]))
        far_b = gather_far(both_b)
        core_b = flip_cores(both_b)
        core_b, piece_c = barrier(core_b, piece_c)
        z_c = gather_columns(piece_c)
        far_b, z_c = barrier(far_b, z_c)
        core_b = core_b + flip_cores(far_b)
        h_c = join(*z_c[0:2]), join(*z_c[2:4])
        near_c = direct_near(h_c)
        bufs_b = in_order(both_b, far_b, core_b[0:2], core_b[2:4])
        mid, ln2, act, slope, *grads_c = run_feed_forward(bufs_b, att, par)
        near_c, grads_c, slope = barrier(near_c, grads_c, slope)
        far_c = direct_far(near_c)
        recv_c, near_c, h_c = barrier(flip(grads_c[1], CORE), near_c, h_c)
        core_c = flip_cores([*h_c, *near_c])
        way_c = Scatter((grads_c[0], recv_c))
        first_c = way_c.first()
        first_c, far_c, core_c, slope = barrier(first_c, far_c, core_c, slope)
        bufs_c = [
            *in_direct_order(h_c, near_c, far_c),
            *in_direct_order(core_c[0:2], core_c[2:6], flip_cores(far_c)),
        ]
        got_c = way_c.send_first(first_c)
        ln2_grad, small, *grads_b = run_feed_backward([*bufs_b, *bufs_c], slope, ln2)
        got_c, grads_b, ln2_grad = barrier(got_c, grads_b, ln2_grad)

        recv_b = flip(grads_b[1], CORE)
        second_c = way_c.second(got_c)
        second_c, ln2_grad = barrier(second_c, ln2_grad)
        got_c = way_c.send_second(second_c)
        mid_grad, att_grad, small, *grads_p = run_mid_backward(
            bufs_b, ln2_grad, mid, att, small, par
        )
        got_c, recv_b, grads_p, mid_grad = barrier(got_c, recv_b, grads_p, mid_grad)

        recv_p = flip(grads_p[1], CORE)
        way_b = Scatter((grads_b[0], recv_b), (grads_p[0], recv_p))
        first_b = way_b.first()
        first_b, mid_grad, got_c = barrier(first_b, mid_grad, got_c)
        got_b = way_b.send_first(first_b)
        third_c = way_c.third(second_c, got_c)
        got_c = [shift(third_c[k], k) for k in (1, 3)]
        input_grad, small, *grads_a = run_attention_backward(
            bufs_a, ln1, qkv, probs, att, att_grad, mid_grad, small, par
        )
        got_b, got_c, third_c, grads_a = barrier(got_b, got_c, third_c, grads_a)

        recv_a = flip(grads_a[1], CORE)
        second_b = way_b.second(got_b)
        second_b, third_c = barrier(second_b, third_c)
        got_b = way_b.send_second(second_b)
        got_c = [*got_c, shift(third_c[2], 2)]
        way_a = Scatter((grads_a[0], recv_a))
        first_a = way_a.first()
        first_a, got_b, got_c, act = barrier(first_a, got_b, got_c, act)
        got_a = way_a.send_first(first_a)
        third_b = way_b.third(second_b, got_b)
        third_b, act = barrier(third_b, act)
        half_b = wide_b // 2
        got_b = [shift(third_b[k], k) for k in (1, 3)] + [shift(third_b[2][:, :half_b], 2)]
        output = run_feed_output(bufs_c, act, mid, par)
        sum_c = way_c.last(third_c, got_c)
        got_a, output, sum_c, got_b, third_b = barrier(got_a, output, sum_c, got_b, third_b)
        second_a = way_a.second(got_a)
        second_a, third_b = barrier(second_a, third_b)
        got_a = way_a.send_second(second_a)
        rest_b = shift(third_b[2][:, half_b:], 2)
        got_b = [*got_b[0:2], jnp.concatenate([got_b[2], rest_b], axis=1)]
        got_a, got_b = barrier(got_a, got_b)
        third_a = way_a.third(second_a, got_a)
        third_a = barrier(*third_a)
        got_a = way_a.send_third(third_a)
        sum_b = way_b.last(third_b, got_b)
        sum_b, proj_grad = sum_b[:, :width], sum_b[:, width : width + wide].T
        sum_b, proj_grad, got_a = barrier(sum_b, proj_grad, got_a)
        vmem = pl.BlockSpec(memory_space=pltpu.VMEM)
        qkv_grad, vec_grad, qv_grad, fc1b_grad = pl.pallas_call(
            functools.partial(finish_attention, chunk),
            out_shape=[
                sds((3, chunk, wide), F32),
                sds((6, sub), F32),
                sds((heads, 2, each), F32),
                sds((each, units // hd), F32),
            ],
            in_specs=[pl.BlockSpec(memory_space=pltpu.SMEM)] + [vmem] * 4,
            out_specs=[vmem] * 4,
            scratch_shapes=[pltpu.VMEM((chunk, SPARE), F32)],
        )(pos, third_a[0], *got_a)
        qv_grad, fc1b_grad = qv_grad.transpose(1, 0, 2), fc1b_grad.T
    else:
        none = jnp.zeros_like(qv_bias[0])
        qkv_col = jnp.stack([qv_bias[0], none, qv_bias[1], none]).reshape(chunk)
        spare = jnp.concatenate([vectors, fc1_bias.reshape(1, chunk), qkv_col[None]], axis=0).T
        spare = jnp.pad(spare, ((0, 0), (0, SPARE - spare.shape[1])))
        piece_a = jnp.concatenate([qkv_weight[0], qkv_weight[1], qkv_weight[2], spare], axis=1)
        piece_b = jnp.concatenate([fc1_weight, proj_weight.T], axis=1)
        piece_b = jnp.pad(piece_b, ((0, 0), (0, wide_b - width - wide)))

        def gather(p):
            return [lax.all_gather(lax.all_gather(p, "dp", axis=0, tiled=True), "tensor", axis=0)]

        bufs_a, bufs_b, bufs_c = gather(piece_a), gather(piece_b), gather(fc2_weight.T)
        cols = bufs_a[0][:, :, three : three + 8]
        vec = cols[0, :, 0:6].T
        by_unit = cols.reshape(groups, n_dp, chunk // each, each, 8).transpose(0, 4, 2, 1, 3)
        by_unit = by_unit.reshape(groups, 8, width)
        par = jnp.concatenate([vec, by_unit[:, 6], by_unit[:, 7]], axis=0).astype(F32)
        par = jnp.pad(par, ((0, 16 - par.shape[0]), (0, 0)))
        ln1, qkv, probs, att, par = run_attention_forward(bufs_a, par)
        mid, ln2, act, slope, grads_c = run_feed_forward(bufs_b, att, par)
        ln2_grad, small, grads_b = run_feed_backward([*bufs_b, *bufs_c], slope, ln2)
        mid_grad, att_grad, small, grads_p = run_mid_backward(
            bufs_b, ln2_grad, mid, att, small, par
        )
        output = run_feed_output(bufs_c, act, mid, par)
        input_grad, small, grads_a = run_attention_backward(
            bufs_a, ln1, qkv, probs, att, att_grad, mid_grad, small, par
        )

        def scatter(g):
            g = lax.psum_scatter(g, "tensor", scatter_dimension=0, tiled=False)
            return lax.psum_scatter(g, "dp", scatter_dimension=0, tiled=True).astype(F32)

        sum_c, sum_b, sum_a = scatter(grads_c), scatter(grads_b), scatter(grads_a)
        sum_p = lax.optimization_barrier(scatter(grads_p))
        small = lax.psum(small, ("dp", "tensor"))
        vec_grad = lax.dynamic_slice(small, (0, d * chunk + z * sub), (6, sub))
        by_unit = small[6:14].reshape(2, groups, chunk // each, hd)
        by_unit = lax.dynamic_slice(
            by_unit, (0, z, 0, d * each), (2, 1, chunk // each, each)
        ).reshape(2, chunk)
        fc1b_grad, qv_grad = by_unit[0], by_unit[1]
        fc1b_grad = fc1b_grad.reshape(fc1_bias.shape)
        qv_grad = qv_grad.reshape(4, heads, each)[0::2]
        qkv_grad = jnp.stack([sum_a[:, c * wide : (c + 1) * wide] for c in range(3)])
        proj_grad = sum_p[:, :wide].T
    return (
        output,
        input_grad,
        qkv_grad,
        qv_grad,
        proj_grad,
        vec_grad,
        sum_b,
        fc1b_grad,
        sum_c.T,
    )


def solution(mesh):
    return jax.shard_map(
        per_device,
        mesh=mesh,
        in_specs=(
            P(("dp", "tensor"), None),
            P(("dp", "tensor"), None),
            P(None, "dp", "tensor"),
            P(None, "tensor", "dp"),
            P("tensor", "dp"),
            P(None, "dp"),
            P("dp", "tensor"),
            P("tensor", "dp"),
            P("tensor", "dp"),
        ),
        out_specs=(
            P(("dp", "tensor"), None),
            P(("dp", "tensor"), None),
            P(None, "dp", "tensor"),
            P(None, "tensor", "dp"),
            P("tensor", "dp"),
            P(None, ("dp", "tensor")),
            P("dp", "tensor"),
            P("tensor", "dp"),
            P("tensor", "dp"),
        ),
        check_vma=False,
    )
```

```python
import functools

import jax
import jax.numpy as jnp
from jax import lax
from jax.experimental import pallas as pl
from jax.experimental.pallas import tpu as pltpu
from jax.sharding import PartitionSpec as P

BF = jnp.bfloat16
F32 = jnp.float32
norm_eps = 1e-06
half_root = 0.7071067811865476
density_scale = 0.3989422804014327
VMEM_LIMIT = 56 * 1024 * 1024


def nn(a, b):
    return jnp.dot(a, b, preferred_element_type=F32)


def nt(a, b):
    return lax.dot_general(a, b, (((1,), (1,)), ((), ())), preferred_element_type=F32)


def tn(a, b):
    return lax.dot_general(a, b, (((0,), (0,)), ((), ())), preferred_element_type=F32)


def norm_parts(values):
    centred = values - jnp.mean(values, axis=-1, keepdims=True)
    recip_root = lax.rsqrt(jnp.mean(centred * centred, axis=-1, keepdims=True) + norm_eps)
    return centred * recip_root, recip_root


def norm_back(upstream, normed, recip_root):
    first_mean = jnp.mean(upstream, axis=-1, keepdims=True)
    second_mean = jnp.mean(upstream * normed, axis=-1, keepdims=True)
    return recip_root * (upstream - first_mean - normed * second_mean)


def gelu_parts(values):
    cumul = 0.5 * (1.0 + lax.erf(values * half_root))
    return (values * cumul, cumul + values * jnp.exp(-0.5 * values * values) * density_scale)


class Layout:
    def __init__(self, fast, groups, width):
        self.fast, self.groups, self.width = fast, groups, width
        self.chunk = width // 8 if fast else width

    def t(self, j, pos):
        return lax.rem(pos[1] + (self.groups - j), self.groups) if self.fast else j

    def out(self, j):
        return (self.groups - j) % self.groups if self.fast else j

    def rows(self, k, pos):
        if not self.fast:
            return pl.ds(0, self.width)
        return pl.ds(pl.multiple_of((pos[0] ^ k) * self.chunk, self.chunk), self.chunk)

    def n_buffers(self):
        return 8 if self.fast else 1

    def n_direct(self):
        return 16 if self.fast else 1

    def n_blocks(self):
        return 8 if self.fast else 1

    def sources(self, bufs, j, direct):
        if not self.fast:
            return [(bufs[0].at[j], 0)]
        found = []
        if direct:
            at = pl.ds((j % 2) * self.chunk, self.chunk)
            for core in range(2):
                for n, k in enumerate((0, AXIS_X, AXIS_Y, AXIS_X | AXIS_Y)):
                    found.append((bufs[8 * core + 4 * (j // 2) + n].at[at, :], k ^ core))
            return found
        first, second = (AXIS_X, AXIS_Y) if j < 2 else (AXIS_Y, AXIS_X)
        for core in range(2):
            near, far = bufs[4 * core + 2 * (j // 2) :][:2]
            for ref, axis in ((near, 0), (far, second)):
                for n in range(2):
                    at = pl.ds((2 * n + j % 2) * self.chunk, self.chunk)
                    found.append((ref.at[at, :], axis ^ (first * n) ^ core))
        return found

    def fetch(self, bufs, dest, sems, pos, direct=False, ahead=2):
        def begin(j):
            found = []
            for n, (src, k) in enumerate(self.sources(bufs, j, direct)):
                copy = pltpu.make_async_copy(src, dest.at[j, self.rows(k, pos), :], sems.at[j, n])
                copy.start()
                found.append(copy)
            return found

        copies = [begin(j) for j in range(min(ahead, self.groups))]

        def use(j):
            for copy in copies[j]:
                copy.wait()
            if j + ahead < self.groups:
                copies.append(begin(j + ahead))

        return use

    def put(self, grad, stage, outs, sems, j, pos):
        at = self.out(j)
        if not self.fast:
            stage[at, :, :] = grad
            copies = [pltpu.make_async_copy(stage.at[at], outs[0].at[at], sems.at[j, 0])]
        else:
            for r in range(8):
                other = pos[0] ^ r
                stage[other & 1, other >> 1, at, :, :] = grad[r * self.chunk : (r + 1) * self.chunk]
            copies = [
                pltpu.make_async_copy(stage.at[n, :, at], outs[n].at[:, at], sems.at[j, n])
                for n in range(2)
            ]
        for copy in copies:
            copy.start()
        return copies

    def stage_shapes(self, wide):
        shape = (2, 4, self.groups, self.chunk, wide) if self.fast else (self.groups, self.width, wide)
        return [pltpu.VMEM(shape, BF), pltpu.SemaphoreType.DMA((self.groups, 2))]

    def n_grads(self):
        return 2 if self.fast else 1

    def grad_shapes(self, wide):
        if not self.fast:
            return [jax.ShapeDtypeStruct((self.groups, self.width, wide), BF)]
        return [jax.ShapeDtypeStruct((4, self.groups, self.chunk, wide), BF)] * 2


SPARE = 64
CORE, AXIS_X, AXIS_Y = 1, 2, 4


def unit_order(width, n):
    i = lax.broadcasted_iota(jnp.int32, (width, width), 0)
    c = lax.broadcasted_iota(jnp.int32, (width, width), 1)
    per = width // n
    hit = i == (lax.rem(c, 64) // 8) * per + (c // 64) * 8 + lax.rem(c, 8)
    same = i == c
    return jnp.where(hit, 1.0, 0.0).astype(BF), jnp.where(same, 1.0, 0.0).astype(BF)


def kernel_call(body, pos, bufs, ins, outs, scratch, n_any=0):
    in_hbm = pl.BlockSpec(memory_space=pl.ANY)
    vmem, smem = pl.BlockSpec(memory_space=pltpu.VMEM), pl.BlockSpec(memory_space=pltpu.SMEM)
    return pl.pallas_call(
        body,
        out_shape=outs,
        in_specs=[smem] + [in_hbm] * len(bufs) + [vmem] * len(ins),
        out_specs=[vmem] * (len(outs) - n_any) + [in_hbm] * n_any,
        scratch_shapes=scratch,
        compiler_params=pltpu.CompilerParams(vmem_limit_bytes=VMEM_LIMIT),
        cost_estimate=pl.CostEstimate(flops=0, bytes_accessed=0, transcendentals=0),
    )(pos, *bufs, *ins)


def split_refs(refs, n_bufs, n_in, n_out):
    bufs, refs = refs[:n_bufs], refs[n_bufs:]
    return bufs, refs[:n_in], refs[n_in : n_in + n_out], refs[n_in + n_out :]


def prepare_qkv(qkv_ref, vec_ref, qv_ref, fb_ref, out_ref, rows_ref, fb_pad, qv_pad):
    wide, chunk = qkv_ref.shape[2], qkv_ref.shape[1]
    heads, each = qv_ref.shape[0], qv_ref.shape[2]
    for c in range(3):
        out_ref[:, c * wide : (c + 1) * wide] = qkv_ref[c]
    for ref in (rows_ref, fb_pad, qv_pad):
        ref[...] = jnp.zeros_like(ref)
    rows_ref[0 : vec_ref.shape[0], :] = vec_ref[...].astype(F32)
    fb_pad[0:each, 0 : fb_ref.shape[1]] = fb_ref[...].astype(F32)
    for h in range(heads):
        both = qv_ref[h].astype(F32)
        qv_pad[h : h + 1, 0:each] = both[0:1]
        qv_pad[2 * heads + h : 2 * heads + h + 1, 0:each] = both[1:2]
    row = lax.broadcasted_iota(jnp.int32, (16, SPARE), 0)
    col = lax.broadcasted_iota(jnp.int32, (16, SPARE), 1)
    spare = tn(rows_ref[...].astype(BF), jnp.where(row == col, 1.0, 0.0).astype(BF))
    at = lax.broadcasted_iota(jnp.int32, (chunk, 16), 0)
    slot = lax.broadcasted_iota(jnp.int32, (chunk, 16), 1)
    by_group = jnp.where(at // each == slot, 1.0, 0.0).astype(BF)
    by_unit = jnp.where(lax.rem(at, each) == slot, 1.0, 0.0).astype(BF)
    at = lax.broadcasted_iota(jnp.int32, (chunk, 128), 0)
    lane = lax.broadcasted_iota(jnp.int32, (chunk, 128), 1)
    out_col = lax.broadcasted_iota(jnp.int32, (chunk, SPARE), 1)
    fb = jnp.where(lane == at // each, nn(by_unit, fb_pad[...].astype(BF)), 0.0)
    qv = jnp.where(lane == lax.rem(at, each), nn(by_group, qv_pad[...].astype(BF)), 0.0)
    for c, spread in ((6, fb), (7, qv)):
        spare += jnp.where(out_col == c, jnp.sum(spread, axis=1, keepdims=True), 0.0)
    out_ref[:, 3 * wide : 3 * wide + SPARE] = spare.astype(BF)


def prepare_fc1(fc1_ref, proj_ref, out_ref):
    width, wide = fc1_ref.shape[1], proj_ref.shape[0]
    out_ref[:, 0:width] = fc1_ref[...]
    row = lax.broadcasted_iota(jnp.int32, (wide, wide), 0)
    col = lax.broadcasted_iota(jnp.int32, (wide, wide), 1)
    one = jnp.where(row == col, 1.0, 0.0).astype(BF)
    out_ref[:, width:] = jnp.zeros_like(out_ref[:, width:])
    out_ref[:, width : width + wide] = tn(proj_ref[...], one).astype(BF)


def pad_rows(dest, source, seq):
    dest[...] = jnp.zeros_like(dest)
    dest[0:seq, :] = source[...].astype(dest.dtype)


def attention_forward(lay, seq, hd, pos, *refs):
    bufs, ins, outs, scratch = split_refs(refs, lay.n_buffers(), 1 if lay.fast else 2, 5)
    tok_ref = ins[0]
    ln_ref, qkv_ref, probs_ref, att_ref, par_ref = outs
    x_ref, w_ref, sems = scratch
    use = lay.fetch(bufs, w_ref, sems, pos, ahead=lay.groups)
    pad_rows(x_ref, tok_ref, seq)
    rows = x_ref.shape[0]
    wide = att_ref.shape[2]
    heads = wide // hd
    normed, _ = norm_parts(x_ref[...])
    if lay.fast:
        width = lay.width
        order, _ = unit_order(width, 8)
        row = lax.broadcasted_iota(jnp.int32, (16, SPARE), 0)
        col = lax.broadcasted_iota(jnp.int32, (16, SPARE), 1)
        par = jnp.zeros((16, width), F32)
        units = jnp.zeros((16, width), F32)
        for j in range(lay.groups):
            use(j)
            spare = w_ref[j, :, 3 * wide : 3 * wide + SPARE]
            t = lay.t(j, pos)
            if j == 0:
                par = nt(jnp.where((row == col) & (row < 6), 1.0, 0.0).astype(BF), spare)
            pick = ((row == 6 + t) & (col == 6)) | ((row == 10 + t) & (col == 7))
            units += nt(jnp.where(pick, 1.0, 0.0).astype(BF), spare)
        par_ref[...] = par + nn(units.astype(BF), order)
    else:
        for j in range(lay.groups):
            use(j)
        par_ref[...] = ins[1][...]
    ln = (normed * par_ref[0:1, :] + par_ref[1:2, :]).astype(BF)
    ln_ref[...] = ln
    valid = lax.broadcasted_iota(jnp.int32, (rows, rows), 1) < seq
    for j in range(lay.groups):
        bias = par_ref[pl.ds(10 + lay.t(j, pos), 1), 0 : 3 * wide]
        qkv_ref[j, :, :] = (nn(ln, w_ref[j, :, 0 : 3 * wide]) + bias).astype(BF)
        for h in range(heads):
            q = qkv_ref[j, :, h * hd : (h + 1) * hd]
            k = qkv_ref[j, :, wide + h * hd : wide + (h + 1) * hd]
            v = qkv_ref[j, :, 2 * wide + h * hd : 2 * wide + (h + 1) * hd]
            scores = jnp.where(valid, nt(q, k) * (hd**-0.5), -1e30)
            top = jnp.max(scores, axis=-1, keepdims=True)
            e = jnp.exp(scores - top)
            p = (e * (1.0 / jnp.sum(e, axis=-1, keepdims=True))).astype(BF)
            probs_ref[j * heads + h, :, :] = p
            att_ref[j, :, h * hd : (h + 1) * hd] = nn(p, v).astype(BF)


def feed_forward(lay, seq, pos, *refs):
    bufs, ins, outs, scratch = split_refs(refs, lay.n_buffers(), 4, 4 + lay.n_grads())
    tok_ref, att_ref, cot_ref, par_ref = ins
    mid_ref, ln_ref, act_ref, slope_ref = outs[:4]
    cotp_ref, w_ref, sems, stage, out_sems = scratch
    use = lay.fetch(bufs, w_ref, sems, pos, ahead=lay.groups)
    pad_rows(cotp_ref, cot_ref, seq)
    pad_rows(mid_ref, tok_ref, seq)
    width, wide = lay.width, att_ref.shape[2]
    mid = mid_ref[...] + par_ref[2:3, :]
    for j in range(lay.groups):
        use(j)
        mid += nt(att_ref[j], w_ref[j, :, width : width + wide])
    mid_ref[...] = mid
    normed, _ = norm_parts(mid)
    ln = (normed * par_ref[3:4, :] + par_ref[4:5, :]).astype(BF)
    ln_ref[...] = ln
    sent = []
    for j in range(lay.groups):
        bias = par_ref[pl.ds(6 + lay.t(j, pos), 1), :]
        act, slope = gelu_parts(nn(ln, w_ref[j, :, 0:width]) + bias)
        act_ref[j, :, :] = act.astype(BF)
        slope_ref[j, :, :] = slope.astype(BF)
        grad = tn(cotp_ref[...], act_ref[j]).astype(BF)
        sent += lay.put(grad, stage, outs[4:], out_sems, j, pos)
    for copy in sent:
        copy.wait()


def feed_backward(lay, seq, pos, *refs):
    nb = lay.n_buffers()
    bufs, ins, outs, scratch = split_refs(refs, nb + lay.n_direct(), 3, 2 + lay.n_grads())
    slope_ref, ln_ref, cot_ref = ins
    lg_ref, small_ref = outs[:2]
    w2_ref, w1_ref, cotp_ref, sems2, sems1, stage, out_sems = scratch
    use2 = lay.fetch(bufs[nb:], w2_ref, sems2, pos, True)
    use1 = lay.fetch(bufs[:nb], w1_ref, sems1, pos)
    pad_rows(cotp_ref, cot_ref, seq)
    cot = cotp_ref[...]
    ln = ln_ref[...]
    small_ref[...] = jnp.zeros_like(small_ref)
    sent = []
    for j in range(lay.groups):
        use2(j)
        pre_grad = nn(cot, w2_ref[j]) * slope_ref[j].astype(F32)
        small_ref[pl.ds(6 + lay.t(j, pos), 1), :] = jnp.sum(pre_grad, axis=0, keepdims=True)
        pgb = pre_grad.astype(BF)
        sent += lay.put(tn(ln, pgb).astype(BF), stage, outs[2:], out_sems, j, pos)
        use1(j)
        part = nt(pgb, w1_ref[j, :, 0 : lay.width])
        if j == 0:
            lg_ref[...] = part
        else:
            lg_ref[...] += part
    for copy in sent:
        copy.wait()


def mid_backward(lay, seq, pos, *refs):
    bufs, ins, outs, scratch = split_refs(refs, lay.n_buffers(), 6, 3 + lay.n_grads())
    lg_ref, mid_ref, att_ref, cot_ref, small_in, par_ref = ins
    mg_ref, ag_ref, small_ref = outs[:3]
    w_ref, cotp_ref, sems, stage, out_sems = scratch
    width, wide = lay.width, ag_ref.shape[2]
    bufs = [buf.at[:, width:] if lay.fast else buf.at[:, :, width:] for buf in bufs]
    use = lay.fetch(bufs, w_ref, sems, pos)
    pad_rows(cotp_ref, cot_ref, seq)
    normed, root = norm_parts(mid_ref[...])
    grad = lg_ref[...]
    cot = cotp_ref[...]
    mid_grad = cot + norm_back(grad * par_ref[3:4, :], normed, root)
    mg_ref[...] = mid_grad
    mgb = mid_grad.astype(BF)
    pad = jnp.zeros((width, outs[3].shape[-1] - wide), F32)
    sent = []
    for j in range(lay.groups):
        proj = jnp.concatenate([tn(mgb, att_ref[j]), pad], axis=1)
        sent += lay.put(proj.astype(BF), stage, outs[3:], out_sems, j, pos)
    small_ref[...] = small_in[...]
    small_ref[2:3, :] = jnp.sum(mid_grad, axis=0, keepdims=True)
    small_ref[3:4, :] = jnp.sum(grad * normed, axis=0, keepdims=True)
    small_ref[4:5, :] = jnp.sum(grad, axis=0, keepdims=True)
    small_ref[5:6, :] = jnp.sum(cot, axis=0, keepdims=True)
    for j in range(lay.groups):
        use(j)
        ag_ref[j, :, :] = nn(mgb, w_ref[j, :, 0:wide]).astype(BF)
    for copy in sent:
        copy.wait()


def feed_output(lay, seq, pos, *refs):
    bufs, ins, (out_ref,), (w_ref, acc, sems) = split_refs(refs, lay.n_direct(), 3, 1)
    act_ref, mid_ref, par_ref = ins
    use = lay.fetch(bufs, w_ref, sems, pos, True)
    acc[...] = mid_ref[...] + par_ref[5:6, :]
    for j in range(lay.groups):
        use(j)
        acc[...] += nt(act_ref[j], w_ref[j])
    out_ref[...] = acc[0:seq, :].astype(BF)


def attention_backward(lay, seq, hd, pos, *refs):
    bufs, ins, outs, scratch = split_refs(refs, lay.n_buffers(), 9, 2 + lay.n_grads())
    tok_ref, ln_ref, qkv_ref, probs_ref, att_ref, ag_ref, mg_ref, small_in, par_ref = ins
    dx_ref, small_ref = outs[:2]
    x_ref, w_ref, dqkv_ref, db_ref, ln_acc, sems, stage, out_sems = scratch
    use = lay.fetch(bufs, w_ref, sems, pos)
    wide = att_ref.shape[2]
    heads = wide // hd
    scale = hd**-0.5
    small_ref[...] = small_in[...]
    pad_rows(x_ref, tok_ref, seq)
    ln_acc[...] = jnp.zeros_like(ln_acc)
    three = slice(0, 3 * wide)
    for j in range(lay.groups):
        use(j)
        att_grad = ag_ref[j]
        prod = att_grad.astype(F32) * att_ref[j].astype(F32)
        for h in range(heads):
            at = slice(h * hd, (h + 1) * hd)
            q = qkv_ref[j, :, h * hd : (h + 1) * hd]
            k = qkv_ref[j, :, wide + h * hd : wide + (h + 1) * hd]
            v = qkv_ref[j, :, 2 * wide + h * hd : 2 * wide + (h + 1) * hd]
            p = probs_ref[j * heads + h]
            da = att_grad[:, at]
            delta = jnp.sum(prod[:, at], axis=-1, keepdims=True)
            ds = (p.astype(F32) * (nt(da, v) - delta) * scale).astype(BF)
            dqkv_ref[:, h * hd : (h + 1) * hd] = nn(ds, k)
            dqkv_ref[:, wide + h * hd : wide + (h + 1) * hd] = tn(ds, q)
            dqkv_ref[:, 2 * wide + h * hd : 2 * wide + (h + 1) * hd] = tn(p, da)
        dqkv = dqkv_ref[...]
        small_ref[pl.ds(10 + lay.t(j, pos), 1), three] = jnp.sum(dqkv, axis=0, keepdims=True)
        dqkv = dqkv.astype(BF)
        db_ref[j, :, :] = dqkv
        ln_acc[...] += nt(dqkv, w_ref[j, :, three])
    normed, root = norm_parts(x_ref[...])
    grad = ln_acc[...]
    dx = mg_ref[...] + norm_back(grad * par_ref[0:1, :], normed, root)
    dx_ref[...] = dx[0:seq, :]
    small_ref[0:1, :] = jnp.sum(grad * normed, axis=0, keepdims=True)
    small_ref[1:2, :] = jnp.sum(grad, axis=0, keepdims=True)
    width = lay.width
    spare = jnp.zeros((width, SPARE), F32)
    if lay.fast:
        small = small_ref[...].astype(BF)
        order, same = unit_order(width, 8)
        col = lax.broadcasted_iota(jnp.int32, (width, 16), 1)
        spare = jnp.where(col < 6, nt(same, small), nt(order, small))
        spare = jnp.concatenate([spare, jnp.zeros((width, SPARE - 16), F32)], axis=1)
    ln = ln_ref[...]
    sent = []
    for j in range(lay.groups):
        grad = jnp.concatenate([tn(ln, db_ref[j]), spare], axis=1).astype(BF)
        sent += lay.put(grad, stage, outs[2:], out_sems, j, pos)
    for copy in sent:
        copy.wait()


def finish_attention(chunk, pos, own_ref, ffn_ref, *refs):
    parts, (qkv_ref, fc1_ref, proj_ref, vec_ref, qv_ref, fb_ref, spare_ref) = refs[:3], refs[3:]
    total = own_ref[...]
    for ref in parts:
        total = total + ref[...].astype(F32)
    width = fc1_ref.shape[1]
    fc1_ref[...] = ffn_ref[:, 0:width]
    proj_ref[...] = ffn_ref[:, width : width + proj_ref.shape[0]].T
    wide = qkv_ref.shape[2]
    for c in range(3):
        qkv_ref[c, :, :] = total[:, c * wide : (c + 1) * wide]
    spare_ref[...] = total[:, 3 * wide : 3 * wide + SPARE]
    exact = dict(precision=lax.Precision.HIGHEST, preferred_element_type=F32)
    sub, each = vec_ref.shape[1], fb_ref.shape[0]
    rows = spare_ref[pl.ds(pl.multiple_of(pos[1] * sub, sub), sub), :]
    row = lax.broadcasted_iota(jnp.int32, (8, SPARE), 0)
    col = lax.broadcasted_iota(jnp.int32, (8, SPARE), 1)
    one = jnp.where(row == col, 1.0, 0.0)
    vec = lax.dot_general(one, rows, (((1,), (1,)), ((), ())), **exact)
    vec_ref[...] = vec[0 : vec_ref.shape[0]]
    lane = lax.broadcasted_iota(jnp.int32, (chunk, SPARE), 1)
    spare = spare_ref[...]

    def column(c):
        return jnp.sum(jnp.where(lane == c + pos[1], spare, 0.0), axis=1, keepdims=True)

    def spread(shape, dim, other, by_unit):
        at = lax.broadcasted_iota(jnp.int32, shape, dim)
        at = lax.rem(at, each) if by_unit else at // each
        return at == lax.broadcasted_iota(jnp.int32, shape, other)

    left = jnp.where(spread((8, chunk), 1, 0, True), 1.0, 0.0)
    right = jnp.where(spread((chunk, 16), 0, 1, False), column(6), 0.0)
    fb_ref[...] = jnp.dot(left, right, **exact)[0:each, 0 : fb_ref.shape[1]]
    left = jnp.where(spread((16, chunk), 1, 0, False), 1.0, 0.0)
    right = jnp.where(spread((chunk, 8), 0, 1, True), column(10), 0.0)
    both = jnp.dot(left, right, **exact)
    heads = qv_ref.shape[0]
    for h in range(heads):
        qv_ref[h, 0:1, :] = both[h : h + 1, 0:each]
        qv_ref[h, 1:2, :] = both[2 * heads + h : 2 * heads + h + 1, 0:each]


def shift(x, by):
    n = lax.axis_size("tensor")
    return lax.ppermute(x, "tensor", [(i, (i + by) % n) for i in range(n)])


def flip(x, bit):
    n = lax.axis_size("dp")
    return lax.ppermute(x, "dp", [(i, i ^ bit) for i in range(n)])


def gather_columns(piece):
    return [piece] + [shift(piece, k) for k in (1, 2, 3)]


def join(a, b):
    return jnp.concatenate([a, b], axis=0)


def gather_near(h):
    return flip(h[0], AXIS_X), flip(h[1], AXIS_Y)


def gather_far(both):
    return flip(both[0], AXIS_Y), flip(both[1], AXIS_X)


def direct_near(h):
    return [flip(h[0], AXIS_X), flip(h[0], AXIS_Y), flip(h[1], AXIS_X), flip(h[1], AXIS_Y)]


def direct_far(near):
    return [flip(near[0], AXIS_Y), flip(near[3], AXIS_X)]


def in_direct_order(h, near, far):
    return [h[0], near[0], near[1], far[0], h[1], near[2], near[3], far[1]]


def flip_cores(blocks):
    return [flip(b, CORE) for b in blocks]


def in_order(near, far, core_near, core_far):
    return [near[0], far[0], near[1], far[1], core_near[0], core_far[0], core_near[1], core_far[1]]


def add(a, b):
    return (a.astype(F32) + b.astype(F32)).astype(BF)


class Scatter:
    def __init__(self, *parts):
        self.parts = parts

    def over_cores(self, at):
        sums = [mine[at].astype(F32) + recv[at].astype(F32) for mine, recv in self.parts]
        return sums[0] if len(sums) == 1 else jnp.concatenate(sums, axis=-1)

    def first(self):
        low, high = (slice(2, 4), slice(0, 2)), (slice(1, 4, 2), slice(2, 4))
        return [self.over_cores(at).astype(BF) for at in (low, high)]

    def send_first(self, values):
        return [flip(values[0], AXIS_Y), flip(values[1], AXIS_X)]

    def second(self, got):
        low, high = (slice(0, 2), slice(0, 2)), (slice(0, 4, 2), slice(2, 4))
        return [add(self.over_cores(at), part) for at, part in zip((low, high), got)]

    def send_second(self, values):
        return [flip(values[0][1], AXIS_X), flip(values[1][1], AXIS_Y)]

    def third(self, values, got):
        low = values[0][0].astype(F32) + got[0].astype(F32)
        high = values[1][0].astype(F32) + got[1].astype(F32)
        return [low[0], low[1].astype(BF), high[0].astype(BF), high[1].astype(BF)]

    def send_third(self, parts):
        return [shift(parts[k], k) for k in (1, 2, 3)]

    def last(self, parts, got):
        total = parts[0]
        for part in got:
            total = total + part.astype(F32)
        return total


def barrier(*groups):
    flat, tree = jax.tree.flatten(groups)
    return jax.tree.unflatten(tree, lax.optimization_barrier(tuple(flat)))


def per_device(
    tokens, cotangent, qkv_weight, qv_bias, proj_weight, vectors, fc1_weight, fc1_bias, fc2_weight
):
    n_dp, groups = lax.axis_size("dp"), lax.axis_size("tensor")
    seq, width = tokens.shape
    chunk, wide = qkv_weight.shape[1], qkv_weight.shape[2]
    heads, each = qv_bias.shape[1], qv_bias.shape[2]
    hd = each * n_dp
    units = fc1_weight.shape[1]
    fast = n_dp == 8 and groups == 4
    lay = Layout(fast, groups, width)
    d, z = lax.axis_index("dp"), lax.axis_index("tensor")
    pos = jnp.stack([d, z]).astype(jnp.int32)
    three = 3 * wide
    rows = -(-seq // 16) * 16
    sds = jax.ShapeDtypeStruct
    nb = lay.n_buffers()
    sems = pltpu.SemaphoreType.DMA((groups, lay.n_blocks()))
    wide_a, wide_b = three + SPARE, -(-(width + wide) // 128) * 128

    def run_attention_forward(bufs, *par):
        return kernel_call(
            functools.partial(attention_forward, lay, seq, hd),
            pos,
            bufs,
            [tokens, *par],
            [
                sds((rows, width), BF),
                sds((groups, rows, three), BF),
                sds((groups * heads, rows, rows), BF),
                sds((groups, rows, wide), BF),
                sds((16, width), F32),
            ],
            [pltpu.VMEM((rows, width), F32), pltpu.VMEM((groups, width, wide_a), BF), sems],
        )

    def run_feed_forward(bufs, att, par):
        return kernel_call(
            functools.partial(feed_forward, lay, seq),
            pos,
            bufs,
            [tokens, att, cotangent, par],
            [
                sds((rows, width), F32),
                sds((rows, width), BF),
                sds((groups, rows, units), BF),
                sds((groups, rows, units), BF),
                *lay.grad_shapes(width),
            ],
            [
                pltpu.VMEM((rows, width), BF),
                pltpu.VMEM((groups, width, wide_b), BF),
                sems,
                *lay.stage_shapes(width),
            ],
            lay.n_grads(),
        )

    def run_feed_backward(bufs, slope, ln2):
        return kernel_call(
            functools.partial(feed_backward, lay, seq),
            pos,
            bufs,
            [slope, ln2, cotangent],
            [sds((rows, width), F32), sds((16, width), F32), *lay.grad_shapes(width)],
            [
                pltpu.VMEM((groups, width, width), BF),
                pltpu.VMEM((groups, width, wide_b), BF),
                pltpu.VMEM((rows, width), BF),
                sems,
                sems,
                *lay.stage_shapes(width),
            ],
            lay.n_grads(),
        )

    def run_mid_backward(bufs, ln2_grad, mid, att, small, par):
        return kernel_call(
            functools.partial(mid_backward, lay, seq),
            pos,
            bufs,
            [ln2_grad, mid, att, cotangent, small, par],
            [
                sds((rows, width), F32),
                sds((groups, rows, wide), BF),
                sds((16, width), F32),
                *lay.grad_shapes(wide_b - width),
            ],
            [
                pltpu.VMEM((groups, width, wide_b - width), BF),
                pltpu.VMEM((rows, width), F32),
                sems,
                *lay.stage_shapes(wide_b - width),
            ],
            lay.n_grads(),
        )

    def run_feed_output(bufs, act, mid, par):
        return kernel_call(
            functools.partial(feed_output, lay, seq),
            pos,
            bufs,
            [act, mid, par],
            [sds((seq, width), BF)],
            [pltpu.VMEM((groups, width, width), BF), pltpu.VMEM((rows, width), F32), sems],
        )[0]

    def run_attention_backward(bufs, ln1, qkv, probs, att, att_grad, mid_grad, small, par):
        return kernel_call(
            functools.partial(attention_backward, lay, seq, hd),
            pos,
            bufs,
            [tokens, ln1, qkv, probs, att, att_grad, mid_grad, small, par],
            [sds((seq, width), F32), sds((16, width), F32), *lay.grad_shapes(wide_a)],
            [
                pltpu.VMEM((rows, width), F32),
                pltpu.VMEM((groups, width, wide_a), BF),
                pltpu.VMEM((rows, three), F32),
                pltpu.VMEM((groups, rows, three), BF),
                pltpu.VMEM((rows, width), F32),
                sems,
                *lay.stage_shapes(wide_a),
            ],
            lay.n_grads(),
        )

    sub = chunk // groups
    if fast:
        vmem = pl.BlockSpec(memory_space=pltpu.VMEM)
        piece_a = pl.pallas_call(
            prepare_qkv,
            out_shape=sds((chunk, wide_a), BF),
            in_specs=[vmem] * 4,
            out_specs=vmem,
            scratch_shapes=[
                pltpu.VMEM((16, chunk), F32),
                pltpu.VMEM((16, 128), F32),
                pltpu.VMEM((16, 128), F32),
            ],
        )(qkv_weight, vectors, qv_bias.transpose(1, 0, 2), fc1_bias.T)
        piece_b = pl.pallas_call(
            prepare_fc1,
            out_shape=sds((chunk, wide_b), BF),
            in_specs=[vmem] * 2,
            out_specs=vmem,
        )(fc1_weight, proj_weight)
        piece_c = fc2_weight.T
        z_a = gather_columns(piece_a)
        z_a, piece_b, pos = barrier(z_a, piece_b, pos)
        h_a = barrier(join(*z_a[0:2]), join(*z_a[2:4]))
        near_a = gather_near(h_a)
        z_b = [piece_b, shift(piece_b, 1)]
        near_a, z_b = barrier(near_a, z_b)
        both_a = barrier(join(h_a[0], near_a[0]), join(h_a[1], near_a[1]))
        far_a = gather_far(both_a)
        z_b = [*z_b, shift(z_b[0], 2), shift(z_b[0], 3)]
        h_b = join(*z_b[0:2])
        far_a, z_b, both_a, h_b = barrier(far_a, z_b, both_a, h_b)
        h_b = h_b, join(*z_b[2:4])
        near_b = gather_near(h_b)
        bufs_a = in_order(both_a, far_a, flip_cores(both_a), flip_cores(far_a))
        ln1, qkv, probs, att, par = run_attention_forward(bufs_a)

        near_b, att = barrier(near_b, att)
        both_b = barrier(join(h_b[0], near_b[0]), join(h_b[1], near_b[1]))
        far_b = gather_far(both_b)
        core_b = flip_cores(both_b)
        core_b, piece_c = barrier(core_b, piece_c)
        z_c = gather_columns(piece_c)
        far_b, z_c = barrier(far_b, z_c)
        core_b = core_b + flip_cores(far_b)
        h_c = join(*z_c[0:2]), join(*z_c[2:4])
        near_c = direct_near(h_c)
        bufs_b = in_order(both_b, far_b, core_b[0:2], core_b[2:4])
        mid, ln2, act, slope, *grads_c = run_feed_forward(bufs_b, att, par)
        near_c, grads_c, slope = barrier(near_c, grads_c, slope)
        far_c = direct_far(near_c)
        recv_c, near_c, h_c = barrier(flip(grads_c[1], CORE), near_c, h_c)
        way_c = Scatter((grads_c[0], recv_c))
        first_c = way_c.first()
        first_c, near_c, h_c = barrier(first_c, near_c, h_c)
        core_c = flip_cores([*h_c, *near_c])
        first_c, far_c, core_c, slope = barrier(first_c, far_c, core_c, slope)
        bufs_c = [
            *in_direct_order(h_c, near_c, far_c),
            *in_direct_order(core_c[0:2], core_c[2:6], flip_cores(far_c)),
        ]
        got_c = way_c.send_first(first_c)
        ln2_grad, small, *grads_b = run_feed_backward([*bufs_b, *bufs_c], slope, ln2)
        got_c, grads_b, ln2_grad = barrier(got_c, grads_b, ln2_grad)

        recv_b = flip(grads_b[1], CORE)
        second_c = way_c.second(got_c)
        second_c, ln2_grad = barrier(second_c, ln2_grad)
        got_c = way_c.send_second(second_c)
        mid_grad, att_grad, small, *grads_p = run_mid_backward(
            bufs_b, ln2_grad, mid, att, small, par
        )
        got_c, recv_b, grads_p, mid_grad = barrier(got_c, recv_b, grads_p, mid_grad)

        recv_p = flip(grads_p[1], CORE)
        way_b = Scatter((grads_b[0], recv_b), (grads_p[0], recv_p))
        first_b = way_b.first()
        first_b, mid_grad, got_c = barrier(first_b, mid_grad, got_c)
        got_b = way_b.send_first(first_b)
        third_c = way_c.third(second_c, got_c)
        got_c = [shift(third_c[k], k) for k in (1, 3)]
        input_grad, small, *grads_a = run_attention_backward(
            bufs_a, ln1, qkv, probs, att, att_grad, mid_grad, small, par
        )
        got_b, got_c, third_c, grads_a = barrier(got_b, got_c, third_c, grads_a)

        recv_a = flip(grads_a[1], CORE)
        second_b = way_b.second(got_b)
        second_b, third_c = barrier(second_b, third_c)
        got_b = way_b.send_second(second_b)
        got_c = [*got_c, shift(third_c[2], 2)]
        way_a = Scatter((grads_a[0], recv_a))
        first_a = way_a.first()
        first_a, got_b, got_c, act = barrier(first_a, got_b, got_c, act)
        got_a = way_a.send_first(first_a)
        third_b = way_b.third(second_b, got_b)
        third_b, act = barrier(third_b, act)
        half_b = wide_b // 2
        got_b = [shift(third_b[k], k) for k in (1, 3)] + [shift(third_b[2][:, :half_b], 2)]
        output = run_feed_output(bufs_c, act, mid, par)
        sum_c = way_c.last(third_c, got_c)
        got_a, output, sum_c, got_b, third_b = barrier(got_a, output, sum_c, got_b, third_b)
        second_a = way_a.second(got_a)
        second_a, third_b = barrier(second_a, third_b)
        got_a = way_a.send_second(second_a)
        rest_b = shift(third_b[2][:, half_b:], 2)
        got_b = [*got_b[0:2], jnp.concatenate([got_b[2], rest_b], axis=1)]
        got_a, got_b = barrier(got_a, got_b)
        third_a = way_a.third(second_a, got_a)[1:]
        third_a, second_a, step_a = barrier(third_a, second_a, got_a)
        got_a = [shift(third_a[k - 1], k) for k in (1, 2, 3)]
        got_a[0], second_a, step_a, got_b = barrier(got_a[0], second_a, step_a, got_b)
        own_a = second_a[0][0, 0].astype(F32) + step_a[0][0].astype(F32)
        sum_b = way_b.last(third_b, got_b)
        sum_b, got_a, own_a = barrier(sum_b, got_a, own_a)
        vmem = pl.BlockSpec(memory_space=pltpu.VMEM)
        qkv_grad, sum_b, proj_grad, vec_grad, qv_grad, fc1b_grad = pl.pallas_call(
            functools.partial(finish_attention, chunk),
            out_shape=[
                sds((3, chunk, wide), F32),
                sds((chunk, width), F32),
                sds((wide, chunk), F32),
                sds((6, sub), F32),
                sds((heads, 2, each), F32),
                sds((each, units // hd), F32),
            ],
            in_specs=[pl.BlockSpec(memory_space=pltpu.SMEM)] + [vmem] * 5,
            out_specs=[vmem] * 6,
            scratch_shapes=[pltpu.VMEM((chunk, SPARE), F32)],
        )(pos, own_a, sum_b, *got_a)
        qv_grad, fc1b_grad = qv_grad.transpose(1, 0, 2), fc1b_grad.T
    else:
        none = jnp.zeros_like(qv_bias[0])
        qkv_col = jnp.stack([qv_bias[0], none, qv_bias[1], none]).reshape(chunk)
        spare = jnp.concatenate([vectors, fc1_bias.reshape(1, chunk), qkv_col[None]], axis=0).T
        spare = jnp.pad(spare, ((0, 0), (0, SPARE - spare.shape[1])))
        piece_a = jnp.concatenate([qkv_weight[0], qkv_weight[1], qkv_weight[2], spare], axis=1)
        piece_b = jnp.concatenate([fc1_weight, proj_weight.T], axis=1)
        piece_b = jnp.pad(piece_b, ((0, 0), (0, wide_b - width - wide)))

        def gather(p):
            return [lax.all_gather(lax.all_gather(p, "dp", axis=0, tiled=True), "tensor", axis=0)]

        bufs_a, bufs_b, bufs_c = gather(piece_a), gather(piece_b), gather(fc2_weight.T)
        cols = bufs_a[0][:, :, three : three + 8]
        vec = cols[0, :, 0:6].T
        by_unit = cols.reshape(groups, n_dp, chunk // each, each, 8).transpose(0, 4, 2, 1, 3)
        by_unit = by_unit.reshape(groups, 8, width)
        par = jnp.concatenate([vec, by_unit[:, 6], by_unit[:, 7]], axis=0).astype(F32)
        par = jnp.pad(par, ((0, 16 - par.shape[0]), (0, 0)))
        ln1, qkv, probs, att, par = run_attention_forward(bufs_a, par)
        mid, ln2, act, slope, grads_c = run_feed_forward(bufs_b, att, par)
        ln2_grad, small, grads_b = run_feed_backward([*bufs_b, *bufs_c], slope, ln2)
        mid_grad, att_grad, small, grads_p = run_mid_backward(
            bufs_b, ln2_grad, mid, att, small, par
        )
        output = run_feed_output(bufs_c, act, mid, par)
        input_grad, small, grads_a = run_attention_backward(
            bufs_a, ln1, qkv, probs, att, att_grad, mid_grad, small, par
        )

        def scatter(g):
            g = lax.psum_scatter(g, "tensor", scatter_dimension=0, tiled=False)
            return lax.psum_scatter(g, "dp", scatter_dimension=0, tiled=True).astype(F32)

        sum_c, sum_b, sum_a = scatter(grads_c), scatter(grads_b), scatter(grads_a)
        sum_p = lax.optimization_barrier(scatter(grads_p))
        small = lax.psum(small, ("dp", "tensor"))
        vec_grad = lax.dynamic_slice(small, (0, d * chunk + z * sub), (6, sub))
        by_unit = small[6:14].reshape(2, groups, chunk // each, hd)
        by_unit = lax.dynamic_slice(
            by_unit, (0, z, 0, d * each), (2, 1, chunk // each, each)
        ).reshape(2, chunk)
        fc1b_grad, qv_grad = by_unit[0], by_unit[1]
        fc1b_grad = fc1b_grad.reshape(fc1_bias.shape)
        qv_grad = qv_grad.reshape(4, heads, each)[0::2]
        qkv_grad = jnp.stack([sum_a[:, c * wide : (c + 1) * wide] for c in range(3)])
        proj_grad = sum_p[:, :wide].T
    return (
        output,
        input_grad,
        qkv_grad,
        qv_grad,
        proj_grad,
        vec_grad,
        sum_b,
        fc1b_grad,
        sum_c.T,
    )


def solution(mesh):
    return jax.shard_map(
        per_device,
        mesh=mesh,
        in_specs=(
            P(("dp", "tensor"), None),
            P(("dp", "tensor"), None),
            P(None, "dp", "tensor"),
            P(None, "tensor", "dp"),
            P("tensor", "dp"),
            P(None, "dp"),
            P("dp", "tensor"),
            P("tensor", "dp"),
            P("tensor", "dp"),
        ),
        out_specs=(
            P(("dp", "tensor"), None),
            P(("dp", "tensor"), None),
            P(None, "dp", "tensor"),
            P(None, "tensor", "dp"),
            P("tensor", "dp"),
            P(None, ("dp", "tensor")),
            P("dp", "tensor"),
            P("tensor", "dp"),
            P("tensor", "dp"),
        ),
        check_vma=False,
    )
```

```python
import functools

import jax
import jax.numpy as jnp
from jax import lax
from jax.experimental import pallas as pl
from jax.experimental.pallas import tpu as pltpu
from jax.sharding import PartitionSpec as P

BF = jnp.bfloat16
F32 = jnp.float32
norm_eps = 1e-06
half_root = 0.7071067811865476
density_scale = 0.3989422804014327
VMEM_LIMIT = 56 * 1024 * 1024


def nn(a, b):
    return jnp.dot(a, b, preferred_element_type=F32)


def nt(a, b):
    return lax.dot_general(a, b, (((1,), (1,)), ((), ())), preferred_element_type=F32)


def tn(a, b):
    return lax.dot_general(a, b, (((0,), (0,)), ((), ())), preferred_element_type=F32)


def norm_parts(values):
    centred = values - jnp.mean(values, axis=-1, keepdims=True)
    recip_root = lax.rsqrt(jnp.mean(centred * centred, axis=-1, keepdims=True) + norm_eps)
    return centred * recip_root, recip_root


def norm_back(upstream, normed, recip_root):
    first_mean = jnp.mean(upstream, axis=-1, keepdims=True)
    second_mean = jnp.mean(upstream * normed, axis=-1, keepdims=True)
    return recip_root * (upstream - first_mean - normed * second_mean)


def gelu_parts(values):
    cumul = 0.5 * (1.0 + lax.erf(values * half_root))
    return (values * cumul, cumul + values * jnp.exp(-0.5 * values * values) * density_scale)


class Layout:
    def __init__(self, fast, groups, width):
        self.fast, self.groups, self.width = fast, groups, width
        self.chunk = width // 8 if fast else width

    def t(self, j, pos):
        return lax.rem(pos[1] + (self.groups - j), self.groups) if self.fast else j

    def out(self, j):
        return (self.groups - j) % self.groups if self.fast else j

    def rows(self, k, pos):
        if not self.fast:
            return pl.ds(0, self.width)
        return pl.ds(pl.multiple_of((pos[0] ^ k) * self.chunk, self.chunk), self.chunk)

    def n_buffers(self):
        return 8 if self.fast else 1

    def n_direct(self):
        return 16 if self.fast else 1

    def n_blocks(self):
        return 8 if self.fast else 1

    def sources(self, bufs, j, direct):
        if not self.fast:
            return [(bufs[0].at[j], 0)]
        found = []
        if direct:
            at = pl.ds((j % 2) * self.chunk, self.chunk)
            for core in range(2):
                for n, k in enumerate((0, AXIS_X, AXIS_Y, AXIS_X | AXIS_Y)):
                    found.append((bufs[8 * core + 4 * (j // 2) + n].at[at, :], k ^ core))
            return found
        first, second = (AXIS_X, AXIS_Y) if j < 2 else (AXIS_Y, AXIS_X)
        for core in range(2):
            near, far = bufs[4 * core + 2 * (j // 2) :][:2]
            for ref, axis in ((near, 0), (far, second)):
                for n in range(2):
                    at = pl.ds((2 * n + j % 2) * self.chunk, self.chunk)
                    found.append((ref.at[at, :], axis ^ (first * n) ^ core))
        return found

    def fetch(self, bufs, dest, sems, pos, direct=False, ahead=2):
        def begin(j):
            found = []
            for n, (src, k) in enumerate(self.sources(bufs, j, direct)):
                copy = pltpu.make_async_copy(src, dest.at[j, self.rows(k, pos), :], sems.at[j, n])
                copy.start()
                found.append(copy)
            return found

        copies = [begin(j) for j in range(min(ahead, self.groups))]

        def use(j):
            for copy in copies[j]:
                copy.wait()
            if j + ahead < self.groups:
                copies.append(begin(j + ahead))

        return use

    def put(self, grad, stage, outs, sems, j, pos):
        at = self.out(j)
        if not self.fast:
            stage[at, :, :] = grad
            copies = [pltpu.make_async_copy(stage.at[at], outs[0].at[at], sems.at[j, 0])]
        else:
            for r in range(8):
                other = pos[0] ^ r
                stage[other & 1, other >> 1, at, :, :] = grad[r * self.chunk : (r + 1) * self.chunk]
            copies = [
                pltpu.make_async_copy(stage.at[n, :, at], outs[n].at[:, at], sems.at[j, n])
                for n in range(2)
            ]
        for copy in copies:
            copy.start()
        return copies

    def stage_shapes(self, wide):
        shape = (2, 4, self.groups, self.chunk, wide) if self.fast else (self.groups, self.width, wide)
        return [pltpu.VMEM(shape, BF), pltpu.SemaphoreType.DMA((self.groups, 2))]

    def n_grads(self):
        return 2 if self.fast else 1

    def grad_shapes(self, wide):
        if not self.fast:
            return [jax.ShapeDtypeStruct((self.groups, self.width, wide), BF)]
        return [jax.ShapeDtypeStruct((4, self.groups, self.chunk, wide), BF)] * 2


SPARE = 64
CORE, AXIS_X, AXIS_Y = 1, 2, 4


def unit_order(width, n):
    i = lax.broadcasted_iota(jnp.int32, (width, width), 0)
    c = lax.broadcasted_iota(jnp.int32, (width, width), 1)
    per = width // n
    hit = i == (lax.rem(c, 64) // 8) * per + (c // 64) * 8 + lax.rem(c, 8)
    same = i == c
    return jnp.where(hit, 1.0, 0.0).astype(BF), jnp.where(same, 1.0, 0.0).astype(BF)


def kernel_call(body, pos, bufs, ins, outs, scratch, n_any=0):
    in_hbm = pl.BlockSpec(memory_space=pl.ANY)
    vmem, smem = pl.BlockSpec(memory_space=pltpu.VMEM), pl.BlockSpec(memory_space=pltpu.SMEM)
    return pl.pallas_call(
        body,
        out_shape=outs,
        in_specs=[smem] + [in_hbm] * len(bufs) + [vmem] * len(ins),
        out_specs=[vmem] * (len(outs) - n_any) + [in_hbm] * n_any,
        scratch_shapes=scratch,
        compiler_params=pltpu.CompilerParams(vmem_limit_bytes=VMEM_LIMIT),
        cost_estimate=pl.CostEstimate(flops=0, bytes_accessed=0, transcendentals=0),
    )(pos, *bufs, *ins)


def split_refs(refs, n_bufs, n_in, n_out):
    bufs, refs = refs[:n_bufs], refs[n_bufs:]
    return bufs, refs[:n_in], refs[n_in : n_in + n_out], refs[n_in + n_out :]


def prepare_qkv(qkv_ref, vec_ref, qv_ref, fb_ref, out_ref, rows_ref, fb_pad, qv_pad):
    wide, chunk = qkv_ref.shape[2], qkv_ref.shape[1]
    heads, each = qv_ref.shape[0], qv_ref.shape[2]
    for c in range(3):
        out_ref[:, c * wide : (c + 1) * wide] = qkv_ref[c]
    for ref in (rows_ref, fb_pad, qv_pad):
        ref[...] = jnp.zeros_like(ref)
    rows_ref[0 : vec_ref.shape[0], :] = vec_ref[...].astype(F32)
    fb_pad[0:each, 0 : fb_ref.shape[1]] = fb_ref[...].astype(F32)
    for h in range(heads):
        both = qv_ref[h].astype(F32)
        qv_pad[h : h + 1, 0:each] = both[0:1]
        qv_pad[2 * heads + h : 2 * heads + h + 1, 0:each] = both[1:2]
    row = lax.broadcasted_iota(jnp.int32, (16, SPARE), 0)
    col = lax.broadcasted_iota(jnp.int32, (16, SPARE), 1)
    spare = tn(rows_ref[...].astype(BF), jnp.where(row == col, 1.0, 0.0).astype(BF))
    at = lax.broadcasted_iota(jnp.int32, (chunk, 16), 0)
    slot = lax.broadcasted_iota(jnp.int32, (chunk, 16), 1)
    by_group = jnp.where(at // each == slot, 1.0, 0.0).astype(BF)
    by_unit = jnp.where(lax.rem(at, each) == slot, 1.0, 0.0).astype(BF)
    at = lax.broadcasted_iota(jnp.int32, (chunk, 128), 0)
    lane = lax.broadcasted_iota(jnp.int32, (chunk, 128), 1)
    out_col = lax.broadcasted_iota(jnp.int32, (chunk, SPARE), 1)
    fb = jnp.where(lane == at // each, nn(by_unit, fb_pad[...].astype(BF)), 0.0)
    qv = jnp.where(lane == lax.rem(at, each), nn(by_group, qv_pad[...].astype(BF)), 0.0)
    for c, spread in ((6, fb), (7, qv)):
        spare += jnp.where(out_col == c, jnp.sum(spread, axis=1, keepdims=True), 0.0)
    out_ref[:, 3 * wide : 3 * wide + SPARE] = spare.astype(BF)


def prepare_fc1(fc1_ref, proj_ref, out_ref):
    width, wide = fc1_ref.shape[1], proj_ref.shape[0]
    out_ref[:, 0:width] = fc1_ref[...]
    row = lax.broadcasted_iota(jnp.int32, (wide, wide), 0)
    col = lax.broadcasted_iota(jnp.int32, (wide, wide), 1)
    one = jnp.where(row == col, 1.0, 0.0).astype(BF)
    out_ref[:, width:] = jnp.zeros_like(out_ref[:, width:])
    out_ref[:, width : width + wide] = tn(proj_ref[...], one).astype(BF)


def pad_rows(dest, source, seq):
    dest[...] = jnp.zeros_like(dest)
    dest[0:seq, :] = source[...].astype(dest.dtype)


def attention_forward(lay, seq, hd, pos, *refs):
    bufs, ins, outs, scratch = split_refs(refs, lay.n_buffers(), 1 if lay.fast else 2, 5)
    tok_ref = ins[0]
    ln_ref, qkv_ref, probs_ref, att_ref, par_ref = outs
    x_ref, w_ref, sems = scratch
    use = lay.fetch(bufs, w_ref, sems, pos, ahead=lay.groups)
    pad_rows(x_ref, tok_ref, seq)
    rows = x_ref.shape[0]
    wide = att_ref.shape[2]
    heads = wide // hd
    normed, _ = norm_parts(x_ref[...])
    if lay.fast:
        width = lay.width
        order, _ = unit_order(width, 8)
        row = lax.broadcasted_iota(jnp.int32, (16, SPARE), 0)
        col = lax.broadcasted_iota(jnp.int32, (16, SPARE), 1)
        par = jnp.zeros((16, width), F32)
        units = jnp.zeros((16, width), F32)
        for j in range(lay.groups):
            use(j)
            spare = w_ref[j, :, 3 * wide : 3 * wide + SPARE]
            t = lay.t(j, pos)
            if j == 0:
                par = nt(jnp.where((row == col) & (row < 6), 1.0, 0.0).astype(BF), spare)
            pick = ((row == 6 + t) & (col == 6)) | ((row == 10 + t) & (col == 7))
            units += nt(jnp.where(pick, 1.0, 0.0).astype(BF), spare)
        par_ref[...] = par + nn(units.astype(BF), order)
    else:
        for j in range(lay.groups):
            use(j)
        par_ref[...] = ins[1][...]
    ln = (normed * par_ref[0:1, :] + par_ref[1:2, :]).astype(BF)
    ln_ref[...] = ln
    valid = lax.broadcasted_iota(jnp.int32, (rows, rows), 1) < seq
    for j in range(lay.groups):
        bias = par_ref[pl.ds(10 + lay.t(j, pos), 1), 0 : 3 * wide]
        qkv_ref[j, :, :] = (nn(ln, w_ref[j, :, 0 : 3 * wide]) + bias).astype(BF)
        for h in range(heads):
            q = qkv_ref[j, :, h * hd : (h + 1) * hd]
            k = qkv_ref[j, :, wide + h * hd : wide + (h + 1) * hd]
            v = qkv_ref[j, :, 2 * wide + h * hd : 2 * wide + (h + 1) * hd]
            scores = jnp.where(valid, nt(q, k) * (hd**-0.5), -1e30)
            top = jnp.max(scores, axis=-1, keepdims=True)
            e = jnp.exp(scores - top)
            p = (e * (1.0 / jnp.sum(e, axis=-1, keepdims=True))).astype(BF)
            probs_ref[j * heads + h, :, :] = p
            att_ref[j, :, h * hd : (h + 1) * hd] = nn(p, v).astype(BF)


def feed_forward(lay, seq, pos, *refs):
    bufs, ins, outs, scratch = split_refs(refs, lay.n_buffers(), 4, 4 + lay.n_grads())
    tok_ref, att_ref, cot_ref, par_ref = ins
    mid_ref, ln_ref, act_ref, slope_ref = outs[:4]
    cotp_ref, w_ref, sems, stage, out_sems = scratch
    use = lay.fetch(bufs, w_ref, sems, pos, ahead=lay.groups)
    pad_rows(cotp_ref, cot_ref, seq)
    pad_rows(mid_ref, tok_ref, seq)
    width, wide = lay.width, att_ref.shape[2]
    mid = mid_ref[...] + par_ref[2:3, :]
    for j in range(lay.groups):
        use(j)
        mid += nt(att_ref[j], w_ref[j, :, width : width + wide])
    mid_ref[...] = mid
    normed, _ = norm_parts(mid)
    ln = (normed * par_ref[3:4, :] + par_ref[4:5, :]).astype(BF)
    ln_ref[...] = ln
    sent = []
    for j in range(lay.groups):
        bias = par_ref[pl.ds(6 + lay.t(j, pos), 1), :]
        act, slope = gelu_parts(nn(ln, w_ref[j, :, 0:width]) + bias)
        act_ref[j, :, :] = act.astype(BF)
        slope_ref[j, :, :] = slope.astype(BF)
        grad = tn(cotp_ref[...], act_ref[j]).astype(BF)
        sent += lay.put(grad, stage, outs[4:], out_sems, j, pos)
    for copy in sent:
        copy.wait()


def feed_backward(lay, seq, pos, *refs):
    nb = lay.n_buffers()
    bufs, ins, outs, scratch = split_refs(refs, nb + lay.n_direct(), 3, 2 + lay.n_grads())
    slope_ref, ln_ref, cot_ref = ins
    lg_ref, small_ref = outs[:2]
    w2_ref, w1_ref, cotp_ref, sems2, sems1, stage, out_sems = scratch
    use2 = lay.fetch(bufs[nb:], w2_ref, sems2, pos, True)
    use1 = lay.fetch(bufs[:nb], w1_ref, sems1, pos)
    pad_rows(cotp_ref, cot_ref, seq)
    cot = cotp_ref[...]
    ln = ln_ref[...]
    small_ref[...] = jnp.zeros_like(small_ref)
    sent = []
    for j in range(lay.groups):
        use2(j)
        pre_grad = nn(cot, w2_ref[j]) * slope_ref[j].astype(F32)
        small_ref[pl.ds(6 + lay.t(j, pos), 1), :] = jnp.sum(pre_grad, axis=0, keepdims=True)
        pgb = pre_grad.astype(BF)
        sent += lay.put(tn(ln, pgb).astype(BF), stage, outs[2:], out_sems, j, pos)
        use1(j)
        part = nt(pgb, w1_ref[j, :, 0 : lay.width])
        if j == 0:
            lg_ref[...] = part
        else:
            lg_ref[...] += part
    for copy in sent:
        copy.wait()


def mid_backward(lay, seq, pos, *refs):
    bufs, ins, outs, scratch = split_refs(refs, lay.n_buffers(), 6, 3 + lay.n_grads())
    lg_ref, mid_ref, att_ref, cot_ref, small_in, par_ref = ins
    mg_ref, ag_ref, small_ref = outs[:3]
    w_ref, cotp_ref, sems, stage, out_sems = scratch
    width, wide = lay.width, ag_ref.shape[2]
    bufs = [buf.at[:, width:] if lay.fast else buf.at[:, :, width:] for buf in bufs]
    use = lay.fetch(bufs, w_ref, sems, pos)
    pad_rows(cotp_ref, cot_ref, seq)
    normed, root = norm_parts(mid_ref[...])
    grad = lg_ref[...]
    cot = cotp_ref[...]
    mid_grad = cot + norm_back(grad * par_ref[3:4, :], normed, root)
    mg_ref[...] = mid_grad
    mgb = mid_grad.astype(BF)
    pad = jnp.zeros((width, outs[3].shape[-1] - wide), F32)
    sent = []
    for j in range(lay.groups):
        proj = jnp.concatenate([tn(mgb, att_ref[j]), pad], axis=1)
        sent += lay.put(proj.astype(BF), stage, outs[3:], out_sems, j, pos)
    small_ref[...] = small_in[...]
    small_ref[2:3, :] = jnp.sum(mid_grad, axis=0, keepdims=True)
    small_ref[3:4, :] = jnp.sum(grad * normed, axis=0, keepdims=True)
    small_ref[4:5, :] = jnp.sum(grad, axis=0, keepdims=True)
    small_ref[5:6, :] = jnp.sum(cot, axis=0, keepdims=True)
    for j in range(lay.groups):
        use(j)
        ag_ref[j, :, :] = nn(mgb, w_ref[j, :, 0:wide]).astype(BF)
    for copy in sent:
        copy.wait()


def feed_output(lay, seq, pos, *refs):
    bufs, ins, (out_ref,), (w_ref, acc, sems) = split_refs(refs, lay.n_direct(), 3, 1)
    act_ref, mid_ref, par_ref = ins
    use = lay.fetch(bufs, w_ref, sems, pos, True)
    acc[...] = mid_ref[...] + par_ref[5:6, :]
    for j in range(lay.groups):
        use(j)
        acc[...] += nt(act_ref[j], w_ref[j])
    out_ref[...] = acc[0:seq, :].astype(BF)


def attention_backward(lay, seq, hd, pos, *refs):
    bufs, ins, outs, scratch = split_refs(refs, lay.n_buffers(), 9, 2 + lay.n_grads())
    tok_ref, ln_ref, qkv_ref, probs_ref, att_ref, ag_ref, mg_ref, small_in, par_ref = ins
    dx_ref, small_ref = outs[:2]
    x_ref, w_ref, dqkv_ref, db_ref, ln_acc, sems, stage, out_sems = scratch
    use = lay.fetch(bufs, w_ref, sems, pos)
    wide = att_ref.shape[2]
    heads = wide // hd
    scale = hd**-0.5
    small_ref[...] = small_in[...]
    pad_rows(x_ref, tok_ref, seq)
    ln_acc[...] = jnp.zeros_like(ln_acc)
    three = slice(0, 3 * wide)
    for j in range(lay.groups):
        use(j)
        att_grad = ag_ref[j]
        prod = att_grad.astype(F32) * att_ref[j].astype(F32)
        for h in range(heads):
            at = slice(h * hd, (h + 1) * hd)
            q = qkv_ref[j, :, h * hd : (h + 1) * hd]
            k = qkv_ref[j, :, wide + h * hd : wide + (h + 1) * hd]
            v = qkv_ref[j, :, 2 * wide + h * hd : 2 * wide + (h + 1) * hd]
            p = probs_ref[j * heads + h]
            da = att_grad[:, at]
            delta = jnp.sum(prod[:, at], axis=-1, keepdims=True)
            ds = (p.astype(F32) * (nt(da, v) - delta) * scale).astype(BF)
            dqkv_ref[:, h * hd : (h + 1) * hd] = nn(ds, k)
            dqkv_ref[:, wide + h * hd : wide + (h + 1) * hd] = tn(ds, q)
            dqkv_ref[:, 2 * wide + h * hd : 2 * wide + (h + 1) * hd] = tn(p, da)
        dqkv = dqkv_ref[...]
        small_ref[pl.ds(10 + lay.t(j, pos), 1), three] = jnp.sum(dqkv, axis=0, keepdims=True)
        dqkv = dqkv.astype(BF)
        db_ref[j, :, :] = dqkv
        ln_acc[...] += nt(dqkv, w_ref[j, :, three])
    normed, root = norm_parts(x_ref[...])
    grad = ln_acc[...]
    dx = mg_ref[...] + norm_back(grad * par_ref[0:1, :], normed, root)
    dx_ref[...] = dx[0:seq, :]
    small_ref[0:1, :] = jnp.sum(grad * normed, axis=0, keepdims=True)
    small_ref[1:2, :] = jnp.sum(grad, axis=0, keepdims=True)
    width = lay.width
    spare = jnp.zeros((width, SPARE), F32)
    if lay.fast:
        small = small_ref[...].astype(BF)
        order, same = unit_order(width, 8)
        col = lax.broadcasted_iota(jnp.int32, (width, 16), 1)
        spare = jnp.where(col < 6, nt(same, small), nt(order, small))
        spare = jnp.concatenate([spare, jnp.zeros((width, SPARE - 16), F32)], axis=1)
    ln = ln_ref[...]
    sent = []
    for j in range(lay.groups):
        grad = jnp.concatenate([tn(ln, db_ref[j]), spare], axis=1).astype(BF)
        sent += lay.put(grad, stage, outs[2:], out_sems, j, pos)
    for copy in sent:
        copy.wait()


def finish_attention(chunk, pos, own_ref, ffn_ref, *refs):
    parts, (qkv_ref, fc1_ref, proj_ref, vec_ref, qv_ref, fb_ref, spare_ref) = refs[:3], refs[3:]
    total = own_ref[...]
    for ref in parts:
        total = total + ref[...].astype(F32)
    width = fc1_ref.shape[1]
    fc1_ref[...] = ffn_ref[:, 0:width]
    proj_ref[...] = ffn_ref[:, width : width + proj_ref.shape[0]].T
    wide = qkv_ref.shape[2]
    for c in range(3):
        qkv_ref[c, :, :] = total[:, c * wide : (c + 1) * wide]
    spare_ref[...] = total[:, 3 * wide : 3 * wide + SPARE]
    exact = dict(precision=lax.Precision.HIGHEST, preferred_element_type=F32)
    sub, each = vec_ref.shape[1], fb_ref.shape[0]
    rows = spare_ref[pl.ds(pl.multiple_of(pos[1] * sub, sub), sub), :]
    row = lax.broadcasted_iota(jnp.int32, (8, SPARE), 0)
    col = lax.broadcasted_iota(jnp.int32, (8, SPARE), 1)
    one = jnp.where(row == col, 1.0, 0.0)
    vec = lax.dot_general(one, rows, (((1,), (1,)), ((), ())), **exact)
    vec_ref[...] = vec[0 : vec_ref.shape[0]]
    lane = lax.broadcasted_iota(jnp.int32, (chunk, SPARE), 1)
    spare = spare_ref[...]

    def column(c):
        return jnp.sum(jnp.where(lane == c + pos[1], spare, 0.0), axis=1, keepdims=True)

    def spread(shape, dim, other, by_unit):
        at = lax.broadcasted_iota(jnp.int32, shape, dim)
        at = lax.rem(at, each) if by_unit else at // each
        return at == lax.broadcasted_iota(jnp.int32, shape, other)

    left = jnp.where(spread((8, chunk), 1, 0, True), 1.0, 0.0)
    right = jnp.where(spread((chunk, 16), 0, 1, False), column(6), 0.0)
    fb_ref[...] = jnp.dot(left, right, **exact)[0:each, 0 : fb_ref.shape[1]]
    left = jnp.where(spread((16, chunk), 1, 0, False), 1.0, 0.0)
    right = jnp.where(spread((chunk, 8), 0, 1, True), column(10), 0.0)
    both = jnp.dot(left, right, **exact)
    heads = qv_ref.shape[0]
    for h in range(heads):
        qv_ref[h, 0:1, :] = both[h : h + 1, 0:each]
        qv_ref[h, 1:2, :] = both[2 * heads + h : 2 * heads + h + 1, 0:each]


def shift(x, by):
    n = lax.axis_size("tensor")
    return lax.ppermute(x, "tensor", [(i, (i + by) % n) for i in range(n)])


def flip(x, bit):
    n = lax.axis_size("dp")
    return lax.ppermute(x, "dp", [(i, i ^ bit) for i in range(n)])


def gather_columns(piece):
    return [piece] + [shift(piece, k) for k in (1, 2, 3)]


def join(a, b):
    return jnp.concatenate([a, b], axis=0)


def gather_near(h):
    return flip(h[0], AXIS_X), flip(h[1], AXIS_Y)


def gather_far(both):
    return flip(both[0], AXIS_Y), flip(both[1], AXIS_X)


def direct_near(h):
    return [flip(h[0], AXIS_X), flip(h[0], AXIS_Y), flip(h[1], AXIS_X), flip(h[1], AXIS_Y)]


def direct_far(near):
    return [flip(near[0], AXIS_Y), flip(near[3], AXIS_X)]


def in_direct_order(h, near, far):
    return [h[0], near[0], near[1], far[0], h[1], near[2], near[3], far[1]]


def flip_cores(blocks):
    return [flip(b, CORE) for b in blocks]


def in_order(near, far, core_near, core_far):
    return [near[0], far[0], near[1], far[1], core_near[0], core_far[0], core_near[1], core_far[1]]


def add(a, b):
    return (a.astype(F32) + b.astype(F32)).astype(BF)


class Scatter:
    def __init__(self, *parts):
        self.parts = parts

    def over_cores(self, at):
        sums = [mine[at].astype(F32) + recv[at].astype(F32) for mine, recv in self.parts]
        return sums[0] if len(sums) == 1 else jnp.concatenate(sums, axis=-1)

    def first(self):
        low, high = (slice(2, 4), slice(0, 2)), (slice(1, 4, 2), slice(2, 4))
        return [self.over_cores(at).astype(BF) for at in (low, high)]

    def send_first(self, values):
        return [flip(values[0], AXIS_Y), flip(values[1], AXIS_X)]

    def second(self, got):
        low, high = (slice(0, 2), slice(0, 2)), (slice(0, 4, 2), slice(2, 4))
        return [add(self.over_cores(at), part) for at, part in zip((low, high), got)]

    def send_second(self, values):
        return [flip(values[0][1], AXIS_X), flip(values[1][1], AXIS_Y)]

    def third(self, values, got):
        low = values[0][0].astype(F32) + got[0].astype(F32)
        high = values[1][0].astype(F32) + got[1].astype(F32)
        return [low[0], low[1].astype(BF), high[0].astype(BF), high[1].astype(BF)]

    def send_third(self, parts):
        return [shift(parts[k], k) for k in (1, 2, 3)]

    def last(self, parts, got):
        total = parts[0]
        for part in got:
            total = total + part.astype(F32)
        return total


def barrier(*groups):
    flat, tree = jax.tree.flatten(groups)
    return jax.tree.unflatten(tree, lax.optimization_barrier(tuple(flat)))


def per_device(
    tokens, cotangent, qkv_weight, qv_bias, proj_weight, vectors, fc1_weight, fc1_bias, fc2_weight
):
    n_dp, groups = lax.axis_size("dp"), lax.axis_size("tensor")
    seq, width = tokens.shape
    chunk, wide = qkv_weight.shape[1], qkv_weight.shape[2]
    heads, each = qv_bias.shape[1], qv_bias.shape[2]
    hd = each * n_dp
    units = fc1_weight.shape[1]
    fast = n_dp == 8 and groups == 4
    lay = Layout(fast, groups, width)
    d, z = lax.axis_index("dp"), lax.axis_index("tensor")
    pos = jnp.stack([d, z]).astype(jnp.int32)
    three = 3 * wide
    rows = -(-seq // 16) * 16
    sds = jax.ShapeDtypeStruct
    nb = lay.n_buffers()
    sems = pltpu.SemaphoreType.DMA((groups, lay.n_blocks()))
    wide_a, wide_b = three + SPARE, -(-(width + wide) // 128) * 128

    def run_attention_forward(bufs, *par):
        return kernel_call(
            functools.partial(attention_forward, lay, seq, hd),
            pos,
            bufs,
            [tokens, *par],
            [
                sds((rows, width), BF),
                sds((groups, rows, three), BF),
                sds((groups * heads, rows, rows), BF),
                sds((groups, rows, wide), BF),
                sds((16, width), F32),
            ],
            [pltpu.VMEM((rows, width), F32), pltpu.VMEM((groups, width, wide_a), BF), sems],
        )

    def run_feed_forward(bufs, att, par):
        return kernel_call(
            functools.partial(feed_forward, lay, seq),
            pos,
            bufs,
            [tokens, att, cotangent, par],
            [
                sds((rows, width), F32),
                sds((rows, width), BF),
                sds((groups, rows, units), BF),
                sds((groups, rows, units), BF),
                *lay.grad_shapes(width),
            ],
            [
                pltpu.VMEM((rows, width), BF),
                pltpu.VMEM((groups, width, wide_b), BF),
                sems,
                *lay.stage_shapes(width),
            ],
            lay.n_grads(),
        )

    def run_feed_backward(bufs, slope, ln2):
        return kernel_call(
            functools.partial(feed_backward, lay, seq),
            pos,
            bufs,
            [slope, ln2, cotangent],
            [sds((rows, width), F32), sds((16, width), F32), *lay.grad_shapes(width)],
            [
                pltpu.VMEM((groups, width, width), BF),
                pltpu.VMEM((groups, width, wide_b), BF),
                pltpu.VMEM((rows, width), BF),
                sems,
                sems,
                *lay.stage_shapes(width),
            ],
            lay.n_grads(),
        )

    def run_mid_backward(bufs, ln2_grad, mid, att, small, par):
        return kernel_call(
            functools.partial(mid_backward, lay, seq),
            pos,
            bufs,
            [ln2_grad, mid, att, cotangent, small, par],
            [
                sds((rows, width), F32),
                sds((groups, rows, wide), BF),
                sds((16, width), F32),
                *lay.grad_shapes(wide_b - width),
            ],
            [
                pltpu.VMEM((groups, width, wide_b - width), BF),
                pltpu.VMEM((rows, width), F32),
                sems,
                *lay.stage_shapes(wide_b - width),
            ],
            lay.n_grads(),
        )

    def run_feed_output(bufs, act, mid, par):
        return kernel_call(
            functools.partial(feed_output, lay, seq),
            pos,
            bufs,
            [act, mid, par],
            [sds((seq, width), BF)],
            [pltpu.VMEM((groups, width, width), BF), pltpu.VMEM((rows, width), F32), sems],
        )[0]

    def run_attention_backward(bufs, ln1, qkv, probs, att, att_grad, mid_grad, small, par):
        return kernel_call(
            functools.partial(attention_backward, lay, seq, hd),
            pos,
            bufs,
            [tokens, ln1, qkv, probs, att, att_grad, mid_grad, small, par],
            [sds((seq, width), F32), sds((16, width), F32), *lay.grad_shapes(wide_a)],
            [
                pltpu.VMEM((rows, width), F32),
                pltpu.VMEM((groups, width, wide_a), BF),
                pltpu.VMEM((rows, three), F32),
                pltpu.VMEM((groups, rows, three), BF),
                pltpu.VMEM((rows, width), F32),
                sems,
                *lay.stage_shapes(wide_a),
            ],
            lay.n_grads(),
        )

    sub = chunk // groups
    if fast:
        vmem = pl.BlockSpec(memory_space=pltpu.VMEM)
        piece_a = pl.pallas_call(
            prepare_qkv,
            out_shape=sds((chunk, wide_a), BF),
            in_specs=[vmem] * 4,
            out_specs=vmem,
            scratch_shapes=[
                pltpu.VMEM((16, chunk), F32),
                pltpu.VMEM((16, 128), F32),
                pltpu.VMEM((16, 128), F32),
            ],
        )(qkv_weight, vectors, qv_bias.transpose(1, 0, 2), fc1_bias.T)
        piece_b = pl.pallas_call(
            prepare_fc1,
            out_shape=sds((chunk, wide_b), BF),
            in_specs=[vmem] * 2,
            out_specs=vmem,
        )(fc1_weight, proj_weight)
        piece_c = fc2_weight.T
        z_a = gather_columns(piece_a)
        z_a, piece_b, pos = barrier(z_a, piece_b, pos)
        h_a = barrier(join(*z_a[0:2]), join(*z_a[2:4]))
        near_a = gather_near(h_a)
        z_b = [piece_b, shift(piece_b, 1)]
        near_a, z_b = barrier(near_a, z_b)
        both_a = barrier(join(h_a[0], near_a[0]), join(h_a[1], near_a[1]))
        far_a = gather_far(both_a)
        z_b = [*z_b, shift(z_b[0], 2), shift(z_b[0], 3)]
        h_b = join(*z_b[0:2])
        far_a, z_b, both_a, h_b = barrier(far_a, z_b, both_a, h_b)
        h_b = h_b, join(*z_b[2:4])
        near_b = gather_near(h_b)
        bufs_a = in_order(both_a, far_a, flip_cores(both_a), flip_cores(far_a))
        ln1, qkv, probs, att, par = run_attention_forward(bufs_a)

        near_b, att = barrier(near_b, att)
        both_b = barrier(join(h_b[0], near_b[0]), join(h_b[1], near_b[1]))
        far_b = gather_far(both_b)
        core_b = flip_cores(both_b)
        core_b, piece_c = barrier(core_b, piece_c)
        z_c = gather_columns(piece_c)
        far_b, z_c = barrier(far_b, z_c)
        core_b = core_b + flip_cores(far_b)
        h_c = join(*z_c[0:2]), join(*z_c[2:4])
        near_c = direct_near(h_c)
        bufs_b = in_order(both_b, far_b, core_b[0:2], core_b[2:4])
        mid, ln2, act, slope, *grads_c = run_feed_forward(bufs_b, att, par)
        near_c, grads_c, slope = barrier(near_c, grads_c, slope)
        far_c = direct_far(near_c)
        recv_c, near_c, h_c = barrier(flip(grads_c[1], CORE), near_c, h_c)
        way_c = Scatter((grads_c[0], recv_c))
        first_c = way_c.first()
        first_c, near_c, h_c = barrier(first_c, near_c, h_c)
        core_c = flip_cores([*h_c, *near_c])
        first_c, far_c, core_c, slope = barrier(first_c, far_c, core_c, slope)
        bufs_c = [
            *in_direct_order(h_c, near_c, far_c),
            *in_direct_order(core_c[0:2], core_c[2:6], flip_cores(far_c)),
        ]
        got_c = way_c.send_first(first_c)
        ln2_grad, small, *grads_b = run_feed_backward([*bufs_b, *bufs_c], slope, ln2)
        got_c, grads_b, ln2_grad = barrier(got_c, grads_b, ln2_grad)

        recv_b = flip(grads_b[1], CORE)
        second_c = way_c.second(got_c)
        second_c, ln2_grad = barrier(second_c, ln2_grad)
        got_c = way_c.send_second(second_c)
        mid_grad, att_grad, small, *grads_p = run_mid_backward(
            bufs_b, ln2_grad, mid, att, small, par
        )
        got_c, recv_b, grads_p, mid_grad = barrier(got_c, recv_b, grads_p, mid_grad)

        recv_p = flip(grads_p[1], CORE)
        way_b = Scatter((grads_b[0], recv_b), (grads_p[0], recv_p))
        first_b = way_b.first()
        third_c = way_c.third(second_c, got_c)
        first_b, mid_grad, third_c = barrier(first_b, mid_grad, third_c)
        got_b = way_b.send_first(first_b)
        got_c = [shift(third_c[k], k) for k in (1, 3)]
        input_grad, small, *grads_a = run_attention_backward(
            bufs_a, ln1, qkv, probs, att, att_grad, mid_grad, small, par
        )
        got_b, got_c, third_c, grads_a = barrier(got_b, got_c, third_c, grads_a)

        recv_a = flip(grads_a[1], CORE)
        second_b = way_b.second(got_b)
        second_b, third_c = barrier(second_b, third_c)
        got_b = way_b.send_second(second_b)
        got_c = [*got_c, shift(third_c[2], 2)]
        way_a = Scatter((grads_a[0], recv_a))
        first_a = way_a.first()
        first_a, got_b, got_c, act = barrier(first_a, got_b, got_c, act)
        got_a = way_a.send_first(first_a)
        third_b = way_b.third(second_b, got_b)
        third_b, act = barrier(third_b, act)
        half_b = wide_b // 2
        got_b = [shift(third_b[k], k) for k in (1, 3)] + [shift(third_b[2][:, :half_b], 2)]
        output = run_feed_output(bufs_c, act, mid, par)
        sum_c = way_c.last(third_c, got_c)
        got_a, output, sum_c, got_b, third_b = barrier(got_a, output, sum_c, got_b, third_b)
        second_a = way_a.second(got_a)
        second_a, third_b = barrier(second_a, third_b)
        got_a = way_a.send_second(second_a)
        rest_b = shift(third_b[2][:, half_b:], 2)
        got_b = [*got_b[0:2], jnp.concatenate([got_b[2], rest_b], axis=1)]
        got_a, got_b = barrier(got_a, got_b)
        third_a = way_a.third(second_a, got_a)[1:]
        third_a, second_a, step_a = barrier(third_a, second_a, got_a)
        got_a = [shift(third_a[k - 1], k) for k in (1, 2, 3)]
        got_a[0], second_a, step_a, got_b = barrier(got_a[0], second_a, step_a, got_b)
        own_a = second_a[0][0, 0].astype(F32) + step_a[0][0].astype(F32)
        sum_b = way_b.last(third_b, got_b)
        sum_b, got_a, own_a = barrier(sum_b, got_a, own_a)
        vmem = pl.BlockSpec(memory_space=pltpu.VMEM)
        qkv_grad, sum_b, proj_grad, vec_grad, qv_grad, fc1b_grad = pl.pallas_call(
            functools.partial(finish_attention, chunk),
            out_shape=[
                sds((3, chunk, wide), F32),
                sds((chunk, width), F32),
                sds((wide, chunk), F32),
                sds((6, sub), F32),
                sds((heads, 2, each), F32),
                sds((each, units // hd), F32),
            ],
            in_specs=[pl.BlockSpec(memory_space=pltpu.SMEM)] + [vmem] * 5,
            out_specs=[vmem] * 6,
            scratch_shapes=[pltpu.VMEM((chunk, SPARE), F32)],
        )(pos, own_a, sum_b, *got_a)
        qv_grad, fc1b_grad = qv_grad.transpose(1, 0, 2), fc1b_grad.T
    else:
        none = jnp.zeros_like(qv_bias[0])
        qkv_col = jnp.stack([qv_bias[0], none, qv_bias[1], none]).reshape(chunk)
        spare = jnp.concatenate([vectors, fc1_bias.reshape(1, chunk), qkv_col[None]], axis=0).T
        spare = jnp.pad(spare, ((0, 0), (0, SPARE - spare.shape[1])))
        piece_a = jnp.concatenate([qkv_weight[0], qkv_weight[1], qkv_weight[2], spare], axis=1)
        piece_b = jnp.concatenate([fc1_weight, proj_weight.T], axis=1)
        piece_b = jnp.pad(piece_b, ((0, 0), (0, wide_b - width - wide)))

        def gather(p):
            return [lax.all_gather(lax.all_gather(p, "dp", axis=0, tiled=True), "tensor", axis=0)]

        bufs_a, bufs_b, bufs_c = gather(piece_a), gather(piece_b), gather(fc2_weight.T)
        cols = bufs_a[0][:, :, three : three + 8]
        vec = cols[0, :, 0:6].T
        by_unit = cols.reshape(groups, n_dp, chunk // each, each, 8).transpose(0, 4, 2, 1, 3)
        by_unit = by_unit.reshape(groups, 8, width)
        par = jnp.concatenate([vec, by_unit[:, 6], by_unit[:, 7]], axis=0).astype(F32)
        par = jnp.pad(par, ((0, 16 - par.shape[0]), (0, 0)))
        ln1, qkv, probs, att, par = run_attention_forward(bufs_a, par)
        mid, ln2, act, slope, grads_c = run_feed_forward(bufs_b, att, par)
        ln2_grad, small, grads_b = run_feed_backward([*bufs_b, *bufs_c], slope, ln2)
        mid_grad, att_grad, small, grads_p = run_mid_backward(
            bufs_b, ln2_grad, mid, att, small, par
        )
        output = run_feed_output(bufs_c, act, mid, par)
        input_grad, small, grads_a = run_attention_backward(
            bufs_a, ln1, qkv, probs, att, att_grad, mid_grad, small, par
        )

        def scatter(g):
            g = lax.psum_scatter(g, "tensor", scatter_dimension=0, tiled=False)
            return lax.psum_scatter(g, "dp", scatter_dimension=0, tiled=True).astype(F32)

        sum_c, sum_b, sum_a = scatter(grads_c), scatter(grads_b), scatter(grads_a)
        sum_p = lax.optimization_barrier(scatter(grads_p))
        small = lax.psum(small, ("dp", "tensor"))
        vec_grad = lax.dynamic_slice(small, (0, d * chunk + z * sub), (6, sub))
        by_unit = small[6:14].reshape(2, groups, chunk // each, hd)
        by_unit = lax.dynamic_slice(
            by_unit, (0, z, 0, d * each), (2, 1, chunk // each, each)
        ).reshape(2, chunk)
        fc1b_grad, qv_grad = by_unit[0], by_unit[1]
        fc1b_grad = fc1b_grad.reshape(fc1_bias.shape)
        qv_grad = qv_grad.reshape(4, heads, each)[0::2]
        qkv_grad = jnp.stack([sum_a[:, c * wide : (c + 1) * wide] for c in range(3)])
        proj_grad = sum_p[:, :wide].T
    return (
        output,
        input_grad,
        qkv_grad,
        qv_grad,
        proj_grad,
        vec_grad,
        sum_b,
        fc1b_grad,
        sum_c.T,
    )


def solution(mesh):
    return jax.shard_map(
        per_device,
        mesh=mesh,
        in_specs=(
            P(("dp", "tensor"), None),
            P(("dp", "tensor"), None),
            P(None, "dp", "tensor"),
            P(None, "tensor", "dp"),
            P("tensor", "dp"),
            P(None, "dp"),
            P("dp", "tensor"),
            P("tensor", "dp"),
            P("tensor", "dp"),
        ),
        out_specs=(
            P(("dp", "tensor"), None),
            P(("dp", "tensor"), None),
            P(None, "dp", "tensor"),
            P(None, "tensor", "dp"),
            P("tensor", "dp"),
            P(None, ("dp", "tensor")),
            P("dp", "tensor"),
            P("tensor", "dp"),
            P("tensor", "dp"),
        ),
        check_vma=False,
    )
```

```python
import functools

import jax
import jax.numpy as jnp
from jax import lax
from jax.experimental import pallas as pl
from jax.experimental.pallas import tpu as pltpu
from jax.sharding import PartitionSpec as P

BF = jnp.bfloat16
F32 = jnp.float32
norm_eps = 1e-06
half_root = 0.7071067811865476
density_scale = 0.3989422804014327
VMEM_LIMIT = 56 * 1024 * 1024


def nn(a, b):
    return jnp.dot(a, b, preferred_element_type=F32)


def nt(a, b):
    return lax.dot_general(a, b, (((1,), (1,)), ((), ())), preferred_element_type=F32)


def tn(a, b):
    return lax.dot_general(a, b, (((0,), (0,)), ((), ())), preferred_element_type=F32)


def norm_parts(values):
    centred = values - jnp.mean(values, axis=-1, keepdims=True)
    recip_root = lax.rsqrt(jnp.mean(centred * centred, axis=-1, keepdims=True) + norm_eps)
    return centred * recip_root, recip_root


def norm_back(upstream, normed, recip_root):
    first_mean = jnp.mean(upstream, axis=-1, keepdims=True)
    second_mean = jnp.mean(upstream * normed, axis=-1, keepdims=True)
    return recip_root * (upstream - first_mean - normed * second_mean)


def gelu_parts(values):
    cumul = 0.5 * (1.0 + lax.erf(values * half_root))
    return (values * cumul, cumul + values * jnp.exp(-0.5 * values * values) * density_scale)


class Layout:
    def __init__(self, fast, groups, width):
        self.fast, self.groups, self.width = fast, groups, width
        self.chunk = width // 8 if fast else width

    def t(self, j, pos):
        return lax.rem(pos[1] + (self.groups - j), self.groups) if self.fast else j

    def out(self, j):
        return (self.groups - j) % self.groups if self.fast else j

    def rows(self, k, pos):
        if not self.fast:
            return pl.ds(0, self.width)
        return pl.ds(pl.multiple_of((pos[0] ^ k) * self.chunk, self.chunk), self.chunk)

    def n_buffers(self):
        return 8 if self.fast else 1

    def n_direct(self):
        return 16 if self.fast else 1

    def n_blocks(self):
        return 8 if self.fast else 1

    def sources(self, bufs, j, direct):
        if not self.fast:
            return [(bufs[0].at[j], 0)]
        found = []
        if direct:
            at = pl.ds((j % 2) * self.chunk, self.chunk)
            for core in range(2):
                for n, k in enumerate((0, AXIS_X, AXIS_Y, AXIS_X | AXIS_Y)):
                    found.append((bufs[8 * core + 4 * (j // 2) + n].at[at, :], k ^ core))
            return found
        first, second = (AXIS_X, AXIS_Y) if j < 2 else (AXIS_Y, AXIS_X)
        for core in range(2):
            near, far = bufs[4 * core + 2 * (j // 2) :][:2]
            for ref, axis in ((near, 0), (far, second)):
                for n in range(2):
                    at = pl.ds((2 * n + j % 2) * self.chunk, self.chunk)
                    found.append((ref.at[at, :], axis ^ (first * n) ^ core))
        return found

    def fetch(self, bufs, dest, sems, pos, direct=False, ahead=2):
        def begin(j):
            found = []
            for n, (src, k) in enumerate(self.sources(bufs, j, direct)):
                copy = pltpu.make_async_copy(src, dest.at[j, self.rows(k, pos), :], sems.at[j, n])
                copy.start()
                found.append(copy)
            return found

        copies = [begin(j) for j in range(min(ahead, self.groups))]

        def use(j):
            for copy in copies[j]:
                copy.wait()
            if j + ahead < self.groups:
                copies.append(begin(j + ahead))

        return use

    def put(self, grad, stage, outs, sems, j, pos):
        at = self.out(j)
        if not self.fast:
            stage[at, :, :] = grad
            copies = [pltpu.make_async_copy(stage.at[at], outs[0].at[at], sems.at[j, 0])]
        else:
            for r in range(8):
                other = pos[0] ^ r
                stage[other & 1, other >> 1, at, :, :] = grad[r * self.chunk : (r + 1) * self.chunk]
            copies = [
                pltpu.make_async_copy(stage.at[n, :, at], outs[n].at[:, at], sems.at[j, n])
                for n in range(2)
            ]
        for copy in copies:
            copy.start()
        return copies

    def stage_shapes(self, wide):
        shape = (2, 4, self.groups, self.chunk, wide) if self.fast else (self.groups, self.width, wide)
        return [pltpu.VMEM(shape, BF), pltpu.SemaphoreType.DMA((self.groups, 2))]

    def n_grads(self):
        return 2 if self.fast else 1

    def grad_shapes(self, wide):
        if not self.fast:
            return [jax.ShapeDtypeStruct((self.groups, self.width, wide), BF)]
        return [jax.ShapeDtypeStruct((4, self.groups, self.chunk, wide), BF)] * 2


SPARE = 64
CORE, AXIS_X, AXIS_Y = 1, 2, 4


def unit_order(width, n):
    i = lax.broadcasted_iota(jnp.int32, (width, width), 0)
    c = lax.broadcasted_iota(jnp.int32, (width, width), 1)
    per = width // n
    hit = i == (lax.rem(c, 64) // 8) * per + (c // 64) * 8 + lax.rem(c, 8)
    same = i == c
    return jnp.where(hit, 1.0, 0.0).astype(BF), jnp.where(same, 1.0, 0.0).astype(BF)


def kernel_call(body, pos, bufs, ins, outs, scratch, n_any=0):
    in_hbm = pl.BlockSpec(memory_space=pl.ANY)
    vmem, smem = pl.BlockSpec(memory_space=pltpu.VMEM), pl.BlockSpec(memory_space=pltpu.SMEM)
    return pl.pallas_call(
        body,
        out_shape=outs,
        in_specs=[smem] + [in_hbm] * len(bufs) + [vmem] * len(ins),
        out_specs=[vmem] * (len(outs) - n_any) + [in_hbm] * n_any,
        scratch_shapes=scratch,
        compiler_params=pltpu.CompilerParams(vmem_limit_bytes=VMEM_LIMIT),
        cost_estimate=pl.CostEstimate(flops=0, bytes_accessed=0, transcendentals=0),
    )(pos, *bufs, *ins)


def split_refs(refs, n_bufs, n_in, n_out):
    bufs, refs = refs[:n_bufs], refs[n_bufs:]
    return bufs, refs[:n_in], refs[n_in : n_in + n_out], refs[n_in + n_out :]


def prepare_qkv(qkv_ref, vec_ref, qv_ref, fb_ref, out_ref, rows_ref, fb_pad, qv_pad):
    wide, chunk = qkv_ref.shape[2], qkv_ref.shape[1]
    heads, each = qv_ref.shape[0], qv_ref.shape[2]
    for c in range(3):
        out_ref[:, c * wide : (c + 1) * wide] = qkv_ref[c]
    for ref in (rows_ref, fb_pad, qv_pad):
        ref[...] = jnp.zeros_like(ref)
    rows_ref[0 : vec_ref.shape[0], :] = vec_ref[...].astype(F32)
    fb_pad[0:each, 0 : fb_ref.shape[1]] = fb_ref[...].astype(F32)
    for h in range(heads):
        both = qv_ref[h].astype(F32)
        qv_pad[h : h + 1, 0:each] = both[0:1]
        qv_pad[2 * heads + h : 2 * heads + h + 1, 0:each] = both[1:2]
    row = lax.broadcasted_iota(jnp.int32, (16, SPARE), 0)
    col = lax.broadcasted_iota(jnp.int32, (16, SPARE), 1)
    spare = tn(rows_ref[...].astype(BF), jnp.where(row == col, 1.0, 0.0).astype(BF))
    at = lax.broadcasted_iota(jnp.int32, (chunk, 16), 0)
    slot = lax.broadcasted_iota(jnp.int32, (chunk, 16), 1)
    by_group = jnp.where(at // each == slot, 1.0, 0.0).astype(BF)
    by_unit = jnp.where(lax.rem(at, each) == slot, 1.0, 0.0).astype(BF)
    at = lax.broadcasted_iota(jnp.int32, (chunk, 128), 0)
    lane = lax.broadcasted_iota(jnp.int32, (chunk, 128), 1)
    out_col = lax.broadcasted_iota(jnp.int32, (chunk, SPARE), 1)
    fb = jnp.where(lane == at // each, nn(by_unit, fb_pad[...].astype(BF)), 0.0)
    qv = jnp.where(lane == lax.rem(at, each), nn(by_group, qv_pad[...].astype(BF)), 0.0)
    for c, spread in ((6, fb), (7, qv)):
        spare += jnp.where(out_col == c, jnp.sum(spread, axis=1, keepdims=True), 0.0)
    out_ref[:, 3 * wide : 3 * wide + SPARE] = spare.astype(BF)


def prepare_fc1(fc1_ref, proj_ref, out_ref):
    width, wide = fc1_ref.shape[1], proj_ref.shape[0]
    out_ref[:, 0:width] = fc1_ref[...]
    row = lax.broadcasted_iota(jnp.int32, (wide, wide), 0)
    col = lax.broadcasted_iota(jnp.int32, (wide, wide), 1)
    one = jnp.where(row == col, 1.0, 0.0).astype(BF)
    out_ref[:, width:] = jnp.zeros_like(out_ref[:, width:])
    out_ref[:, width : width + wide] = tn(proj_ref[...], one).astype(BF)


def pad_rows(dest, source, seq):
    dest[...] = jnp.zeros_like(dest)
    dest[0:seq, :] = source[...].astype(dest.dtype)


def attention_forward(lay, seq, hd, pos, *refs):
    bufs, ins, outs, scratch = split_refs(refs, lay.n_buffers(), 1 if lay.fast else 2, 5)
    tok_ref = ins[0]
    ln_ref, qkv_ref, probs_ref, att_ref, par_ref = outs
    x_ref, w_ref, sems = scratch
    use = lay.fetch(bufs, w_ref, sems, pos, ahead=lay.groups)
    pad_rows(x_ref, tok_ref, seq)
    rows = x_ref.shape[0]
    wide = att_ref.shape[2]
    heads = wide // hd
    normed, _ = norm_parts(x_ref[...])
    if lay.fast:
        width = lay.width
        order, _ = unit_order(width, 8)
        row = lax.broadcasted_iota(jnp.int32, (16, SPARE), 0)
        col = lax.broadcasted_iota(jnp.int32, (16, SPARE), 1)
        par = jnp.zeros((16, width), F32)
        units = jnp.zeros((16, width), F32)
        for j in range(lay.groups):
            use(j)
            spare = w_ref[j, :, 3 * wide : 3 * wide + SPARE]
            t = lay.t(j, pos)
            if j == 0:
                par = nt(jnp.where((row == col) & (row < 6), 1.0, 0.0).astype(BF), spare)
            pick = ((row == 6 + t) & (col == 6)) | ((row == 10 + t) & (col == 7))
            units += nt(jnp.where(pick, 1.0, 0.0).astype(BF), spare)
        par_ref[...] = par + nn(units.astype(BF), order)
    else:
        for j in range(lay.groups):
            use(j)
        par_ref[...] = ins[1][...]
    ln = (normed * par_ref[0:1, :] + par_ref[1:2, :]).astype(BF)
    ln_ref[...] = ln
    valid = lax.broadcasted_iota(jnp.int32, (rows, rows), 1) < seq
    for j in range(lay.groups):
        bias = par_ref[pl.ds(10 + lay.t(j, pos), 1), 0 : 3 * wide]
        qkv_ref[j, :, :] = (nn(ln, w_ref[j, :, 0 : 3 * wide]) + bias).astype(BF)
        for h in range(heads):
            q = qkv_ref[j, :, h * hd : (h + 1) * hd]
            k = qkv_ref[j, :, wide + h * hd : wide + (h + 1) * hd]
            v = qkv_ref[j, :, 2 * wide + h * hd : 2 * wide + (h + 1) * hd]
            scores = jnp.where(valid, nt(q, k) * (hd**-0.5), -1e30)
            top = jnp.max(scores, axis=-1, keepdims=True)
            e = jnp.exp(scores - top)
            p = (e * (1.0 / jnp.sum(e, axis=-1, keepdims=True))).astype(BF)
            probs_ref[j * heads + h, :, :] = p
            att_ref[j, :, h * hd : (h + 1) * hd] = nn(p, v).astype(BF)


def feed_forward(lay, seq, pos, *refs):
    bufs, ins, outs, scratch = split_refs(refs, lay.n_buffers(), 4, 4 + lay.n_grads())
    tok_ref, att_ref, cot_ref, par_ref = ins
    mid_ref, ln_ref, act_ref, slope_ref = outs[:4]
    cotp_ref, w_ref, sems, stage, out_sems = scratch
    use = lay.fetch(bufs, w_ref, sems, pos, ahead=lay.groups)
    pad_rows(cotp_ref, cot_ref, seq)
    pad_rows(mid_ref, tok_ref, seq)
    width, wide = lay.width, att_ref.shape[2]
    mid = mid_ref[...] + par_ref[2:3, :]
    for j in range(lay.groups):
        use(j)
        mid += nt(att_ref[j], w_ref[j, :, width : width + wide])
    mid_ref[...] = mid
    normed, _ = norm_parts(mid)
    ln = (normed * par_ref[3:4, :] + par_ref[4:5, :]).astype(BF)
    ln_ref[...] = ln
    sent = []
    for j in range(lay.groups):
        bias = par_ref[pl.ds(6 + lay.t(j, pos), 1), :]
        act, slope = gelu_parts(nn(ln, w_ref[j, :, 0:width]) + bias)
        act_ref[j, :, :] = act.astype(BF)
        slope_ref[j, :, :] = slope.astype(BF)
        grad = tn(cotp_ref[...], act_ref[j]).astype(BF)
        sent += lay.put(grad, stage, outs[4:], out_sems, j, pos)
    for copy in sent:
        copy.wait()


def feed_backward(lay, seq, pos, *refs):
    nb = lay.n_buffers()
    bufs, ins, outs, scratch = split_refs(refs, nb + lay.n_direct(), 3, 2 + lay.n_grads())
    slope_ref, ln_ref, cot_ref = ins
    lg_ref, small_ref = outs[:2]
    w2_ref, w1_ref, cotp_ref, sems2, sems1, stage, out_sems = scratch
    use2 = lay.fetch(bufs[nb:], w2_ref, sems2, pos, True)
    use1 = lay.fetch(bufs[:nb], w1_ref, sems1, pos)
    pad_rows(cotp_ref, cot_ref, seq)
    cot = cotp_ref[...]
    ln = ln_ref[...]
    small_ref[...] = jnp.zeros_like(small_ref)
    sent = []
    for j in range(lay.groups):
        use2(j)
        pre_grad = nn(cot, w2_ref[j]) * slope_ref[j].astype(F32)
        small_ref[pl.ds(6 + lay.t(j, pos), 1), :] = jnp.sum(pre_grad, axis=0, keepdims=True)
        pgb = pre_grad.astype(BF)
        sent += lay.put(tn(ln, pgb).astype(BF), stage, outs[2:], out_sems, j, pos)
        use1(j)
        part = nt(pgb, w1_ref[j, :, 0 : lay.width])
        if j == 0:
            lg_ref[...] = part
        else:
            lg_ref[...] += part
    for copy in sent:
        copy.wait()


def mid_backward(lay, seq, pos, *refs):
    bufs, ins, outs, scratch = split_refs(refs, lay.n_buffers(), 6, 3 + lay.n_grads())
    lg_ref, mid_ref, att_ref, cot_ref, small_in, par_ref = ins
    mg_ref, ag_ref, small_ref = outs[:3]
    w_ref, cotp_ref, sems, stage, out_sems = scratch
    width, wide = lay.width, ag_ref.shape[2]
    bufs = [buf.at[:, width:] if lay.fast else buf.at[:, :, width:] for buf in bufs]
    use = lay.fetch(bufs, w_ref, sems, pos)
    pad_rows(cotp_ref, cot_ref, seq)
    normed, root = norm_parts(mid_ref[...])
    grad = lg_ref[...]
    cot = cotp_ref[...]
    mid_grad = cot + norm_back(grad * par_ref[3:4, :], normed, root)
    mg_ref[...] = mid_grad
    mgb = mid_grad.astype(BF)
    pad = jnp.zeros((width, outs[3].shape[-1] - wide), F32)
    sent = []
    for j in range(lay.groups):
        proj = jnp.concatenate([tn(mgb, att_ref[j]), pad], axis=1)
        sent += lay.put(proj.astype(BF), stage, outs[3:], out_sems, j, pos)
    small_ref[...] = small_in[...]
    small_ref[2:3, :] = jnp.sum(mid_grad, axis=0, keepdims=True)
    small_ref[3:4, :] = jnp.sum(grad * normed, axis=0, keepdims=True)
    small_ref[4:5, :] = jnp.sum(grad, axis=0, keepdims=True)
    small_ref[5:6, :] = jnp.sum(cot, axis=0, keepdims=True)
    for j in range(lay.groups):
        use(j)
        ag_ref[j, :, :] = nn(mgb, w_ref[j, :, 0:wide]).astype(BF)
    for copy in sent:
        copy.wait()


def feed_output(lay, seq, pos, *refs):
    bufs, ins, (out_ref,), (w_ref, acc, sems) = split_refs(refs, lay.n_direct(), 3, 1)
    act_ref, mid_ref, par_ref = ins
    use = lay.fetch(bufs, w_ref, sems, pos, True)
    acc[...] = mid_ref[...] + par_ref[5:6, :]
    for j in range(lay.groups):
        use(j)
        acc[...] += nt(act_ref[j], w_ref[j])
    out_ref[...] = acc[0:seq, :].astype(BF)


def attention_backward(lay, seq, hd, pos, *refs):
    bufs, ins, outs, scratch = split_refs(refs, lay.n_buffers(), 9, 2 + lay.n_grads())
    tok_ref, ln_ref, qkv_ref, probs_ref, att_ref, ag_ref, mg_ref, small_in, par_ref = ins
    dx_ref, small_ref = outs[:2]
    x_ref, w_ref, dqkv_ref, db_ref, ln_acc, sems, stage, out_sems = scratch
    use = lay.fetch(bufs, w_ref, sems, pos)
    wide = att_ref.shape[2]
    heads = wide // hd
    scale = hd**-0.5
    small_ref[...] = small_in[...]
    pad_rows(x_ref, tok_ref, seq)
    ln_acc[...] = jnp.zeros_like(ln_acc)
    three = slice(0, 3 * wide)
    for j in range(lay.groups):
        use(j)
        att_grad = ag_ref[j]
        prod = att_grad.astype(F32) * att_ref[j].astype(F32)
        for h in range(heads):
            at = slice(h * hd, (h + 1) * hd)
            q = qkv_ref[j, :, h * hd : (h + 1) * hd]
            k = qkv_ref[j, :, wide + h * hd : wide + (h + 1) * hd]
            v = qkv_ref[j, :, 2 * wide + h * hd : 2 * wide + (h + 1) * hd]
            p = probs_ref[j * heads + h]
            da = att_grad[:, at]
            delta = jnp.sum(prod[:, at], axis=-1, keepdims=True)
            ds = (p.astype(F32) * (nt(da, v) - delta) * scale).astype(BF)
            dqkv_ref[:, h * hd : (h + 1) * hd] = nn(ds, k)
            dqkv_ref[:, wide + h * hd : wide + (h + 1) * hd] = tn(ds, q)
            dqkv_ref[:, 2 * wide + h * hd : 2 * wide + (h + 1) * hd] = tn(p, da)
        dqkv = dqkv_ref[...]
        small_ref[pl.ds(10 + lay.t(j, pos), 1), three] = jnp.sum(dqkv, axis=0, keepdims=True)
        dqkv = dqkv.astype(BF)
        db_ref[j, :, :] = dqkv
        ln_acc[...] += nt(dqkv, w_ref[j, :, three])
    normed, root = norm_parts(x_ref[...])
    grad = ln_acc[...]
    dx = mg_ref[...] + norm_back(grad * par_ref[0:1, :], normed, root)
    dx_ref[...] = dx[0:seq, :]
    small_ref[0:1, :] = jnp.sum(grad * normed, axis=0, keepdims=True)
    small_ref[1:2, :] = jnp.sum(grad, axis=0, keepdims=True)
    width = lay.width
    spare = jnp.zeros((width, SPARE), F32)
    if lay.fast:
        small = small_ref[...].astype(BF)
        order, same = unit_order(width, 8)
        col = lax.broadcasted_iota(jnp.int32, (width, 16), 1)
        spare = jnp.where(col < 6, nt(same, small), nt(order, small))
        spare = jnp.concatenate([spare, jnp.zeros((width, SPARE - 16), F32)], axis=1)
    ln = ln_ref[...]
    sent = []
    for j in range(lay.groups):
        grad = jnp.concatenate([tn(ln, db_ref[j]), spare], axis=1).astype(BF)
        sent += lay.put(grad, stage, outs[2:], out_sems, j, pos)
    for copy in sent:
        copy.wait()


def finish_attention(chunk, pos, sum_ref, ffn_ref, *refs):
    qkv_ref, fc1_ref, proj_ref, vec_ref, qv_ref, fb_ref, spare_ref = refs
    total = sum_ref[...]
    width = fc1_ref.shape[1]
    fc1_ref[...] = ffn_ref[:, 0:width]
    proj_ref[...] = ffn_ref[:, width : width + proj_ref.shape[0]].T
    wide = qkv_ref.shape[2]
    for c in range(3):
        qkv_ref[c, :, :] = total[:, c * wide : (c + 1) * wide]
    spare_ref[...] = total[:, 3 * wide : 3 * wide + SPARE]
    exact = dict(precision=lax.Precision.HIGHEST, preferred_element_type=F32)
    sub, each = vec_ref.shape[1], fb_ref.shape[0]
    rows = spare_ref[pl.ds(pl.multiple_of(pos[1] * sub, sub), sub), :]
    row = lax.broadcasted_iota(jnp.int32, (8, SPARE), 0)
    col = lax.broadcasted_iota(jnp.int32, (8, SPARE), 1)
    one = jnp.where(row == col, 1.0, 0.0)
    vec = lax.dot_general(one, rows, (((1,), (1,)), ((), ())), **exact)
    vec_ref[...] = vec[0 : vec_ref.shape[0]]
    lane = lax.broadcasted_iota(jnp.int32, (chunk, SPARE), 1)
    spare = spare_ref[...]

    def column(c):
        return jnp.sum(jnp.where(lane == c + pos[1], spare, 0.0), axis=1, keepdims=True)

    def spread(shape, dim, other, by_unit):
        at = lax.broadcasted_iota(jnp.int32, shape, dim)
        at = lax.rem(at, each) if by_unit else at // each
        return at == lax.broadcasted_iota(jnp.int32, shape, other)

    left = jnp.where(spread((8, chunk), 1, 0, True), 1.0, 0.0)
    right = jnp.where(spread((chunk, 16), 0, 1, False), column(6), 0.0)
    fb_ref[...] = jnp.dot(left, right, **exact)[0:each, 0 : fb_ref.shape[1]]
    left = jnp.where(spread((16, chunk), 1, 0, False), 1.0, 0.0)
    right = jnp.where(spread((chunk, 8), 0, 1, True), column(10), 0.0)
    both = jnp.dot(left, right, **exact)
    heads = qv_ref.shape[0]
    for h in range(heads):
        qv_ref[h, 0:1, :] = both[h : h + 1, 0:each]
        qv_ref[h, 1:2, :] = both[2 * heads + h : 2 * heads + h + 1, 0:each]


def shift(x, by):
    n = lax.axis_size("tensor")
    return lax.ppermute(x, "tensor", [(i, (i + by) % n) for i in range(n)])


def flip(x, bit):
    n = lax.axis_size("dp")
    return lax.ppermute(x, "dp", [(i, i ^ bit) for i in range(n)])


def gather_columns(piece):
    return [piece] + [shift(piece, k) for k in (1, 2, 3)]


def join(a, b):
    return jnp.concatenate([a, b], axis=0)


def gather_near(h):
    return flip(h[0], AXIS_X), flip(h[1], AXIS_Y)


def gather_far(both):
    return flip(both[0], AXIS_Y), flip(both[1], AXIS_X)


def direct_near(h):
    return [flip(h[0], AXIS_X), flip(h[0], AXIS_Y), flip(h[1], AXIS_X), flip(h[1], AXIS_Y)]


def direct_far(near):
    return [flip(near[0], AXIS_Y), flip(near[3], AXIS_X)]


def in_direct_order(h, near, far):
    return [h[0], near[0], near[1], far[0], h[1], near[2], near[3], far[1]]


def flip_cores(blocks):
    return [flip(b, CORE) for b in blocks]


def in_order(near, far, core_near, core_far):
    return [near[0], far[0], near[1], far[1], core_near[0], core_far[0], core_near[1], core_far[1]]


def add(a, b):
    return (a.astype(F32) + b.astype(F32)).astype(BF)


class Scatter:
    def __init__(self, *parts):
        self.parts = parts

    def over_cores(self, at):
        sums = [mine[at].astype(F32) + recv[at].astype(F32) for mine, recv in self.parts]
        return sums[0] if len(sums) == 1 else jnp.concatenate(sums, axis=-1)

    def first(self):
        low, high = (slice(2, 4), slice(0, 2)), (slice(1, 4, 2), slice(2, 4))
        return [self.over_cores(at).astype(BF) for at in (low, high)]

    def send_first(self, values):
        return [flip(values[0], AXIS_Y), flip(values[1], AXIS_X)]

    def second(self, got):
        low, high = (slice(0, 2), slice(0, 2)), (slice(0, 4, 2), slice(2, 4))
        return [add(self.over_cores(at), part) for at, part in zip((low, high), got)]

    def send_second(self, values):
        return [flip(values[0][1], AXIS_X), flip(values[1][1], AXIS_Y)]

    def third(self, values, got):
        low = values[0][0].astype(F32) + got[0].astype(F32)
        high = values[1][0].astype(F32) + got[1].astype(F32)
        return [low[0], low[1].astype(BF), high[0].astype(BF), high[1].astype(BF)]

    def send_third(self, parts):
        return [shift(parts[k], k) for k in (1, 2, 3)]

    def last(self, parts, got):
        total = parts[0]
        for part in got:
            total = total + part.astype(F32)
        return total


def barrier(*groups):
    flat, tree = jax.tree.flatten(groups)
    return jax.tree.unflatten(tree, lax.optimization_barrier(tuple(flat)))


def per_device(
    tokens, cotangent, qkv_weight, qv_bias, proj_weight, vectors, fc1_weight, fc1_bias, fc2_weight
):
    n_dp, groups = lax.axis_size("dp"), lax.axis_size("tensor")
    seq, width = tokens.shape
    chunk, wide = qkv_weight.shape[1], qkv_weight.shape[2]
    heads, each = qv_bias.shape[1], qv_bias.shape[2]
    hd = each * n_dp
    units = fc1_weight.shape[1]
    fast = n_dp == 8 and groups == 4
    lay = Layout(fast, groups, width)
    d, z = lax.axis_index("dp"), lax.axis_index("tensor")
    pos = jnp.stack([d, z]).astype(jnp.int32)
    three = 3 * wide
    rows = -(-seq // 16) * 16
    sds = jax.ShapeDtypeStruct
    nb = lay.n_buffers()
    sems = pltpu.SemaphoreType.DMA((groups, lay.n_blocks()))
    wide_a, wide_b = three + SPARE, -(-(width + wide) // 128) * 128

    def run_attention_forward(bufs, *par):
        return kernel_call(
            functools.partial(attention_forward, lay, seq, hd),
            pos,
            bufs,
            [tokens, *par],
            [
                sds((rows, width), BF),
                sds((groups, rows, three), BF),
                sds((groups * heads, rows, rows), BF),
                sds((groups, rows, wide), BF),
                sds((16, width), F32),
            ],
            [pltpu.VMEM((rows, width), F32), pltpu.VMEM((groups, width, wide_a), BF), sems],
        )

    def run_feed_forward(bufs, att, par):
        return kernel_call(
            functools.partial(feed_forward, lay, seq),
            pos,
            bufs,
            [tokens, att, cotangent, par],
            [
                sds((rows, width), F32),
                sds((rows, width), BF),
                sds((groups, rows, units), BF),
                sds((groups, rows, units), BF),
                *lay.grad_shapes(width),
            ],
            [
                pltpu.VMEM((rows, width), BF),
                pltpu.VMEM((groups, width, wide_b), BF),
                sems,
                *lay.stage_shapes(width),
            ],
            lay.n_grads(),
        )

    def run_feed_backward(bufs, slope, ln2):
        return kernel_call(
            functools.partial(feed_backward, lay, seq),
            pos,
            bufs,
            [slope, ln2, cotangent],
            [sds((rows, width), F32), sds((16, width), F32), *lay.grad_shapes(width)],
            [
                pltpu.VMEM((groups, width, width), BF),
                pltpu.VMEM((groups, width, wide_b), BF),
                pltpu.VMEM((rows, width), BF),
                sems,
                sems,
                *lay.stage_shapes(width),
            ],
            lay.n_grads(),
        )

    def run_mid_backward(bufs, ln2_grad, mid, att, small, par):
        return kernel_call(
            functools.partial(mid_backward, lay, seq),
            pos,
            bufs,
            [ln2_grad, mid, att, cotangent, small, par],
            [
                sds((rows, width), F32),
                sds((groups, rows, wide), BF),
                sds((16, width), F32),
                *lay.grad_shapes(wide_b - width),
            ],
            [
                pltpu.VMEM((groups, width, wide_b - width), BF),
                pltpu.VMEM((rows, width), F32),
                sems,
                *lay.stage_shapes(wide_b - width),
            ],
            lay.n_grads(),
        )

    def run_feed_output(bufs, act, mid, par):
        return kernel_call(
            functools.partial(feed_output, lay, seq),
            pos,
            bufs,
            [act, mid, par],
            [sds((seq, width), BF)],
            [pltpu.VMEM((groups, width, width), BF), pltpu.VMEM((rows, width), F32), sems],
        )[0]

    def run_attention_backward(bufs, ln1, qkv, probs, att, att_grad, mid_grad, small, par):
        return kernel_call(
            functools.partial(attention_backward, lay, seq, hd),
            pos,
            bufs,
            [tokens, ln1, qkv, probs, att, att_grad, mid_grad, small, par],
            [sds((seq, width), F32), sds((16, width), F32), *lay.grad_shapes(wide_a)],
            [
                pltpu.VMEM((rows, width), F32),
                pltpu.VMEM((groups, width, wide_a), BF),
                pltpu.VMEM((rows, three), F32),
                pltpu.VMEM((groups, rows, three), BF),
                pltpu.VMEM((rows, width), F32),
                sems,
                *lay.stage_shapes(wide_a),
            ],
            lay.n_grads(),
        )

    sub = chunk // groups
    if fast:
        vmem = pl.BlockSpec(memory_space=pltpu.VMEM)
        piece_a = pl.pallas_call(
            prepare_qkv,
            out_shape=sds((chunk, wide_a), BF),
            in_specs=[vmem] * 4,
            out_specs=vmem,
            scratch_shapes=[
                pltpu.VMEM((16, chunk), F32),
                pltpu.VMEM((16, 128), F32),
                pltpu.VMEM((16, 128), F32),
            ],
        )(qkv_weight, vectors, qv_bias.transpose(1, 0, 2), fc1_bias.T)
        piece_b = pl.pallas_call(
            prepare_fc1,
            out_shape=sds((chunk, wide_b), BF),
            in_specs=[vmem] * 2,
            out_specs=vmem,
        )(fc1_weight, proj_weight)
        piece_c = fc2_weight.T
        z_a = gather_columns(piece_a)
        z_a, piece_b, pos = barrier(z_a, piece_b, pos)
        h_a = barrier(join(*z_a[0:2]), join(*z_a[2:4]))
        near_a = gather_near(h_a)
        z_b = [piece_b, shift(piece_b, 1)]
        near_a, z_b = barrier(near_a, z_b)
        both_a = barrier(join(h_a[0], near_a[0]), join(h_a[1], near_a[1]))
        far_a = gather_far(both_a)
        z_b = [*z_b, shift(z_b[0], 2), shift(z_b[0], 3)]
        h_b = join(*z_b[0:2])
        far_a, z_b, both_a, h_b = barrier(far_a, z_b, both_a, h_b)
        h_b = h_b, join(*z_b[2:4])
        near_b = gather_near(h_b)
        bufs_a = in_order(both_a, far_a, flip_cores(both_a), flip_cores(far_a))
        ln1, qkv, probs, att, par = run_attention_forward(bufs_a)

        near_b, att = barrier(near_b, att)
        both_b = barrier(join(h_b[0], near_b[0]), join(h_b[1], near_b[1]))
        far_b = gather_far(both_b)
        core_b = flip_cores(both_b)
        core_b, piece_c = barrier(core_b, piece_c)
        z_c = gather_columns(piece_c)
        far_b, z_c = barrier(far_b, z_c)
        core_b = core_b + flip_cores(far_b)
        h_c = join(*z_c[0:2]), join(*z_c[2:4])
        near_c = direct_near(h_c)
        bufs_b = in_order(both_b, far_b, core_b[0:2], core_b[2:4])
        mid, ln2, act, slope, *grads_c = run_feed_forward(bufs_b, att, par)
        near_c, grads_c, slope = barrier(near_c, grads_c, slope)
        far_c = direct_far(near_c)
        recv_c, near_c, h_c = barrier(flip(grads_c[1], CORE), near_c, h_c)
        way_c = Scatter((grads_c[0], recv_c))
        first_c = way_c.first()
        first_c, near_c, h_c = barrier(first_c, near_c, h_c)
        core_c = flip_cores([*h_c, *near_c])
        first_c, far_c, core_c, slope = barrier(first_c, far_c, core_c, slope)
        bufs_c = [
            *in_direct_order(h_c, near_c, far_c),
            *in_direct_order(core_c[0:2], core_c[2:6], flip_cores(far_c)),
        ]
        got_c = way_c.send_first(first_c)
        ln2_grad, small, *grads_b = run_feed_backward([*bufs_b, *bufs_c], slope, ln2)
        got_c, grads_b, ln2_grad = barrier(got_c, grads_b, ln2_grad)

        recv_b = flip(grads_b[1], CORE)
        second_c = way_c.second(got_c)
        second_c, ln2_grad = barrier(second_c, ln2_grad)
        got_c = way_c.send_second(second_c)
        mid_grad, att_grad, small, *grads_p = run_mid_backward(
            bufs_b, ln2_grad, mid, att, small, par
        )
        got_c, recv_b, grads_p, mid_grad = barrier(got_c, recv_b, grads_p, mid_grad)

        recv_p = flip(grads_p[1], CORE)
        way_b = Scatter((grads_b[0], recv_b), (grads_p[0], recv_p))
        first_b = way_b.first()
        third_c = way_c.third(second_c, got_c)
        first_b, mid_grad, third_c = barrier(first_b, mid_grad, third_c)
        got_b = way_b.send_first(first_b)
        got_c = [shift(third_c[k], k) for k in (1, 3)]
        input_grad, small, *grads_a = run_attention_backward(
            bufs_a, ln1, qkv, probs, att, att_grad, mid_grad, small, par
        )
        got_b, got_c, third_c, grads_a = barrier(got_b, got_c, third_c, grads_a)

        recv_a = flip(grads_a[1], CORE)
        second_b = way_b.second(got_b)
        second_b, third_c = barrier(second_b, third_c)
        got_b = way_b.send_second(second_b)
        got_c = [*got_c, shift(third_c[2], 2)]
        way_a = Scatter((grads_a[0], recv_a))
        first_a = way_a.first()
        first_a, got_b, got_c, act = barrier(first_a, got_b, got_c, act)
        got_a = way_a.send_first(first_a)
        third_b = way_b.third(second_b, got_b)
        third_b, act = barrier(third_b, act)
        half_b = wide_b // 2
        got_b = [shift(third_b[k], k) for k in (1, 3)] + [shift(third_b[2][:, :half_b], 2)]
        output = run_feed_output(bufs_c, act, mid, par)
        sum_c = way_c.last(third_c, got_c)
        got_a, output, sum_c, got_b, third_b = barrier(got_a, output, sum_c, got_b, third_b)
        second_a = way_a.second(got_a)
        second_a, third_b = barrier(second_a, third_b)
        got_a = way_a.send_second(second_a)
        rest_b = shift(third_b[2][:, half_b:], 2)
        got_b = [*got_b[0:2], jnp.concatenate([got_b[2], rest_b], axis=1)]
        got_a, got_b = barrier(got_a, got_b)
        third_a = way_a.third(second_a, got_a)[1:]
        third_a, second_a, step_a = barrier(third_a, second_a, got_a)
        got_a = [shift(third_a[k - 1], k) for k in (1, 2, 3)]
        got_a[0], second_a, step_a, got_b = barrier(got_a[0], second_a, step_a, got_b)
        own_a = second_a[0][0, 0].astype(F32) + step_a[0][0].astype(F32)
        sum_b = way_b.last(third_b, got_b)
        sum_b, got_a, own_a = barrier(sum_b, got_a, own_a)
        sum_a = way_a.last([own_a], got_a)
        vmem = pl.BlockSpec(memory_space=pltpu.VMEM)
        qkv_grad, sum_b, proj_grad, vec_grad, qv_grad, fc1b_grad = pl.pallas_call(
            functools.partial(finish_attention, chunk),
            out_shape=[
                sds((3, chunk, wide), F32),
                sds((chunk, width), F32),
                sds((wide, chunk), F32),
                sds((6, sub), F32),
                sds((heads, 2, each), F32),
                sds((each, units // hd), F32),
            ],
            in_specs=[pl.BlockSpec(memory_space=pltpu.SMEM)] + [vmem] * 2,
            out_specs=[vmem] * 6,
            scratch_shapes=[pltpu.VMEM((chunk, SPARE), F32)],
        )(pos, sum_a, sum_b)
        qv_grad, fc1b_grad = qv_grad.transpose(1, 0, 2), fc1b_grad.T
    else:
        none = jnp.zeros_like(qv_bias[0])
        qkv_col = jnp.stack([qv_bias[0], none, qv_bias[1], none]).reshape(chunk)
        spare = jnp.concatenate([vectors, fc1_bias.reshape(1, chunk), qkv_col[None]], axis=0).T
        spare = jnp.pad(spare, ((0, 0), (0, SPARE - spare.shape[1])))
        piece_a = jnp.concatenate([qkv_weight[0], qkv_weight[1], qkv_weight[2], spare], axis=1)
        piece_b = jnp.concatenate([fc1_weight, proj_weight.T], axis=1)
        piece_b = jnp.pad(piece_b, ((0, 0), (0, wide_b - width - wide)))

        def gather(p):
            return [lax.all_gather(lax.all_gather(p, "dp", axis=0, tiled=True), "tensor", axis=0)]

        bufs_a, bufs_b, bufs_c = gather(piece_a), gather(piece_b), gather(fc2_weight.T)
        cols = bufs_a[0][:, :, three : three + 8]
        vec = cols[0, :, 0:6].T
        by_unit = cols.reshape(groups, n_dp, chunk // each, each, 8).transpose(0, 4, 2, 1, 3)
        by_unit = by_unit.reshape(groups, 8, width)
        par = jnp.concatenate([vec, by_unit[:, 6], by_unit[:, 7]], axis=0).astype(F32)
        par = jnp.pad(par, ((0, 16 - par.shape[0]), (0, 0)))
        ln1, qkv, probs, att, par = run_attention_forward(bufs_a, par)
        mid, ln2, act, slope, grads_c = run_feed_forward(bufs_b, att, par)
        ln2_grad, small, grads_b = run_feed_backward([*bufs_b, *bufs_c], slope, ln2)
        mid_grad, att_grad, small, grads_p = run_mid_backward(
            bufs_b, ln2_grad, mid, att, small, par
        )
        output = run_feed_output(bufs_c, act, mid, par)
        input_grad, small, grads_a = run_attention_backward(
            bufs_a, ln1, qkv, probs, att, att_grad, mid_grad, small, par
        )

        def scatter(g):
            g = lax.psum_scatter(g, "tensor", scatter_dimension=0, tiled=False)
            return lax.psum_scatter(g, "dp", scatter_dimension=0, tiled=True).astype(F32)

        sum_c, sum_b, sum_a = scatter(grads_c), scatter(grads_b), scatter(grads_a)
        sum_p = lax.optimization_barrier(scatter(grads_p))
        small = lax.psum(small, ("dp", "tensor"))
        vec_grad = lax.dynamic_slice(small, (0, d * chunk + z * sub), (6, sub))
        by_unit = small[6:14].reshape(2, groups, chunk // each, hd)
        by_unit = lax.dynamic_slice(
            by_unit, (0, z, 0, d * each), (2, 1, chunk // each, each)
        ).reshape(2, chunk)
        fc1b_grad, qv_grad = by_unit[0], by_unit[1]
        fc1b_grad = fc1b_grad.reshape(fc1_bias.shape)
        qv_grad = qv_grad.reshape(4, heads, each)[0::2]
        qkv_grad = jnp.stack([sum_a[:, c * wide : (c + 1) * wide] for c in range(3)])
        proj_grad = sum_p[:, :wide].T
    return (
        output,
        input_grad,
        qkv_grad,
        qv_grad,
        proj_grad,
        vec_grad,
        sum_b,
        fc1b_grad,
        sum_c.T,
    )


def solution(mesh):
    return jax.shard_map(
        per_device,
        mesh=mesh,
        in_specs=(
            P(("dp", "tensor"), None),
            P(("dp", "tensor"), None),
            P(None, "dp", "tensor"),
            P(None, "tensor", "dp"),
            P("tensor", "dp"),
            P(None, "dp"),
            P("dp", "tensor"),
            P("tensor", "dp"),
            P("tensor", "dp"),
        ),
        out_specs=(
            P(("dp", "tensor"), None),
            P(("dp", "tensor"), None),
            P(None, "dp", "tensor"),
            P(None, "tensor", "dp"),
            P("tensor", "dp"),
            P(None, ("dp", "tensor")),
            P("dp", "tensor"),
            P("tensor", "dp"),
            P("tensor", "dp"),
        ),
        check_vma=False,
    )
```

```python
import functools

import jax
import jax.numpy as jnp
from jax import lax
from jax.experimental import pallas as pl
from jax.experimental.pallas import tpu as pltpu
from jax.sharding import PartitionSpec as P

BF = jnp.bfloat16
F32 = jnp.float32
norm_eps = 1e-06
half_root = 0.7071067811865476
density_scale = 0.3989422804014327
VMEM_LIMIT = 56 * 1024 * 1024


def nn(a, b):
    return jnp.dot(a, b, preferred_element_type=F32)


def nt(a, b):
    return lax.dot_general(a, b, (((1,), (1,)), ((), ())), preferred_element_type=F32)


def tn(a, b):
    return lax.dot_general(a, b, (((0,), (0,)), ((), ())), preferred_element_type=F32)


def norm_parts(values):
    centred = values - jnp.mean(values, axis=-1, keepdims=True)
    recip_root = lax.rsqrt(jnp.mean(centred * centred, axis=-1, keepdims=True) + norm_eps)
    return centred * recip_root, recip_root


def norm_back(upstream, normed, recip_root):
    first_mean = jnp.mean(upstream, axis=-1, keepdims=True)
    second_mean = jnp.mean(upstream * normed, axis=-1, keepdims=True)
    return recip_root * (upstream - first_mean - normed * second_mean)


def gelu_parts(values):
    cumul = 0.5 * (1.0 + lax.erf(values * half_root))
    return (values * cumul, cumul + values * jnp.exp(-0.5 * values * values) * density_scale)


class Layout:
    def __init__(self, fast, groups, width):
        self.fast, self.groups, self.width = fast, groups, width
        self.chunk = width // 8 if fast else width

    def t(self, j, pos):
        return lax.rem(pos[1] + (self.groups - j), self.groups) if self.fast else j

    def out(self, j):
        return (self.groups - j) % self.groups if self.fast else j

    def rows(self, k, pos):
        if not self.fast:
            return pl.ds(0, self.width)
        return pl.ds(pl.multiple_of((pos[0] ^ k) * self.chunk, self.chunk), self.chunk)

    def n_buffers(self):
        return 8 if self.fast else 1

    def n_direct(self):
        return 16 if self.fast else 1

    def n_blocks(self):
        return 8 if self.fast else 1

    def sources(self, bufs, j, direct):
        if not self.fast:
            return [(bufs[0].at[j], 0)]
        found = []
        if direct:
            at = pl.ds((j % 2) * self.chunk, self.chunk)
            for core in range(2):
                for n, k in enumerate((0, AXIS_X, AXIS_Y, AXIS_X | AXIS_Y)):
                    found.append((bufs[8 * core + 4 * (j // 2) + n].at[at, :], k ^ core))
            return found
        first, second = (AXIS_X, AXIS_Y) if j < 2 else (AXIS_Y, AXIS_X)
        for core in range(2):
            near, far = bufs[4 * core + 2 * (j // 2) :][:2]
            for ref, axis in ((near, 0), (far, second)):
                for n in range(2):
                    at = pl.ds((2 * n + j % 2) * self.chunk, self.chunk)
                    found.append((ref.at[at, :], axis ^ (first * n) ^ core))
        return found

    def fetch(self, bufs, dest, sems, pos, direct=False, ahead=2):
        def begin(j):
            found = []
            for n, (src, k) in enumerate(self.sources(bufs, j, direct)):
                copy = pltpu.make_async_copy(src, dest.at[j, self.rows(k, pos), :], sems.at[j, n])
                copy.start()
                found.append(copy)
            return found

        copies = [begin(j) for j in range(min(ahead, self.groups))]

        def use(j):
            for copy in copies[j]:
                copy.wait()
            if j + ahead < self.groups:
                copies.append(begin(j + ahead))

        return use

    def put(self, grad, stage, outs, sems, j, pos):
        at = self.out(j)
        if not self.fast:
            stage[at, :, :] = grad
            copies = [pltpu.make_async_copy(stage.at[at], outs[0].at[at], sems.at[j, 0])]
        else:
            for r in range(8):
                other = pos[0] ^ r
                stage[other & 1, other >> 1, at, :, :] = grad[r * self.chunk : (r + 1) * self.chunk]
            copies = [
                pltpu.make_async_copy(stage.at[n, :, at], outs[n].at[:, at], sems.at[j, n])
                for n in range(2)
            ]
        for copy in copies:
            copy.start()
        return copies

    def stage_shapes(self, wide):
        shape = (2, 4, self.groups, self.chunk, wide) if self.fast else (self.groups, self.width, wide)
        return [pltpu.VMEM(shape, BF), pltpu.SemaphoreType.DMA((self.groups, 2))]

    def n_grads(self):
        return 2 if self.fast else 1

    def grad_shapes(self, wide):
        if not self.fast:
            return [jax.ShapeDtypeStruct((self.groups, self.width, wide), BF)]
        return [jax.ShapeDtypeStruct((4, self.groups, self.chunk, wide), BF)] * 2


SPARE = 64
CORE, AXIS_X, AXIS_Y = 1, 2, 4


def unit_order(width, n):
    i = lax.broadcasted_iota(jnp.int32, (width, width), 0)
    c = lax.broadcasted_iota(jnp.int32, (width, width), 1)
    per = width // n
    hit = i == (lax.rem(c, 64) // 8) * per + (c // 64) * 8 + lax.rem(c, 8)
    same = i == c
    return jnp.where(hit, 1.0, 0.0).astype(BF), jnp.where(same, 1.0, 0.0).astype(BF)


def kernel_call(body, pos, bufs, ins, outs, scratch, n_any=0):
    in_hbm = pl.BlockSpec(memory_space=pl.ANY)
    vmem, smem = pl.BlockSpec(memory_space=pltpu.VMEM), pl.BlockSpec(memory_space=pltpu.SMEM)
    return pl.pallas_call(
        body,
        out_shape=outs,
        in_specs=[smem] + [in_hbm] * len(bufs) + [vmem] * len(ins),
        out_specs=[vmem] * (len(outs) - n_any) + [in_hbm] * n_any,
        scratch_shapes=scratch,
        compiler_params=pltpu.CompilerParams(vmem_limit_bytes=VMEM_LIMIT),
        cost_estimate=pl.CostEstimate(flops=0, bytes_accessed=0, transcendentals=0),
    )(pos, *bufs, *ins)


def split_refs(refs, n_bufs, n_in, n_out):
    bufs, refs = refs[:n_bufs], refs[n_bufs:]
    return bufs, refs[:n_in], refs[n_in : n_in + n_out], refs[n_in + n_out :]


def prepare_qkv(qkv_ref, vec_ref, qv_ref, fb_ref, out_ref, rows_ref, fb_pad, qv_pad):
    wide, chunk = qkv_ref.shape[2], qkv_ref.shape[1]
    heads, each = qv_ref.shape[0], qv_ref.shape[2]
    for c in range(3):
        out_ref[:, c * wide : (c + 1) * wide] = qkv_ref[c]
    for ref in (rows_ref, fb_pad, qv_pad):
        ref[...] = jnp.zeros_like(ref)
    rows_ref[0 : vec_ref.shape[0], :] = vec_ref[...].astype(F32)
    fb_pad[0:each, 0 : fb_ref.shape[1]] = fb_ref[...].astype(F32)
    for h in range(heads):
        both = qv_ref[h].astype(F32)
        qv_pad[h : h + 1, 0:each] = both[0:1]
        qv_pad[2 * heads + h : 2 * heads + h + 1, 0:each] = both[1:2]
    row = lax.broadcasted_iota(jnp.int32, (16, SPARE), 0)
    col = lax.broadcasted_iota(jnp.int32, (16, SPARE), 1)
    spare = tn(rows_ref[...].astype(BF), jnp.where(row == col, 1.0, 0.0).astype(BF))
    at = lax.broadcasted_iota(jnp.int32, (chunk, 16), 0)
    slot = lax.broadcasted_iota(jnp.int32, (chunk, 16), 1)
    by_group = jnp.where(at // each == slot, 1.0, 0.0).astype(BF)
    by_unit = jnp.where(lax.rem(at, each) == slot, 1.0, 0.0).astype(BF)
    at = lax.broadcasted_iota(jnp.int32, (chunk, 128), 0)
    lane = lax.broadcasted_iota(jnp.int32, (chunk, 128), 1)
    out_col = lax.broadcasted_iota(jnp.int32, (chunk, SPARE), 1)
    fb = jnp.where(lane == at // each, nn(by_unit, fb_pad[...].astype(BF)), 0.0)
    qv = jnp.where(lane == lax.rem(at, each), nn(by_group, qv_pad[...].astype(BF)), 0.0)
    for c, spread in ((6, fb), (7, qv)):
        spare += jnp.where(out_col == c, jnp.sum(spread, axis=1, keepdims=True), 0.0)
    out_ref[:, 3 * wide : 3 * wide + SPARE] = spare.astype(BF)


def prepare_fc1(fc1_ref, proj_ref, out_ref):
    width, wide = fc1_ref.shape[1], proj_ref.shape[0]
    out_ref[:, 0:width] = fc1_ref[...]
    row = lax.broadcasted_iota(jnp.int32, (wide, wide), 0)
    col = lax.broadcasted_iota(jnp.int32, (wide, wide), 1)
    one = jnp.where(row == col, 1.0, 0.0).astype(BF)
    out_ref[:, width:] = jnp.zeros_like(out_ref[:, width:])
    out_ref[:, width : width + wide] = tn(proj_ref[...], one).astype(BF)


def pad_rows(dest, source, seq):
    dest[...] = jnp.zeros_like(dest)
    dest[0:seq, :] = source[...].astype(dest.dtype)


def attention_forward(lay, seq, hd, pos, *refs):
    bufs, ins, outs, scratch = split_refs(refs, lay.n_buffers(), 1 if lay.fast else 2, 5)
    tok_ref = ins[0]
    ln_ref, qkv_ref, probs_ref, att_ref, par_ref = outs
    x_ref, w_ref, sems = scratch
    use = lay.fetch(bufs, w_ref, sems, pos, ahead=lay.groups)
    pad_rows(x_ref, tok_ref, seq)
    rows = x_ref.shape[0]
    wide = att_ref.shape[2]
    heads = wide // hd
    normed, _ = norm_parts(x_ref[...])
    if lay.fast:
        width = lay.width
        order, _ = unit_order(width, 8)
        row = lax.broadcasted_iota(jnp.int32, (16, SPARE), 0)
        col = lax.broadcasted_iota(jnp.int32, (16, SPARE), 1)
        par = jnp.zeros((16, width), F32)
        units = jnp.zeros((16, width), F32)
        for j in range(lay.groups):
            use(j)
            spare = w_ref[j, :, 3 * wide : 3 * wide + SPARE]
            t = lay.t(j, pos)
            if j == 0:
                par = nt(jnp.where((row == col) & (row < 6), 1.0, 0.0).astype(BF), spare)
            pick = ((row == 6 + t) & (col == 6)) | ((row == 10 + t) & (col == 7))
            units += nt(jnp.where(pick, 1.0, 0.0).astype(BF), spare)
        par_ref[...] = par + nn(units.astype(BF), order)
    else:
        for j in range(lay.groups):
            use(j)
        par_ref[...] = ins[1][...]
    ln = (normed * par_ref[0:1, :] + par_ref[1:2, :]).astype(BF)
    ln_ref[...] = ln
    valid = lax.broadcasted_iota(jnp.int32, (rows, rows), 1) < seq
    for j in range(lay.groups):
        bias = par_ref[pl.ds(10 + lay.t(j, pos), 1), 0 : 3 * wide]
        qkv_ref[j, :, :] = (nn(ln, w_ref[j, :, 0 : 3 * wide]) + bias).astype(BF)
        for h in range(heads):
            q = qkv_ref[j, :, h * hd : (h + 1) * hd]
            k = qkv_ref[j, :, wide + h * hd : wide + (h + 1) * hd]
            v = qkv_ref[j, :, 2 * wide + h * hd : 2 * wide + (h + 1) * hd]
            scores = jnp.where(valid, nt(q, k) * (hd**-0.5), -1e30)
            top = jnp.max(scores, axis=-1, keepdims=True)
            e = jnp.exp(scores - top)
            p = (e * (1.0 / jnp.sum(e, axis=-1, keepdims=True))).astype(BF)
            probs_ref[j * heads + h, :, :] = p
            att_ref[j, :, h * hd : (h + 1) * hd] = nn(p, v).astype(BF)


def feed_forward(lay, seq, pos, *refs):
    bufs, ins, outs, scratch = split_refs(refs, lay.n_buffers(), 4, 4 + lay.n_grads())
    tok_ref, att_ref, cot_ref, par_ref = ins
    mid_ref, ln_ref, act_ref, slope_ref = outs[:4]
    cotp_ref, w_ref, sems, stage, out_sems = scratch
    use = lay.fetch(bufs, w_ref, sems, pos, ahead=lay.groups)
    pad_rows(cotp_ref, cot_ref, seq)
    pad_rows(mid_ref, tok_ref, seq)
    width, wide = lay.width, att_ref.shape[2]
    mid = mid_ref[...] + par_ref[2:3, :]
    for j in range(lay.groups):
        use(j)
        mid += nt(att_ref[j], w_ref[j, :, width : width + wide])
    mid_ref[...] = mid
    normed, _ = norm_parts(mid)
    ln = (normed * par_ref[3:4, :] + par_ref[4:5, :]).astype(BF)
    ln_ref[...] = ln
    sent = []
    for j in range(lay.groups):
        bias = par_ref[pl.ds(6 + lay.t(j, pos), 1), :]
        act, slope = gelu_parts(nn(ln, w_ref[j, :, 0:width]) + bias)
        act_ref[j, :, :] = act.astype(BF)
        slope_ref[j, :, :] = slope.astype(BF)
        grad = tn(cotp_ref[...], act_ref[j]).astype(BF)
        sent += lay.put(grad, stage, outs[4:], out_sems, j, pos)
    for copy in sent:
        copy.wait()


def feed_backward(lay, seq, pos, *refs):
    nb = lay.n_buffers()
    bufs, ins, outs, scratch = split_refs(refs, nb + lay.n_direct(), 3, 2 + lay.n_grads())
    slope_ref, ln_ref, cot_ref = ins
    lg_ref, small_ref = outs[:2]
    w2_ref, w1_ref, cotp_ref, sems2, sems1, stage, out_sems = scratch
    use2 = lay.fetch(bufs[nb:], w2_ref, sems2, pos, True)
    use1 = lay.fetch(bufs[:nb], w1_ref, sems1, pos)
    pad_rows(cotp_ref, cot_ref, seq)
    cot = cotp_ref[...]
    ln = ln_ref[...]
    small_ref[...] = jnp.zeros_like(small_ref)
    sent = []
    for j in range(lay.groups):
        use2(j)
        pre_grad = nn(cot, w2_ref[j]) * slope_ref[j].astype(F32)
        small_ref[pl.ds(6 + lay.t(j, pos), 1), :] = jnp.sum(pre_grad, axis=0, keepdims=True)
        pgb = pre_grad.astype(BF)
        sent += lay.put(tn(ln, pgb).astype(BF), stage, outs[2:], out_sems, j, pos)
        use1(j)
        part = nt(pgb, w1_ref[j, :, 0 : lay.width])
        if j == 0:
            lg_ref[...] = part
        else:
            lg_ref[...] += part
    for copy in sent:
        copy.wait()


def mid_backward(lay, seq, pos, *refs):
    bufs, ins, outs, scratch = split_refs(refs, lay.n_buffers(), 6, 3 + lay.n_grads())
    lg_ref, mid_ref, att_ref, cot_ref, small_in, par_ref = ins
    mg_ref, ag_ref, small_ref = outs[:3]
    w_ref, cotp_ref, sems, stage, out_sems = scratch
    width, wide = lay.width, ag_ref.shape[2]
    bufs = [buf.at[:, width:] if lay.fast else buf.at[:, :, width:] for buf in bufs]
    use = lay.fetch(bufs, w_ref, sems, pos)
    pad_rows(cotp_ref, cot_ref, seq)
    normed, root = norm_parts(mid_ref[...])
    grad = lg_ref[...]
    cot = cotp_ref[...]
    mid_grad = cot + norm_back(grad * par_ref[3:4, :], normed, root)
    mg_ref[...] = mid_grad
    mgb = mid_grad.astype(BF)
    pad = jnp.zeros((width, outs[3].shape[-1] - wide), F32)
    sent = []
    for j in range(lay.groups):
        proj = jnp.concatenate([tn(mgb, att_ref[j]), pad], axis=1)
        sent += lay.put(proj.astype(BF), stage, outs[3:], out_sems, j, pos)
    small_ref[...] = small_in[...]
    small_ref[2:3, :] = jnp.sum(mid_grad, axis=0, keepdims=True)
    small_ref[3:4, :] = jnp.sum(grad * normed, axis=0, keepdims=True)
    small_ref[4:5, :] = jnp.sum(grad, axis=0, keepdims=True)
    small_ref[5:6, :] = jnp.sum(cot, axis=0, keepdims=True)
    for j in range(lay.groups):
        use(j)
        ag_ref[j, :, :] = nn(mgb, w_ref[j, :, 0:wide]).astype(BF)
    for copy in sent:
        copy.wait()


def feed_output(lay, seq, pos, *refs):
    bufs, ins, (out_ref,), (w_ref, acc, sems) = split_refs(refs, lay.n_direct(), 3, 1)
    act_ref, mid_ref, par_ref = ins
    use = lay.fetch(bufs, w_ref, sems, pos, True)
    acc[...] = mid_ref[...] + par_ref[5:6, :]
    for j in range(lay.groups):
        use(j)
        acc[...] += nt(act_ref[j], w_ref[j])
    out_ref[...] = acc[0:seq, :].astype(BF)


def attention_backward(lay, seq, hd, pos, *refs):
    bufs, ins, outs, scratch = split_refs(refs, lay.n_buffers(), 9, 2 + lay.n_grads())
    tok_ref, ln_ref, qkv_ref, probs_ref, att_ref, ag_ref, mg_ref, small_in, par_ref = ins
    dx_ref, small_ref = outs[:2]
    x_ref, w_ref, dqkv_ref, db_ref, ln_acc, sems, stage, out_sems = scratch
    use = lay.fetch(bufs, w_ref, sems, pos)
    wide = att_ref.shape[2]
    heads = wide // hd
    scale = hd**-0.5
    small_ref[...] = small_in[...]
    pad_rows(x_ref, tok_ref, seq)
    ln_acc[...] = jnp.zeros_like(ln_acc)
    three = slice(0, 3 * wide)
    for j in range(lay.groups):
        use(j)
        att_grad = ag_ref[j]
        prod = att_grad.astype(F32) * att_ref[j].astype(F32)
        for h in range(heads):
            at = slice(h * hd, (h + 1) * hd)
            q = qkv_ref[j, :, h * hd : (h + 1) * hd]
            k = qkv_ref[j, :, wide + h * hd : wide + (h + 1) * hd]
            v = qkv_ref[j, :, 2 * wide + h * hd : 2 * wide + (h + 1) * hd]
            p = probs_ref[j * heads + h]
            da = att_grad[:, at]
            delta = jnp.sum(prod[:, at], axis=-1, keepdims=True)
            ds = (p.astype(F32) * (nt(da, v) - delta) * scale).astype(BF)
            dqkv_ref[:, h * hd : (h + 1) * hd] = nn(ds, k)
            dqkv_ref[:, wide + h * hd : wide + (h + 1) * hd] = tn(ds, q)
            dqkv_ref[:, 2 * wide + h * hd : 2 * wide + (h + 1) * hd] = tn(p, da)
        dqkv = dqkv_ref[...]
        small_ref[pl.ds(10 + lay.t(j, pos), 1), three] = jnp.sum(dqkv, axis=0, keepdims=True)
        dqkv = dqkv.astype(BF)
        db_ref[j, :, :] = dqkv
        ln_acc[...] += nt(dqkv, w_ref[j, :, three])
    normed, root = norm_parts(x_ref[...])
    grad = ln_acc[...]
    dx = mg_ref[...] + norm_back(grad * par_ref[0:1, :], normed, root)
    dx_ref[...] = dx[0:seq, :]
    small_ref[0:1, :] = jnp.sum(grad * normed, axis=0, keepdims=True)
    small_ref[1:2, :] = jnp.sum(grad, axis=0, keepdims=True)
    width = lay.width
    spare = jnp.zeros((width, SPARE), F32)
    if lay.fast:
        small = small_ref[...].astype(BF)
        order, same = unit_order(width, 8)
        col = lax.broadcasted_iota(jnp.int32, (width, 16), 1)
        spare = jnp.where(col < 6, nt(same, small), nt(order, small))
        spare = jnp.concatenate([spare, jnp.zeros((width, SPARE - 16), F32)], axis=1)
    ln = ln_ref[...]
    sent = []
    for j in range(lay.groups):
        grad = jnp.concatenate([tn(ln, db_ref[j]), spare], axis=1).astype(BF)
        sent += lay.put(grad, stage, outs[2:], out_sems, j, pos)
    for copy in sent:
        copy.wait()


def finish_attention(chunk, pos, sum_ref, ffn_ref, *refs):
    qkv_ref, fc1_ref, proj_ref, vec_ref, qv_ref, fb_ref, spare_ref = refs
    total = sum_ref[...]
    width = fc1_ref.shape[1]
    fc1_ref[...] = ffn_ref[:, 0:width]
    proj_ref[...] = ffn_ref[:, width : width + proj_ref.shape[0]].T
    wide = qkv_ref.shape[2]
    for c in range(3):
        qkv_ref[c, :, :] = total[:, c * wide : (c + 1) * wide]
    spare_ref[...] = total[:, 3 * wide : 3 * wide + SPARE]
    exact = dict(precision=lax.Precision.HIGHEST, preferred_element_type=F32)
    sub, each = vec_ref.shape[1], fb_ref.shape[0]
    rows = spare_ref[pl.ds(pl.multiple_of(pos[1] * sub, sub), sub), :]
    row = lax.broadcasted_iota(jnp.int32, (8, SPARE), 0)
    col = lax.broadcasted_iota(jnp.int32, (8, SPARE), 1)
    one = jnp.where(row == col, 1.0, 0.0)
    vec = lax.dot_general(one, rows, (((1,), (1,)), ((), ())), **exact)
    vec_ref[...] = vec[0 : vec_ref.shape[0]]
    lane = lax.broadcasted_iota(jnp.int32, (chunk, SPARE), 1)
    spare = spare_ref[...]

    def column(c):
        return jnp.sum(jnp.where(lane == c + pos[1], spare, 0.0), axis=1, keepdims=True)

    def spread(shape, dim, other, by_unit):
        at = lax.broadcasted_iota(jnp.int32, shape, dim)
        at = lax.rem(at, each) if by_unit else at // each
        return at == lax.broadcasted_iota(jnp.int32, shape, other)

    left = jnp.where(spread((8, chunk), 1, 0, True), 1.0, 0.0)
    right = jnp.where(spread((chunk, 16), 0, 1, False), column(6), 0.0)
    fb_ref[...] = jnp.dot(left, right, **exact)[0:each, 0 : fb_ref.shape[1]]
    left = jnp.where(spread((16, chunk), 1, 0, False), 1.0, 0.0)
    right = jnp.where(spread((chunk, 8), 0, 1, True), column(10), 0.0)
    both = jnp.dot(left, right, **exact)
    heads = qv_ref.shape[0]
    for h in range(heads):
        qv_ref[h, 0:1, :] = both[h : h + 1, 0:each]
        qv_ref[h, 1:2, :] = both[2 * heads + h : 2 * heads + h + 1, 0:each]


def shift(x, by):
    n = lax.axis_size("tensor")
    return lax.ppermute(x, "tensor", [(i, (i + by) % n) for i in range(n)])


def flip(x, bit):
    n = lax.axis_size("dp")
    return lax.ppermute(x, "dp", [(i, i ^ bit) for i in range(n)])


def gather_columns(piece):
    return [piece] + [shift(piece, k) for k in (1, 2, 3)]


def join(a, b):
    return jnp.concatenate([a, b], axis=0)


def gather_near(h):
    return flip(h[0], AXIS_X), flip(h[1], AXIS_Y)


def gather_far(both):
    return flip(both[0], AXIS_Y), flip(both[1], AXIS_X)


def direct_near(h):
    return [flip(h[0], AXIS_X), flip(h[0], AXIS_Y), flip(h[1], AXIS_X), flip(h[1], AXIS_Y)]


def direct_far(near):
    return [flip(near[0], AXIS_Y), flip(near[3], AXIS_X)]


def in_direct_order(h, near, far):
    return [h[0], near[0], near[1], far[0], h[1], near[2], near[3], far[1]]


def flip_cores(blocks):
    return [flip(b, CORE) for b in blocks]


def in_order(near, far, core_near, core_far):
    return [near[0], far[0], near[1], far[1], core_near[0], core_far[0], core_near[1], core_far[1]]


def add(a, b):
    return (a.astype(F32) + b.astype(F32)).astype(BF)


class Scatter:
    def __init__(self, *parts):
        self.parts = parts

    def over_cores(self, at):
        sums = [mine[at].astype(F32) + recv[at].astype(F32) for mine, recv in self.parts]
        return sums[0] if len(sums) == 1 else jnp.concatenate(sums, axis=-1)

    def first(self):
        low, high = (slice(2, 4), slice(0, 2)), (slice(1, 4, 2), slice(2, 4))
        return [self.over_cores(at).astype(BF) for at in (low, high)]

    def send_first(self, values):
        return [flip(values[0], AXIS_Y), flip(values[1], AXIS_X)]

    def second(self, got):
        low, high = (slice(0, 2), slice(0, 2)), (slice(0, 4, 2), slice(2, 4))
        return [add(self.over_cores(at), part) for at, part in zip((low, high), got)]

    def send_second(self, values):
        return [flip(values[0][1], AXIS_X), flip(values[1][1], AXIS_Y)]

    def third(self, values, got):
        low = values[0][0].astype(F32) + got[0].astype(F32)
        high = values[1][0].astype(F32) + got[1].astype(F32)
        return [low[0], low[1].astype(BF), high[0].astype(BF), high[1].astype(BF)]

    def send_third(self, parts):
        return [shift(parts[k], k) for k in (1, 2, 3)]

    def last(self, parts, got):
        total = parts[0]
        for part in got:
            total = total + part.astype(F32)
        return total


def barrier(*groups):
    flat, tree = jax.tree.flatten(groups)
    return jax.tree.unflatten(tree, lax.optimization_barrier(tuple(flat)))


def per_device(
    tokens, cotangent, qkv_weight, qv_bias, proj_weight, vectors, fc1_weight, fc1_bias, fc2_weight
):
    n_dp, groups = lax.axis_size("dp"), lax.axis_size("tensor")
    seq, width = tokens.shape
    chunk, wide = qkv_weight.shape[1], qkv_weight.shape[2]
    heads, each = qv_bias.shape[1], qv_bias.shape[2]
    hd = each * n_dp
    units = fc1_weight.shape[1]
    fast = n_dp == 8 and groups == 4
    lay = Layout(fast, groups, width)
    d, z = lax.axis_index("dp"), lax.axis_index("tensor")
    pos = jnp.stack([d, z]).astype(jnp.int32)
    three = 3 * wide
    rows = -(-seq // 16) * 16
    sds = jax.ShapeDtypeStruct
    nb = lay.n_buffers()
    sems = pltpu.SemaphoreType.DMA((groups, lay.n_blocks()))
    wide_a, wide_b = three + SPARE, -(-(width + wide) // 128) * 128

    def run_attention_forward(bufs, *par):
        return kernel_call(
            functools.partial(attention_forward, lay, seq, hd),
            pos,
            bufs,
            [tokens, *par],
            [
                sds((rows, width), BF),
                sds((groups, rows, three), BF),
                sds((groups * heads, rows, rows), BF),
                sds((groups, rows, wide), BF),
                sds((16, width), F32),
            ],
            [pltpu.VMEM((rows, width), F32), pltpu.VMEM((groups, width, wide_a), BF), sems],
        )

    def run_feed_forward(bufs, att, par):
        return kernel_call(
            functools.partial(feed_forward, lay, seq),
            pos,
            bufs,
            [tokens, att, cotangent, par],
            [
                sds((rows, width), F32),
                sds((rows, width), BF),
                sds((groups, rows, units), BF),
                sds((groups, rows, units), BF),
                *lay.grad_shapes(width),
            ],
            [
                pltpu.VMEM((rows, width), BF),
                pltpu.VMEM((groups, width, wide_b), BF),
                sems,
                *lay.stage_shapes(width),
            ],
            lay.n_grads(),
        )

    def run_feed_backward(bufs, slope, ln2):
        return kernel_call(
            functools.partial(feed_backward, lay, seq),
            pos,
            bufs,
            [slope, ln2, cotangent],
            [sds((rows, width), F32), sds((16, width), F32), *lay.grad_shapes(width)],
            [
                pltpu.VMEM((groups, width, width), BF),
                pltpu.VMEM((groups, width, wide_b), BF),
                pltpu.VMEM((rows, width), BF),
                sems,
                sems,
                *lay.stage_shapes(width),
            ],
            lay.n_grads(),
        )

    def run_mid_backward(bufs, ln2_grad, mid, att, small, par):
        return kernel_call(
            functools.partial(mid_backward, lay, seq),
            pos,
            bufs,
            [ln2_grad, mid, att, cotangent, small, par],
            [
                sds((rows, width), F32),
                sds((groups, rows, wide), BF),
                sds((16, width), F32),
                *lay.grad_shapes(wide_b - width),
            ],
            [
                pltpu.VMEM((groups, width, wide_b - width), BF),
                pltpu.VMEM((rows, width), F32),
                sems,
                *lay.stage_shapes(wide_b - width),
            ],
            lay.n_grads(),
        )

    def run_feed_output(bufs, act, mid, par):
        return kernel_call(
            functools.partial(feed_output, lay, seq),
            pos,
            bufs,
            [act, mid, par],
            [sds((seq, width), BF)],
            [pltpu.VMEM((groups, width, width), BF), pltpu.VMEM((rows, width), F32), sems],
        )[0]

    def run_attention_backward(bufs, ln1, qkv, probs, att, att_grad, mid_grad, small, par):
        return kernel_call(
            functools.partial(attention_backward, lay, seq, hd),
            pos,
            bufs,
            [tokens, ln1, qkv, probs, att, att_grad, mid_grad, small, par],
            [sds((seq, width), F32), sds((16, width), F32), *lay.grad_shapes(wide_a)],
            [
                pltpu.VMEM((rows, width), F32),
                pltpu.VMEM((groups, width, wide_a), BF),
                pltpu.VMEM((rows, three), F32),
                pltpu.VMEM((groups, rows, three), BF),
                pltpu.VMEM((rows, width), F32),
                sems,
                *lay.stage_shapes(wide_a),
            ],
            lay.n_grads(),
        )

    sub = chunk // groups
    if fast:
        vmem = pl.BlockSpec(memory_space=pltpu.VMEM)
        piece_a = pl.pallas_call(
            prepare_qkv,
            out_shape=sds((chunk, wide_a), BF),
            in_specs=[vmem] * 4,
            out_specs=vmem,
            scratch_shapes=[
                pltpu.VMEM((16, chunk), F32),
                pltpu.VMEM((16, 128), F32),
                pltpu.VMEM((16, 128), F32),
            ],
        )(qkv_weight, vectors, qv_bias.transpose(1, 0, 2), fc1_bias.T)
        piece_b = pl.pallas_call(
            prepare_fc1,
            out_shape=sds((chunk, wide_b), BF),
            in_specs=[vmem] * 2,
            out_specs=vmem,
        )(fc1_weight, proj_weight)
        piece_c = fc2_weight.T
        z_a = gather_columns(piece_a)
        z_a, piece_b, pos = barrier(z_a, piece_b, pos)
        h_a = barrier(join(*z_a[0:2]), join(*z_a[2:4]))
        near_a = gather_near(h_a)
        z_b = [piece_b, shift(piece_b, 1)]
        near_a, z_b = barrier(near_a, z_b)
        both_a = barrier(join(h_a[0], near_a[0]), join(h_a[1], near_a[1]))
        far_a = gather_far(both_a)
        z_b = [*z_b, shift(z_b[0], 2), shift(z_b[0], 3)]
        h_b = join(*z_b[0:2])
        far_a, z_b, both_a, h_b = barrier(far_a, z_b, both_a, h_b)
        h_b = h_b, join(*z_b[2:4])
        near_b = gather_near(h_b)
        bufs_a = in_order(both_a, far_a, flip_cores(both_a), flip_cores(far_a))
        ln1, qkv, probs, att, par = run_attention_forward(bufs_a)

        near_b, att = barrier(near_b, att)
        both_b = barrier(join(h_b[0], near_b[0]), join(h_b[1], near_b[1]))
        far_b = gather_far(both_b)
        core_b = flip_cores(both_b)
        core_b, piece_c = barrier(core_b, piece_c)
        z_c = gather_columns(piece_c)
        far_b, z_c = barrier(far_b, z_c)
        core_b = core_b + flip_cores(far_b)
        h_c = join(*z_c[0:2]), join(*z_c[2:4])
        near_c = direct_near(h_c)
        bufs_b = in_order(both_b, far_b, core_b[0:2], core_b[2:4])
        mid, ln2, act, slope, *grads_c = run_feed_forward(bufs_b, att, par)
        near_c, grads_c, slope = barrier(near_c, grads_c, slope)
        far_c = direct_far(near_c)
        recv_c, near_c, h_c = barrier(flip(grads_c[1], CORE), near_c, h_c)
        way_c = Scatter((grads_c[0], recv_c))
        first_c = way_c.first()
        first_c, near_c, h_c = barrier(first_c, near_c, h_c)
        core_c = flip_cores([*h_c, *near_c])
        first_c, far_c, core_c, slope = barrier(first_c, far_c, core_c, slope)
        bufs_c = [
            *in_direct_order(h_c, near_c, far_c),
            *in_direct_order(core_c[0:2], core_c[2:6], flip_cores(far_c)),
        ]
        got_c = way_c.send_first(first_c)
        ln2_grad, small, *grads_b = run_feed_backward([*bufs_b, *bufs_c], slope, ln2)
        got_c, grads_b, ln2_grad = barrier(got_c, grads_b, ln2_grad)

        recv_b = flip(grads_b[1], CORE)
        second_c = way_c.second(got_c)
        second_c, ln2_grad = barrier(second_c, ln2_grad)
        got_c = way_c.send_second(second_c)
        mid_grad, att_grad, small, *grads_p = run_mid_backward(
            bufs_b, ln2_grad, mid, att, small, par
        )
        got_c, recv_b, grads_p, mid_grad = barrier(got_c, recv_b, grads_p, mid_grad)

        recv_p = flip(grads_p[1], CORE)
        way_b = Scatter((grads_b[0], recv_b), (grads_p[0], recv_p))
        first_b = way_b.first()
        third_c = way_c.third(second_c, got_c)
        first_b, mid_grad, third_c = barrier(first_b, mid_grad, third_c)
        got_b = way_b.send_first(first_b)
        got_c = [shift(third_c[k], k) for k in (1, 3)]
        input_grad, small, *grads_a = run_attention_backward(
            bufs_a, ln1, qkv, probs, att, att_grad, mid_grad, small, par
        )
        got_b, got_c, third_c, grads_a = barrier(got_b, got_c, third_c, grads_a)

        recv_a = flip(grads_a[1], CORE)
        second_b = way_b.second(got_b)
        second_b, third_c = barrier(second_b, third_c)
        got_b = way_b.send_second(second_b)
        got_c = [*got_c, shift(third_c[2], 2)]
        way_a = Scatter((grads_a[0], recv_a))
        first_a = way_a.first()
        first_a, got_b, got_c, act = barrier(first_a, got_b, got_c, act)
        got_a = way_a.send_first(first_a)
        third_b = way_b.third(second_b, got_b)
        third_b, act = barrier(third_b, act)
        half_b = 3 * wide_b // 8
        got_b = [shift(third_b[k], k) for k in (1, 3)] + [shift(third_b[2][:, :half_b], 2)]
        output = run_feed_output(bufs_c, act, mid, par)
        sum_c = way_c.last(third_c, got_c)
        got_a, output, sum_c, got_b, third_b = barrier(got_a, output, sum_c, got_b, third_b)
        second_a = way_a.second(got_a)
        second_a, third_b = barrier(second_a, third_b)
        got_a = way_a.send_second(second_a)
        rest_b = shift(third_b[2][:, half_b:], 2)
        got_b = [*got_b[0:2], jnp.concatenate([got_b[2], rest_b], axis=1)]
        got_a, got_b = barrier(got_a, got_b)
        third_a = way_a.third(second_a, got_a)[1:]
        third_a, second_a, step_a = barrier(third_a, second_a, got_a)
        got_a = [shift(third_a[k - 1], k) for k in (1, 2, 3)]
        got_a[0], second_a, step_a, got_b = barrier(got_a[0], second_a, step_a, got_b)
        own_a = second_a[0][0, 0].astype(F32) + step_a[0][0].astype(F32)
        sum_b = way_b.last(third_b, got_b)
        sum_b, got_a, own_a = barrier(sum_b, got_a, own_a)
        sum_a = way_a.last([own_a], got_a)
        vmem = pl.BlockSpec(memory_space=pltpu.VMEM)
        qkv_grad, sum_b, proj_grad, vec_grad, qv_grad, fc1b_grad = pl.pallas_call(
            functools.partial(finish_attention, chunk),
            out_shape=[
                sds((3, chunk, wide), F32),
                sds((chunk, width), F32),
                sds((wide, chunk), F32),
                sds((6, sub), F32),
                sds((heads, 2, each), F32),
                sds((each, units // hd), F32),
            ],
            in_specs=[pl.BlockSpec(memory_space=pltpu.SMEM)] + [vmem] * 2,
            out_specs=[vmem] * 6,
            scratch_shapes=[pltpu.VMEM((chunk, SPARE), F32)],
        )(pos, sum_a, sum_b)
        qv_grad, fc1b_grad = qv_grad.transpose(1, 0, 2), fc1b_grad.T
    else:
        none = jnp.zeros_like(qv_bias[0])
        qkv_col = jnp.stack([qv_bias[0], none, qv_bias[1], none]).reshape(chunk)
        spare = jnp.concatenate([vectors, fc1_bias.reshape(1, chunk), qkv_col[None]], axis=0).T
        spare = jnp.pad(spare, ((0, 0), (0, SPARE - spare.shape[1])))
        piece_a = jnp.concatenate([qkv_weight[0], qkv_weight[1], qkv_weight[2], spare], axis=1)
        piece_b = jnp.concatenate([fc1_weight, proj_weight.T], axis=1)
        piece_b = jnp.pad(piece_b, ((0, 0), (0, wide_b - width - wide)))

        def gather(p):
            return [lax.all_gather(lax.all_gather(p, "dp", axis=0, tiled=True), "tensor", axis=0)]

        bufs_a, bufs_b, bufs_c = gather(piece_a), gather(piece_b), gather(fc2_weight.T)
        cols = bufs_a[0][:, :, three : three + 8]
        vec = cols[0, :, 0:6].T
        by_unit = cols.reshape(groups, n_dp, chunk // each, each, 8).transpose(0, 4, 2, 1, 3)
        by_unit = by_unit.reshape(groups, 8, width)
        par = jnp.concatenate([vec, by_unit[:, 6], by_unit[:, 7]], axis=0).astype(F32)
        par = jnp.pad(par, ((0, 16 - par.shape[0]), (0, 0)))
        ln1, qkv, probs, att, par = run_attention_forward(bufs_a, par)
        mid, ln2, act, slope, grads_c = run_feed_forward(bufs_b, att, par)
        ln2_grad, small, grads_b = run_feed_backward([*bufs_b, *bufs_c], slope, ln2)
        mid_grad, att_grad, small, grads_p = run_mid_backward(
            bufs_b, ln2_grad, mid, att, small, par
        )
        output = run_feed_output(bufs_c, act, mid, par)
        input_grad, small, grads_a = run_attention_backward(
            bufs_a, ln1, qkv, probs, att, att_grad, mid_grad, small, par
        )

        def scatter(g):
            g = lax.psum_scatter(g, "tensor", scatter_dimension=0, tiled=False)
            return lax.psum_scatter(g, "dp", scatter_dimension=0, tiled=True).astype(F32)

        sum_c, sum_b, sum_a = scatter(grads_c), scatter(grads_b), scatter(grads_a)
        sum_p = lax.optimization_barrier(scatter(grads_p))
        small = lax.psum(small, ("dp", "tensor"))
        vec_grad = lax.dynamic_slice(small, (0, d * chunk + z * sub), (6, sub))
        by_unit = small[6:14].reshape(2, groups, chunk // each, hd)
        by_unit = lax.dynamic_slice(
            by_unit, (0, z, 0, d * each), (2, 1, chunk // each, each)
        ).reshape(2, chunk)
        fc1b_grad, qv_grad = by_unit[0], by_unit[1]
        fc1b_grad = fc1b_grad.reshape(fc1_bias.shape)
        qv_grad = qv_grad.reshape(4, heads, each)[0::2]
        qkv_grad = jnp.stack([sum_a[:, c * wide : (c + 1) * wide] for c in range(3)])
        proj_grad = sum_p[:, :wide].T
    return (
        output,
        input_grad,
        qkv_grad,
        qv_grad,
        proj_grad,
        vec_grad,
        sum_b,
        fc1b_grad,
        sum_c.T,
    )


def solution(mesh):
    return jax.shard_map(
        per_device,
        mesh=mesh,
        in_specs=(
            P(("dp", "tensor"), None),
            P(("dp", "tensor"), None),
            P(None, "dp", "tensor"),
            P(None, "tensor", "dp"),
            P("tensor", "dp"),
            P(None, "dp"),
            P("dp", "tensor"),
            P("tensor", "dp"),
            P("tensor", "dp"),
        ),
        out_specs=(
            P(("dp", "tensor"), None),
            P(("dp", "tensor"), None),
            P(None, "dp", "tensor"),
            P(None, "tensor", "dp"),
            P("tensor", "dp"),
            P(None, ("dp", "tensor")),
            P("dp", "tensor"),
            P("tensor", "dp"),
            P("tensor", "dp"),
        ),
        check_vma=False,
    )
```
